256 devices in a mesh: expert: 4 (over x_lo, core), tensor: 32 (over y, z), kv: 2 (over x_hi).
Axes of the slice: x: 4 (x_hi: 2, x_lo: 2; x = x_hi * 2 + x_lo), y: 4, z: 8, core: 2. Of those that a mesh axis runs over, the one named last changes fastest.
Arguments:
- residual_stream: bfloat16 [1024, 4096], P('expert', ('tensor', 'kv')), may hold values from -13 to 13
- grad_output: bfloat16 [1024, 4096], P('expert', ('tensor', 'kv')), may hold values from -6 to 6
- norm_gain: bfloat16 [4096], P(('tensor', 'kv')), may hold values from 0.5 to 1.5
- expert_ids: int32 [1024, 2], P('expert'), may hold values from 0 to 3, all different within a row; in each aligned block of 256 rows (0 to 255, 256 to 511, ...) at most 160 rows name the same one
- gate_probs: float32 [1024, 2], P('expert'), may hold values from 0.1 to 0.9
- w_gate: bfloat16 [4, 14336, 4096], P('expert', ('tensor', 'kv')), may hold values from -0.25 to 0.25
- w_up: bfloat16 [4, 14336, 4096], P('expert', ('tensor', 'kv')), may hold values from -0.25 to 0.25
- w_down: bfloat16 [4, 14336, 4096], P('expert', ('tensor', 'kv')), may hold values from -0.046875 to 0.046875
Outputs:
- input_grad: bfloat16 [1024, 4096], P('expert', ('tensor', 'kv'))
The draws below stay inside these ranges and needn't reach their ends.
Inputs may be any that keep to these rules, and one draw needn't show every extreme that they name: `expert_ids`: each row names two different experts. In each aligned block of 256 rows (the rows of one index of the expert axis) no expert is named by more than 160 rows, a bound that some block reaches.
All inputs are finite; a program needn't handle non-finite values.
Results may differ from the reference program's by a relative error of at most 0.018.
Values may be sent and summed in bfloat16 or wider, within the bound.
No kernel may reach another device: no remote copies, remote signals or barrier semaphores. Data moves between devices by JAX's collectives and lax.ppermute only.
A program may use at most 128 MiB of HBM per device.

```python
import math
import jax
import jax.numpy as jnp
import numpy as np
from jax import lax

D = 4096
FF = 14336
TOK_DEV = 256
CAP = 160
EXPERTS = 4
TOKENS = 1024
N_EXPERT = 4


def draw_residual_stream(key, part):
    keys = jax.random.split(jax.random.fold_in(key, 17), 3)
    row_scale = 10.0 ** jax.random.uniform(keys[0], (TOKENS, 1), jnp.float32, -1.5, -0.5)
    ramp = jnp.arange(D, dtype=jnp.float32)[None, :] / D
    col_scale = 10.0 ** (0.5 * ramp + 0.5 * jax.random.uniform(keys[1], (1, D), jnp.float32))
    base = jax.random.normal(keys[2], (TOKENS, D), jnp.float32)
    base = jnp.clip(base, -4.0, 4.0)
    return (base * row_scale * col_scale).astype(jnp.bfloat16)


def with_spikes(drawn, own_key, source, target, blocks, factor):
    owner, partner = [(jnp.arange(drawn.shape[dim]) // (drawn.shape[dim] // blocks)).reshape([-1 if axis == dim else 1 for axis in range(drawn.ndim)]) for dim in (source, target)]
    chosen = jax.random.permutation(own_key, blocks)[partner]
    strong = (owner == chosen) | (owner == (partner + blocks // 2) % blocks)
    return jnp.where(strong, factor * drawn, drawn)


def shard_levels(own_key, dims, cuts, low, top_value):
    factor_of, own = 1.0, jax.random.fold_in(own_key, 6)
    for axis_at, blocks in cuts:
        heights = jnp.exp(jax.random.uniform(jax.random.fold_in(own, axis_at), (blocks,), jnp.float32, low / len(cuts), top_value / len(cuts)))
        factor_of = factor_of * jnp.repeat(heights, dims[axis_at] // blocks).reshape([-1 if axis == axis_at else 1 for axis in range(len(dims))])
    return factor_of


def routed_block(stream_key, own, number, rows, amount, top, bound, skew):
    order = jax.random.permutation(stream_key, amount)
    packed, usual = portions_of(amount, rows * top, bound, skew, True), portions_of(amount, rows * top, bound, skew, False)
    places = jnp.arange(amount)

    def named(tallies, rotation):
        used = int((tallies > 0).sum())
        fixed = max(1, used // 4)
        moved = fixed + (places - fixed + rotation * (used - fixed)) % max(1, amount - fixed)
        return jnp.zeros((amount,), jnp.int32).at[order[jnp.where(places < fixed, places, moved)]].set(jnp.asarray(tallies, jnp.int32))

    tallies = jnp.where(number % 4 == 0, named(packed, number // 4), named(usual, number - number // 4 - 1))
    mixed = jax.random.permutation(jax.random.fold_in(own, 3), amount)
    donor, taker = mixed[0:amount // 2 * 2:2], mixed[1:amount // 2 * 2:2]
    slack = jnp.minimum(tallies[donor] - 1, bound - tallies[taker]) // 2
    slack = jnp.where((donor == order[0]) | (taker == order[0]) | (tallies[taker] == 0), 0, jnp.maximum(slack, 0))
    moved = jax.random.randint(jax.random.fold_in(own, 4), (amount // 2,), 0, 1 << 20) % (slack + 1)
    tallies = tallies.at[donor].add(-moved).at[taker].add(moved)
    items = jnp.searchsorted(jnp.cumsum(tallies), jnp.arange(rows * top), side="right").astype(jnp.int32)
    table = items.reshape(top, rows).T
    table = table[jax.random.permutation(jax.random.fold_in(own, 1), rows)]
    rotation = jax.random.randint(jax.random.fold_in(own, 2), (rows, 1), 0, top)
    return jnp.take_along_axis(table, (jnp.arange(top)[None, :] + rotation) % top, axis=1)


def portions_of(amount, total, bound, lean, full):
    loads = [(1 << 20) // math.isqrt(standing ** lean) + 1 for standing in range(1, amount + 1)]
    largest = bound if full else min(bound, max(-(-total // amount), total * loads[0] // sum(loads)))
    least = 1 if total - largest >= amount - 1 else 0
    counts, rest = [largest] + [least] * (amount - 1), total - largest - least * (amount - 1)
    while rest > 0:
        movable = [i for i in range(1, amount) if counts[i] < largest] or [i for i in range(1, amount) if counts[i] < bound]
        whole, remaining = sum([loads[i] for i in movable]), rest
        for i in movable:
            addition = min(bound - counts[i], max(1, remaining * loads[i] // whole), rest)
            counts[i] = counts[i] + addition
            rest = rest - addition
    return np.array(counts)


def centred(own_key, dims, width, limit, cuts=(), kind=jnp.bfloat16):
    factor_of = shard_levels(own_key, dims, cuts, -0.22, 0.18) if cuts else 1.0
    drawn = jax.random.normal(own_key, dims, jnp.float32) * width * factor_of
    return jnp.minimum(jnp.maximum(drawn, -limit), limit).astype(kind)


def bell_draw_with(stream_key, shape, scale, most, cuts, heavy, kind=jnp.bfloat16):
    values = scale * jax.random.normal(stream_key, shape, jnp.float32)
    if cuts:
        values = values * shard_levels(stream_key, shape, cuts, -0.22, 0.18)
    return jnp.clip(with_spikes(values, jax.random.fold_in(stream_key, 3), *heavy), -most, most).astype(kind)


def setup_inputs(seed: int = 0) -> dict:
    seeds = jax.random.split(jax.random.key(seed), 9)
    residual_stream = draw_residual_stream(jax.random.fold_in(seeds[8], 71), 0)
    grad_output = centred(seeds[1], (TOKENS, D), 1.0, 6.0, ((0, 4), (1, 64)))
    norm_gain = jnp.clip(1.0 + 0.1 * jax.random.normal(seeds[2], (D,), jnp.float32), 0.5, 1.5).astype(jnp.bfloat16)
    expert_ids_keys = jax.random.split(jax.random.fold_in(seeds[3], 1), TOKENS // TOK_DEV)
    expert_ids_turns = jax.random.permutation(jax.random.fold_in(seeds[3], 3), TOKENS // TOK_DEV)
    expert_ids = jax.vmap(lambda own, number: routed_block(jax.random.fold_in(seeds[3], 2), own, number, TOK_DEV, EXPERTS, 2, CAP, 2))(expert_ids_keys, expert_ids_turns).reshape((TOKENS, 2))
    gate_probs = jnp.clip(0.1 + 0.79999997 * jax.random.uniform(seeds[4], (TOKENS, 2), jnp.float32) ** shard_levels(seeds[4], (TOKENS, 2), ((0, 4),), -0.2, 0.2), 0.1, 0.9)
    w_gate = bell_draw_with(seeds[5], (EXPERTS, FF, D), D ** -0.5, 0.25, ((0, 4), (1, 64)), (1, 2, 64, 4.0))
    w_up = bell_draw_with(seeds[6], (EXPERTS, FF, D), D ** -0.5, 0.25, ((0, 4), (1, 64)), (1, 2, 64, 4.0))
    w_down = centred(seeds[7], (EXPERTS, FF, D), FF ** -0.5, 0.046875, ((0, 4), (1, 64)))
    return dict(residual_stream=residual_stream, grad_output=grad_output, norm_gain=norm_gain, expert_ids=expert_ids, gate_probs=gate_probs, w_gate=w_gate, w_up=w_up, w_down=w_down)


epsilon = 1e-05
contract_width = (((1,), (1,)), ((), ()))

def slot_matrix(ids_block, experts):
    flattened = ids_block.reshape(-1)
    onehot = (flattened[:, None] == jnp.arange(experts, dtype=jnp.int32)[None, :]).astype(jnp.int32)
    before = jnp.cumsum(onehot, axis=0) - onehot
    position = lax.optimization_barrier(jnp.sum(before * onehot, axis=1))
    slot_index = flattened * CAP + position
    table = jnp.arange(experts * CAP, dtype=jnp.int32)
    return (slot_index[None, :] == table[:, None]).astype(jnp.bfloat16)

def dispatch_block(ids_block, normed_block, grad_block, prob_block):
    table = slot_matrix(ids_block, EXPERTS)
    repeated_x = jnp.repeat(normed_block, 2, axis=0)
    scaled = (jnp.repeat(grad_block.astype(jnp.float32), 2, axis=0) * prob_block.reshape(-1, 1)).astype(jnp.bfloat16)
    routed_x = jnp.dot(table, repeated_x, preferred_element_type=jnp.float32).astype(jnp.bfloat16)
    routed_grad = jnp.dot(table, scaled, preferred_element_type=jnp.float32).astype(jnp.bfloat16)
    return (table, routed_x, routed_grad)

def expert_grad(operands):
    routed_x, routed_grad, gate_weight, up_weight, down_weight = operands
    gate_value = lax.dot_general(routed_x, gate_weight, contract_width, preferred_element_type=jnp.float32)
    up_value = lax.dot_general(routed_x, up_weight, contract_width, preferred_element_type=jnp.float32)
    act_grad = lax.dot_general(routed_grad, down_weight, contract_width, preferred_element_type=jnp.float32)
    sigmoid_gate = jax.nn.sigmoid(gate_value)
    activated = gate_value * sigmoid_gate
    gate_grad = (act_grad * up_value * sigmoid_gate * (1.0 + gate_value * (1.0 - sigmoid_gate))).astype(jnp.bfloat16)
    up_grad = (act_grad * activated).astype(jnp.bfloat16)
    slot_grad = jnp.dot(gate_grad, gate_weight, preferred_element_type=jnp.float32)
    slot_grad = slot_grad + jnp.dot(up_grad, up_weight, preferred_element_type=jnp.float32)
    return slot_grad.astype(jnp.bfloat16)

def combine_block(table, values):
    summed = lax.dot_general(table, values, (((0,), (0,)), ((), ())), preferred_element_type=jnp.float32)
    return summed.reshape(TOK_DEV, 2, D).sum(axis=1)

def reference(residual_stream, grad_output, norm_gain, expert_ids, gate_probs, w_gate, w_up, w_down):
    stream = residual_stream.astype(jnp.float32)
    squares = lax.optimization_barrier(jnp.sum(stream * stream, axis=1, keepdims=True))
    inverse_rms = lax.rsqrt(squares / D + epsilon)
    gains = norm_gain.astype(jnp.float32)
    normed = (stream * inverse_rms * gains).astype(jnp.bfloat16)
    blocks = N_EXPERT
    tables, routed_x, routed_grad = jax.vmap(dispatch_block)(expert_ids.reshape(blocks, TOK_DEV, 2), normed.reshape(blocks, TOK_DEV, D), grad_output.reshape(blocks, TOK_DEV, D), gate_probs.reshape(blocks, TOK_DEV, 2))
    expert_x = routed_x.reshape(blocks, EXPERTS, CAP, D).transpose(1, 0, 2, 3).reshape(EXPERTS, blocks * CAP, D)
    expert_dy = routed_grad.reshape(blocks, EXPERTS, CAP, D).transpose(1, 0, 2, 3).reshape(EXPERTS, blocks * CAP, D)
    expert_out = lax.map(expert_grad, (expert_x, expert_dy, w_gate, w_up, w_down))
    returned = expert_out.reshape(EXPERTS, blocks, CAP, D).transpose(1, 0, 2, 3).reshape(blocks, EXPERTS * CAP, D)
    token_grad = jax.vmap(combine_block)(tables, returned).reshape(TOKENS, D)
    scaled_grad = token_grad * gains
    projection = lax.optimization_barrier(jnp.sum(scaled_grad * stream, axis=1, keepdims=True))
    result = inverse_rms * scaled_grad - stream * inverse_rms ** 3 * projection / D
    return result.astype(jnp.bfloat16)
```

```python
import jax
import jax.numpy as jnp
from jax import lax
from jax.experimental import pallas as pl
from jax.experimental.pallas import tpu as pltpu
from jax.sharding import Mesh
from jax.sharding import PartitionSpec as P

D = 4096
CAP = 160
EPS = 1e-05
GROUPS = 4
NY = 4
NZ = 8
LANES = 128
ROWS = GROUPS * CAP
HALF = ROWS // 2
GAIN_ROWS = 16
TENSOR_KV = ("tensor_0", "tensor_1", "kv")
F32 = jnp.float32
BF16 = jnp.bfloat16
NT = (((1,), (1,)), ((), ()))
TN = (((0,), (0,)), ((), ()))
VMEM_LIMIT = 60 * 1024 * 1024


def call(kernel, outs, cost, scratch=()):
    flops, moved = cost
    return pl.pallas_call(
        kernel,
        out_shape=[jax.ShapeDtypeStruct(s, t) for s, t in outs],
        scratch_shapes=list(scratch),
        compiler_params=pltpu.CompilerParams(vmem_limit_bytes=VMEM_LIMIT),
        cost_estimate=pl.CostEstimate(flops=flops, bytes_accessed=moved, transcendentals=0),
    )


def slots_of(ids):
    tokens = ids.shape[1]
    first, second = ids[0:1], ids[1:2]
    groups = lax.broadcasted_iota(jnp.int32, (8, tokens), 0)
    named = jnp.where(first == groups, 1.0, 0.0) + jnp.where(second == groups, 1.0, 0.0)
    earlier = jnp.where(
        lax.broadcasted_iota(jnp.int32, (tokens, tokens), 0)
        < lax.broadcasted_iota(jnp.int32, (tokens, tokens), 1),
        1.0,
        0.0,
    ).astype(BF16)
    before = jnp.dot(named.astype(BF16), earlier, preferred_element_type=F32).astype(jnp.int32)
    at_first = jnp.sum(jnp.where(first == groups, before, 0), axis=0, keepdims=True)
    at_second = jnp.sum(jnp.where(second == groups, before, 0), axis=0, keepdims=True)
    return first * CAP + at_first, second * CAP + at_second


def dispatch_kernel(ids_ref, probs_ref, x_ref, grad_ref, out_ref):
    mine = lax.axis_index("expert")
    one, two = slots_of((ids_ref[...] - mine + GROUPS) % GROUPS)
    tokens = ids_ref.shape[1]
    rows = lax.broadcasted_iota(jnp.int32, (ROWS, tokens), 0)
    x = x_ref[...]
    grad = grad_ref[...].astype(F32)
    probs = probs_ref[...]
    terms = []
    for slot, k in ((one, 0), (two, 1)):
        table = jnp.where(rows == slot, 1.0, 0.0).astype(BF16)
        values = jnp.concatenate([x, (grad * probs[k : k + 1]).astype(BF16)], axis=0)
        terms.append(lax.dot_general(table, values, NT, preferred_element_type=F32))
    out_ref[...] = (terms[0] + terms[1]).astype(BF16).reshape(GROUPS, CAP, LANES)


def assemble_kernel(*refs):
    same, other = refs[:GROUPS], refs[GROUPS : 2 * GROUPS]
    gain_ref, gain_other_ref, x_ref, grad_ref = refs[2 * GROUPS :]
    low = lax.axis_index("kv") == 0

    def ordered(a, b):
        return jnp.where(low, a, b), jnp.where(low, b, a)

    for g in range(GROUPS):
        a, b = ordered(same[g][...].astype(F32), other[g][...].astype(F32))
        rows = pl.ds(g * CAP, CAP)
        x_ref[rows, :] = jnp.concatenate([a[:, :64], b[:, :64]], axis=1).astype(BF16)
        grad_ref[rows, :] = jnp.concatenate([a[:, 64:], b[:, 64:]], axis=1).astype(BF16)
    a, b = ordered(gain_ref[...].astype(F32), gain_other_ref[...].astype(F32))
    x_ref[pl.ds(ROWS, GAIN_ROWS), :] = jnp.concatenate([a[:, :64], b[:, :64]], axis=1).astype(BF16)


def column(a, b):
    y = lax.rem(lax.axis_index("tensor_0") + a, NY)
    z = lax.rem(lax.axis_index("tensor_1") + b, NZ)
    return pl.ds(pl.multiple_of((y * NZ + z) * LANES, LANES), LANES)


def forward_kernel(x0, x1, x3, x2lo, x2hi, wg_ref, wu_ref, gate_ref, up_ref, inv_ref, xn_ref):
    def piece(a, b):
        if a == 2:
            return (x2lo, b) if b < NZ // 2 else (x2hi, b - NZ // 2)
        return (x0, x1, None, x3)[a], b

    places = [(a, b) for a in range(NY) for b in range(NZ)]

    @pl.loop(0, ROWS // LANES)
    def _(i):
        rows = pl.ds(pl.multiple_of(i * LANES, LANES), LANES)
        total = jnp.zeros((LANES, LANES), F32)
        for a, b in places:
            ref, at = piece(a, b)
            v = ref[at, rows, :].astype(F32)
            total = total + v * v
        inv = lax.rsqrt(jnp.sum(total, axis=1, keepdims=True) / D + EPS)
        inv_ref[:, rows] = jnp.transpose(jnp.broadcast_to(inv, (LANES, LANES)))[0:1]
        for a, b in places:
            ref, at = piece(a, b)
            gain = ref[at, pl.ds(ROWS, GAIN_ROWS), :].astype(F32)[0:1]
            xn_ref[rows, column(a, b)] = (ref[at, rows, :].astype(F32) * inv * gain).astype(BF16)

    @pl.loop(0, 2)
    def _(i):
        rows = pl.ds(pl.multiple_of(i * HALF, HALF), HALF)
        x = xn_ref[rows, :]
        gate_ref[rows, :] = lax.dot_general(x, wg_ref[...], NT, preferred_element_type=F32)
        up_ref[rows, :] = lax.dot_general(x, wu_ref[...], NT, preferred_element_type=F32)


def hidden_kernel(*refs):
    *pieces, wd_ref, gate_ref, up_ref, gg_ref, ug_ref, p_ref, dn_ref, product_ref = refs
    d0, d1, d2, d3, d4lo, d4hi, d5, d6, d7 = pieces
    for b, ref in ((0, d0), (1, d1), (2, d2), (3, d3), (5, d5), (6, d6), (7, d7)):
        for a in range(NY):
            dn_ref[:, column(a, b)] = ref[a]
    for a in range(NY):
        dn_ref[:, column(a, 4)] = (d4lo, d4hi)[a // 2][a % 2]

    @pl.loop(0, 2)
    def _(i):
        rows = pl.ds(pl.multiple_of(i * HALF, HALF), HALF)
        act = lax.dot_general(dn_ref[rows, :], wd_ref[...], NT, preferred_element_type=F32)
        gate, up = gate_ref[rows, :], up_ref[rows, :]
        sigma = jax.nn.sigmoid(gate)
        gg = (act * up * sigma * (1.0 + gate * (1.0 - sigma))).astype(BF16)
        ug = (act * (gate * sigma)).astype(BF16)
        gg_ref[rows, :] = gg
        ug_ref[rows, :] = ug
        product_ref[rows, :] = gg.astype(F32) * gate + ug.astype(F32) * up

    for i in range(ROWS // LANES):
        rows = pl.ds(i * LANES, LANES)
        sums = jnp.sum(product_ref[rows, :], axis=1, keepdims=True)
        p_ref[:, rows] = jnp.transpose(jnp.broadcast_to(sums, (LANES, LANES)))[0:1]


def back_kernel(gg_ref, ug_ref, wg_ref, wu_ref, a0, a1, a2, a3, a4lo, a4hi, a5, a6, a7, b0, b1, b2lo, b2hi, b3):
    by_z = (a0, a1, a2, a3, None, a5, a6, a7)
    by_y = (b0, b1, None, b3)
    for a in range(NY):
        for pair in range(NZ // 2):
            at = [column(a, 2 * pair), column(a, 2 * pair + 1)]
            wg = jnp.concatenate([wg_ref[:, c] for c in at], axis=1)
            wu = jnp.concatenate([wu_ref[:, c] for c in at], axis=1)
            total = jnp.dot(gg_ref[...], wg, preferred_element_type=F32) + jnp.dot(
                ug_ref[...], wu, preferred_element_type=F32
            )
            total = total.astype(BF16)
            for j in range(2):
                b = 2 * pair + j
                top = total[:HALF, j * LANES : (j + 1) * LANES]
                bottom = total[HALF:, j * LANES : (j + 1) * LANES]
                if b == 4:
                    (a4lo, a4hi)[a // 2][a % 2] = top
                else:
                    by_z[b][a] = top
                if a == 2:
                    (b2lo, b2hi)[b // 4][b % 4] = bottom
                else:
                    by_y[a][b] = bottom


def combine_kernel(*refs):
    same, other = refs[:GROUPS], refs[GROUPS : 2 * GROUPS]
    ids_ref, scalars_ref, x_ref, gain_ref, out_ref = refs[2 * GROUPS :]
    mine = lax.axis_index("expert")
    one, two = slots_of((ids_ref[...] - mine + GROUPS) % GROUPS)
    tokens = ids_ref.shape[1]
    rows = lax.broadcasted_iota(jnp.int32, (ROWS, tokens), 0)
    table = jnp.where((rows == one) | (rows == two), 1.0, 0.0).astype(BF16)
    slot_grad = jnp.concatenate(
        [(s[...].astype(F32) + o[...].astype(F32)).astype(BF16) for s, o in zip(same, other)], axis=0
    )
    both = lax.dot_general(slot_grad, table, TN, preferred_element_type=F32)
    token_grad = jnp.where(lax.axis_index("kv") == 0, both[:64], both[64:])
    value, found = scalars_ref[...], 0.0
    for _ in range(3):
        term = value.astype(BF16)
        value = value - term.astype(F32)
        found = found + jnp.dot(term, table, preferred_element_type=F32)
    coefficient = found[0:1]
    inverse_rms = 0.5 * found[1:2]
    gain = jnp.transpose(gain_ref[...].astype(F32))[:, 0:1]
    x = x_ref[...].astype(F32)
    out_ref[...] = (inverse_rms * (token_grad * gain) - x * coefficient).astype(BF16)


def shift(value, axis, by):
    n = lax.axis_size(axis)
    return lax.ppermute(value, axis, [(i, (i + by) % n) for i in range(n)])


def shift_pair(value, by, cross):
    n = GROUPS
    return lax.ppermute(
        value,
        ("expert", "kv"),
        [(e * 2 + k, ((e + by) % n) * 2 + (k ^ cross)) for e in range(n) for k in range(2)],
    )


def butterfly(value, axis, bit):
    n = lax.axis_size(axis)
    return value + lax.ppermute(value, axis, [(i, i ^ bit) for i in range(n)])


def gather_ring(value, axis, split):
    n = lax.axis_size(axis)
    got = {0: value}
    right = left = value
    for step in range(1, n // 2):
        right, left = shift(right, axis, 1), shift(left, axis, -1)
        got[n - step], got[step] = right, left
    far = (shift(right[:split], axis, 1), shift(left[split:], axis, -1))
    return got, far


def plus(a, b):
    return (a.astype(F32) + b.astype(F32)).astype(BF16)


def scatter_ring(own, far, axis):
    n = lax.axis_size(axis)
    half = n // 2
    split = far[0].shape[0]
    right, left = shift(far[0], axis, 1), shift(far[1], axis, -1)
    for step in range(half - 1, 0, -1):
        to_right, to_left = own[step], own[n - step]
        if step == half - 1:
            right = jnp.concatenate([plus(right, to_right[:split]), to_right[split:]], axis=0)
            left = jnp.concatenate([to_left[:split], plus(left, to_left[split:])], axis=0)
        else:
            right, left = plus(right, to_right), plus(left, to_left)
        right, left = shift(right, axis, 1), shift(left, axis, -1)
    return (own[0].astype(F32) + right.astype(F32) + left.astype(F32)).astype(BF16)


def shards(residual_stream, grad_output, norm_gain, expert_ids, gate_probs, w_gate, w_up, w_down):
    wg, wu, wd = w_gate[0], w_up[0], w_down[0]
    ids, probs = expert_ids.T, gate_probs.T
    x_t, grad_t = residual_stream.T, grad_output.T
    gain_rows = jnp.broadcast_to(jnp.concatenate([norm_gain, norm_gain])[None], (GAIN_ROWS, LANES))

    with jax.named_scope("dispatch"):
        [routed] = call(dispatch_kernel, [((GROUPS, CAP, LANES), BF16)], (2 * 640 * 512 * 128, 400000))(
            ids, probs, x_t, grad_t
        )
        same, other = [routed[0]], []
        for g in range(GROUPS):
            if g:
                same.append(shift_pair(routed[g], g, 0))
            else:
                packed = shift_pair(jnp.concatenate([routed[0], gain_rows], axis=0), 0, 1)
                gain_other = packed[CAP:]
                other.append(packed[:CAP])
            if g:
                other.append(shift_pair(routed[g], g, 1))
        x_piece, grad_piece = call(
            assemble_kernel, [((ROWS + GAIN_ROWS, LANES), BF16), ((ROWS, LANES), BF16)], (0, 800000)
        )(*same, *other, gain_rows, gain_other)

    with jax.named_scope("gather_x"):
        got, far = gather_ring(x_piece, "tensor_1", HALF + GAIN_ROWS)
        got[NZ // 2] = jnp.concatenate(far, axis=0)
        line = jnp.stack([got[j] for j in range(NZ)])
        x_got, x_far = gather_ring(line, "tensor_0", NZ // 2)
    with jax.named_scope("gather_grad"):
        got, far = gather_ring(grad_piece, "tensor_0", HALF)
        got[NY // 2] = jnp.concatenate(far, axis=0)
        line = jnp.stack([got[j] for j in range(NY)])
        d_got, d_far = gather_ring(line, "tensor_1", NY // 2)

    hidden = wg.shape[0]
    big = 2 * ROWS * D * hidden
    with jax.named_scope("forward"):
        gate, up, inv = call(
            forward_kernel,
            [((ROWS, hidden), F32), ((ROWS, hidden), F32), ((1, ROWS), F32)],
            (2 * big, 10_000_000),
            [pltpu.VMEM((ROWS, D), BF16)],
        )(x_got[0], x_got[1], x_got[3], *x_far, wg, wu)
    with jax.named_scope("hidden"):
        gg, ug, p = call(
            hidden_kernel,
            [((ROWS, hidden), BF16), ((ROWS, hidden), BF16), ((1, ROWS), F32)],
            (big, 9_000_000),
            [pltpu.VMEM((ROWS, D), BF16), pltpu.VMEM((ROWS, hidden), F32)],
        )(d_got[0], d_got[1], d_got[2], d_got[3], *d_far, d_got[5], d_got[6], d_got[7], wd, gate, up)
    with jax.named_scope("back"):
        line_z, line_y, half_z, half_y = (
            ((NY, HALF, LANES), BF16),
            ((NZ, HALF, LANES), BF16),
            ((NY // 2, HALF, LANES), BF16),
            ((NZ // 2, HALF, LANES), BF16),
        )
        out = call(back_kernel, [line_z] * 4 + [half_z] * 2 + [line_z] * 3 + [line_y] * 2 + [half_y] * 2 + [line_y], (2 * big, 9_000_000))(
            gg, ug, wg, wu
        )
        a0, a1, a2, a3, a4lo, a4hi, a5, a6, a7, b0, b1, b2lo, b2hi, b3 = out

    with jax.named_scope("projection_sum"):
        for axis, bits in (("tensor_1", (1, 2, 4)), ("tensor_0", (1, 2)), ("kv", (1,))):
            for bit in bits:
                p = butterfly(p, axis, bit)
        scalars = jnp.concatenate([inv * inv * p / D, inv], axis=0)
        parts = [scalars] + [shift(scalars, "expert", -g) for g in range(1, GROUPS)]
        scalars = jnp.concatenate([s[:, g * CAP : (g + 1) * CAP] for g, s in enumerate(parts)], axis=1)
        scalars = jnp.concatenate([scalars, jnp.zeros((6, ROWS), F32)], axis=0)

    with jax.named_scope("scatter_top"):
        top = scatter_ring({0: a0, 1: a1, 2: a2, 3: a3, 5: a5, 6: a6, 7: a7}, (a4lo, a4hi), "tensor_1")
        top = scatter_ring({0: top[0], 1: top[1], 3: top[3]}, (top[2, : HALF // 2], top[2, HALF // 2 :]), "tensor_0")
    with jax.named_scope("scatter_bottom"):
        low = scatter_ring({0: b0, 1: b1, 3: b3}, (b2lo, b2hi), "tensor_0")
        low = scatter_ring(
            {j: low[j] for j in range(NZ) if j != 4}, (low[4, : HALF // 2], low[4, HALF // 2 :]), "tensor_1"
        )

    with jax.named_scope("combine"):
        pieces = [top[:CAP], top[CAP:], low[:CAP], low[CAP:]]
        same = [pieces[0]] + [shift_pair(pieces[g], -g, 0) for g in range(1, GROUPS)]
        other = [shift_pair(pieces[g], -g, 1) for g in range(GROUPS)]
        gain_square = jnp.broadcast_to(norm_gain[None], (LANES, norm_gain.shape[0]))
        [out] = call(combine_kernel, [(x_t.shape, BF16)], (2 * 640 * 256 * 128, 800000))(
            *same, *other, ids, scalars, x_t, gain_square
        )
    return out.T


def solution(mesh):
    torus = Mesh(
        mesh.devices.reshape(mesh.shape["expert"], NY, NZ, mesh.shape["kv"]),
        ("expert", "tensor_0", "tensor_1", "kv"),
    )
    return jax.shard_map(
        shards,
        mesh=torus,
        in_specs=(
            P("expert", TENSOR_KV),
            P("expert", TENSOR_KV),
            P(TENSOR_KV),
            P("expert", None),
            P("expert", None),
            P("expert", TENSOR_KV, None),
            P("expert", TENSOR_KV, None),
            P("expert", TENSOR_KV, None),
        ),
        out_specs=P("expert", TENSOR_KV),
        check_vma=False,
    )
```

```python
import jax
import jax.numpy as jnp
from jax import lax
from jax.experimental import pallas as pl
from jax.experimental.pallas import tpu as pltpu
from jax.sharding import Mesh
from jax.sharding import PartitionSpec as P

D = 4096
CAP = 160
EPS = 1e-05
GROUPS = 4
NY = 4
NZ = 8
LANES = 128
ROWS = GROUPS * CAP
HALF = ROWS // 2
GAIN_ROWS = 16
XROWS = ROWS + GAIN_ROWS
TENSOR_KV = ("tensor_0", "tensor_1", "kv")
LINE = ("expert", "kv")
F32 = jnp.float32
BF16 = jnp.bfloat16
NT = (((1,), (1,)), ((), ()))
TN = (((0,), (0,)), ((), ()))
VMEM_LIMIT = 60 * 1024 * 1024


def call(kernel, outs, cost, scratch=()):
    flops, moved = cost
    return pl.pallas_call(
        kernel,
        out_shape=[jax.ShapeDtypeStruct(s, t) for s, t in outs],
        scratch_shapes=list(scratch),
        compiler_params=pltpu.CompilerParams(vmem_limit_bytes=VMEM_LIMIT),
        cost_estimate=pl.CostEstimate(flops=flops, bytes_accessed=moved, transcendentals=0),
    )


def slots_of(ids):
    tokens = ids.shape[1]
    first, second = ids[0:1], ids[1:2]
    groups = lax.broadcasted_iota(jnp.int32, (8, tokens), 0)
    named = jnp.where(first == groups, 1.0, 0.0) + jnp.where(second == groups, 1.0, 0.0)
    earlier = jnp.where(
        lax.broadcasted_iota(jnp.int32, (tokens, tokens), 0)
        < lax.broadcasted_iota(jnp.int32, (tokens, tokens), 1),
        1.0,
        0.0,
    ).astype(BF16)
    before = jnp.dot(named.astype(BF16), earlier, preferred_element_type=F32).astype(jnp.int32)
    at_first = jnp.sum(jnp.where(first == groups, before, 0), axis=0, keepdims=True)
    at_second = jnp.sum(jnp.where(second == groups, before, 0), axis=0, keepdims=True)
    return first * CAP + at_first, second * CAP + at_second


def dispatch_kernel(ids_ref, probs_ref, x_ref, grad_ref, gain_ref, out_ref):
    one, two = slots_of(ids_ref[...])
    tokens = ids_ref.shape[1]
    rows = lax.broadcasted_iota(jnp.int32, (ROWS, tokens), 0)
    x = x_ref[...]
    grad = grad_ref[...].astype(F32)
    probs = probs_ref[...]
    terms = []
    for slot, k in ((one, 0), (two, 1)):
        table = jnp.where(rows == slot, 1.0, 0.0).astype(BF16)
        values = jnp.concatenate([x, (grad * probs[k : k + 1]).astype(BF16)], axis=0)
        terms.append(lax.dot_general(table, values, NT, preferred_element_type=F32))
    routed = (terms[0] + terms[1]).astype(BF16)
    for e in range(GROUPS):
        for k in range(2):
            out_ref[e, k, pl.ds(0, CAP), :] = routed[e * CAP : (e + 1) * CAP]
            out_ref[e, k, pl.ds(CAP, GAIN_ROWS), :] = gain_ref[...]


def assemble_kernel(got_ref, out_ref):
    for g in range(GROUPS):
        low, high = got_ref[g, 0].astype(F32), got_ref[g, 1].astype(F32)
        x = jnp.concatenate([low[:, :64], high[:, :64]], axis=1).astype(BF16)
        grad = jnp.concatenate([low[:CAP, 64:], high[:CAP, 64:]], axis=1).astype(BF16)
        out_ref[pl.ds(g * CAP, CAP), :] = x[:CAP]
        if g == 0:
            out_ref[pl.ds(ROWS, GAIN_ROWS), :] = x[CAP:]
        out_ref[pl.ds(XROWS + g * CAP, CAP), :] = grad


def block(y, z):
    return pl.ds(pl.multiple_of((y * NZ + z) * LANES, LANES), LANES)


def column(a, b):
    y = lax.rem(lax.axis_index("tensor_0") + a, NY)
    z = lax.rem(lax.axis_index("tensor_1") + b, NZ)
    return block(y, z)


def forward_kernel(places, refs_of, n_pieces, begins, ends):
    def kernel(*refs):
        pieces, rest = refs[:n_pieces], list(refs[n_pieces:])
        wg_ref, wu_ref = rest[:2]
        rest = rest[2:]
        before = None
        if not begins:
            before, rest = rest[:3], rest[3:]
        gate_ref, up_ref, last_ref, xs_ref, wgs_ref, wus_ref, *more = rest
        sq_ref = more[0] if ends else last_ref

        def view(i, rows):
            ref, at = pieces[refs_of[i][0]], refs_of[i][1]
            return ref[rows, :] if at is None else ref[at, rows, :]

        for i, (a, b) in enumerate(places):
            here = pl.ds(i * LANES, LANES)
            wgs_ref[:, here] = wg_ref[:, column(a, b)]
            wus_ref[:, here] = wu_ref[:, column(a, b)]

        @pl.loop(0, ROWS // LANES)
        def _(r):
            rows = pl.ds(pl.multiple_of(r * LANES, LANES), LANES)
            total = jnp.zeros((LANES, LANES), F32) if begins else before[2][rows, :]
            for i in range(len(places)):
                v = view(i, rows).astype(F32)
                total = total + v * v
                gain = view(i, pl.ds(ROWS, GAIN_ROWS)).astype(F32)[0:1]
                xs_ref[rows, pl.ds(i * LANES, LANES)] = (v * gain).astype(BF16)
            sq_ref[rows, :] = total

        @pl.loop(0, 2)
        def _(r):
            rows = pl.ds(pl.multiple_of(r * HALF, HALF), HALF)
            x = xs_ref[rows, :]
            gate = lax.dot_general(x, wgs_ref[...], NT, preferred_element_type=F32)
            up = lax.dot_general(x, wus_ref[...], NT, preferred_element_type=F32)
            if not begins:
                gate, up = gate + before[0][rows, :], up + before[1][rows, :]
            if ends:
                inv = lax.rsqrt(jnp.sum(sq_ref[rows, :], axis=1, keepdims=True) / D + EPS)
                gate, up = gate * inv, up * inv
            gate_ref[rows, :] = gate
            up_ref[rows, :] = up

        if ends:
            for r in range(ROWS // LANES):
                rows = pl.ds(r * LANES, LANES)
                inv = lax.rsqrt(jnp.sum(sq_ref[rows, :], axis=1, keepdims=True) / D + EPS)
                last_ref[:, rows] = jnp.transpose(jnp.broadcast_to(inv, (LANES, LANES)))[0:1]

    return kernel


def hidden_kernel(places, refs_of, n_pieces, begins, ends):
    def kernel(*refs):
        pieces, rest = refs[:n_pieces], list(refs[n_pieces:])
        wd_ref, rest = rest[0], rest[1:]
        if not begins:
            act_ref, rest = rest[0], rest[1:]
        if ends:
            gate_ref, up_ref, gg_ref, ug_ref, p_ref, ds_ref, wds_ref, product_ref = rest
        else:
            out_ref, ds_ref, wds_ref = rest

        for i, (a, b) in enumerate(places):
            ref, at, start = pieces[refs_of[i][0]], refs_of[i][1], refs_of[i][2]
            here = pl.ds(i * LANES, LANES)
            rows = pl.ds(start, ROWS)
            ds_ref[:, here] = ref[rows, :] if at is None else ref[at, rows, :]
            wds_ref[:, here] = wd_ref[:, column(a, b)]

        @pl.loop(0, 2)
        def _(r):
            rows = pl.ds(pl.multiple_of(r * HALF, HALF), HALF)
            act = lax.dot_general(ds_ref[rows, :], wds_ref[...], NT, preferred_element_type=F32)
            if not begins:
                act = act + act_ref[rows, :]
            if not ends:
                out_ref[rows, :] = act
            else:
                gate, up = gate_ref[rows, :], up_ref[rows, :]
                sigma = jax.nn.sigmoid(gate)
                gg = (act * up * sigma * (1.0 + gate * (1.0 - sigma))).astype(BF16)
                ug = (act * (gate * sigma)).astype(BF16)
                gg_ref[rows, :] = gg
                ug_ref[rows, :] = ug
                product_ref[rows, :] = gg.astype(F32) * gate + ug.astype(F32) * up

        if ends:
            for r in range(ROWS // LANES):
                rows = pl.ds(r * LANES, LANES)
                sums = jnp.sum(product_ref[rows, :], axis=1, keepdims=True)
                p_ref[:, rows] = jnp.transpose(jnp.broadcast_to(sums, (LANES, LANES)))[0:1]

    return kernel


def back_products(gg_ref, ug_ref, wg_ref, wu_ref, rows, at):
    wg = jnp.concatenate([wg_ref[:, c] for c in at], axis=1)
    wu = jnp.concatenate([wu_ref[:, c] for c in at], axis=1)
    total = jnp.dot(gg_ref[rows, :], wg, preferred_element_type=F32) + jnp.dot(
        ug_ref[rows, :], wu, preferred_element_type=F32
    )
    return total.astype(BF16)


def back_top(refs, b, outs):
    z = lax.rem(lax.axis_index("tensor_1") + b, NZ)
    for y in range(0, NY, 2):
        total = back_products(*refs, pl.ds(0, HALF), [block(y, z), block(y + 1, z)])
        for j in range(2):
            ref, at = outs[y + j]
            ref[at] = total[:, j * LANES : (j + 1) * LANES]


def back_bottom(refs, a, outs):
    y = lax.rem(lax.axis_index("tensor_0") + a, NY)
    for z in range(0, NZ, 2):
        total = back_products(*refs, pl.ds(HALF, HALF), [block(y, z), block(y, z + 1)])
        for j in range(2):
            ref, at = outs[z + j]
            ref[at] = total[:, j * LANES : (j + 1) * LANES]


def back_far_kernel(gg, ug, wg, wu, a4lo, a4hi, b2lo, b2hi):
    refs = (gg, ug, wg, wu)
    back_top(refs, 4, [(a4lo, 0), (a4lo, 1), (a4hi, 0), (a4hi, 1)])
    back_bottom(refs, 2, [((b2lo, b2hi)[z // 4], z % 4) for z in range(NZ)])


def back_near_kernel(gg, ug, wg, wu, a3, a5, b1, b3, a2, a6, a1, a7, a0, b0):
    refs = (gg, ug, wg, wu)
    for b, ref in ((3, a3), (5, a5), (2, a2), (6, a6), (1, a1), (7, a7), (0, a0)):
        back_top(refs, b, [(ref, y) for y in range(NY)])
    for a, ref in ((1, b1), (3, b3), (0, b0)):
        back_bottom(refs, a, [(ref, z) for z in range(NZ)])


def combine_kernel(got_ref, ids_ref, scalars_ref, x_ref, gain_ref, out_ref):
    one, two = slots_of(ids_ref[...])
    tokens = ids_ref.shape[1]
    rows = lax.broadcasted_iota(jnp.int32, (ROWS, tokens), 0)
    table = jnp.where((rows == one) | (rows == two), 1.0, 0.0).astype(BF16)
    slot_grad = jnp.concatenate(
        [(got_ref[e, 0].astype(F32) + got_ref[e, 1].astype(F32)).astype(BF16) for e in range(GROUPS)], axis=0
    )
    both = lax.dot_general(slot_grad, table, TN, preferred_element_type=F32)
    token_grad = jnp.where(lax.axis_index("kv") == 0, both[:64], both[64:])
    value, found = scalars_ref[...], 0.0
    for _ in range(3):
        term = value.astype(BF16)
        value = value - term.astype(F32)
        found = found + jnp.dot(term, table, preferred_element_type=F32)
    coefficient = found[0:1]
    inverse_rms = 0.5 * found[1:2]
    gain = jnp.transpose(gain_ref[...].astype(F32))[:, 0:1]
    x = x_ref[...].astype(F32)
    out_ref[...] = (inverse_rms * (token_grad * gain) - x * coefficient).astype(BF16)


def shift(value, axis, by):
    n = lax.axis_size(axis)
    return lax.ppermute(value, axis, [(i, (i + by) % n) for i in range(n)])


def butterfly(value, axis, bit):
    n = lax.axis_size(axis)
    return value + lax.ppermute(value, axis, [(i, i ^ bit) for i in range(n)])


def gather_ring(value, axis, cut):
    n = lax.axis_size(axis)
    got = {0: value}
    right = left = value
    for step in range(1, n // 2):
        right, left = shift(right, axis, 1), shift(left, axis, -1)
        got[n - step], got[step] = right, left
    return got, (shift(right[:cut], axis, 1), shift(left[cut:], axis, -1))


def plus(a, b):
    return (a.astype(F32) + b.astype(F32)).astype(BF16)


def scatter_ring(own, far, axis, beside=None, after=()):
    n = lax.axis_size(axis)
    half = n // 2
    cut = far[0].shape[0]
    right, left = far
    for step in range(half, 0, -1):
        if step < half:
            to_right, to_left = own[step], own[n - step]
            if step == half - 1:
                right = jnp.concatenate([plus(right, to_right[:cut]), to_right[cut:]], axis=0)
                left = jnp.concatenate([to_left[:cut], plus(left, to_left[cut:])], axis=0)
            else:
                right, left = plus(right, to_right), plus(left, to_left)
        if half - step < len(after):
            right, left, beside = lax.optimization_barrier((right, left, beside))
        right, left = shift(right, axis, 1), shift(left, axis, -1)
        if half - step < len(after):
            beside = after[half - step](beside)
    total = (own[0].astype(F32) + right.astype(F32) + left.astype(F32)).astype(BF16)
    return total, beside


def exchange_sum(value, axis):
    got = lax.all_to_all(value, axis, 0, 0, tiled=True)
    return jnp.sum(got.astype(F32), axis=0).astype(BF16)


def shards(residual_stream, grad_output, norm_gain, expert_ids, gate_probs, w_gate, w_up, w_down):
    wg, wu, wd = w_gate[0], w_up[0], w_down[0]
    ids, probs = expert_ids.T, gate_probs.T
    x_t, grad_t = residual_stream.T, grad_output.T
    gain_rows = jnp.broadcast_to(jnp.concatenate([norm_gain, norm_gain])[None], (GAIN_ROWS, LANES))
    hidden = wg.shape[0]

    with jax.named_scope("dispatch"):
        [routed] = call(
            dispatch_kernel, [((GROUPS, 2, CAP + GAIN_ROWS, LANES), BF16)], (2 * 640 * 512 * 128, 800000)
        )(ids, probs, x_t, grad_t, gain_rows)
        routed = routed.reshape(2 * GROUPS, CAP + GAIN_ROWS, LANES)
        got = lax.all_to_all(routed, LINE, 0, 0, tiled=True)
        [piece] = call(assemble_kernel, [((XROWS + ROWS, LANES), BF16)], (0, 800000))(
            got.reshape(GROUPS, 2, CAP + GAIN_ROWS, LANES)
        )

    with jax.named_scope("gather_z"):
        z_got, (x_far, grad_far) = gather_ring(piece, "tensor_1", XROWS)
    with jax.named_scope("gather_x"):
        x_at = {b: v[:XROWS] for b, v in z_got.items()}
        x_at[4] = x_far
        first = jnp.stack([x_at[b] for b in (0, 1, 7)])
        second = jnp.stack([x_at[b] for b in (2, 3, 4, 5, 6)])
        f_got, f_far = gather_ring(first, "tensor_0", 2)
        s_got, s_far = gather_ring(second, "tensor_0", 2)
    with jax.named_scope("gather_grad"):
        d_got, d_far = gather_ring(piece[XROWS:], "tensor_0", HALF)
        line = jnp.stack([d_got[1], jnp.concatenate(d_far, axis=0), d_got[3]])
        g_got, g_far = gather_ring(line, "tensor_1", 2)

    near, rest = (0, 1, 7), (2, 3, 4, 5, 6)

    def forward(pieces, places, refs_of, before, ends):
        n = len(places) * LANES
        scratch = [pltpu.VMEM((ROWS, n), BF16), pltpu.VMEM((hidden, n), BF16), pltpu.VMEM((hidden, n), BF16)]
        return call(
            forward_kernel(places, refs_of, len(pieces), before is None, ends),
            [((ROWS, hidden), F32)] * 2 + [((1, ROWS), F32) if ends else ((ROWS, LANES), F32)],
            (4 * ROWS * n * hidden, 2 * ROWS * n + 2_000_000),
            scratch + ([pltpu.VMEM((ROWS, LANES), F32)] if ends else []),
        )(*pieces, wg, wu, *(before or ()))

    with jax.named_scope("forward"):
        state = forward(
            [z_got[b] if b != 4 else x_far for b in range(NZ)],
            [(0, b) for b in range(NZ)],
            [(b, None) for b in range(NZ)],
            None,
            False,
        )
        state = forward(
            [f_got[1], s_got[1], f_got[3], s_got[3]],
            [(a, b) for a in (1, 3) for b in near + rest],
            [(2 * i + j, at) for i in range(2) for j, part in enumerate((near, rest)) for at in range(len(part))],
            state,
            False,
        )
        gate, up, inv = forward(
            [*f_far, *s_far],
            [(2, b) for b in near + rest],
            [(0, 0), (0, 1), (1, 0), (2, 0), (2, 1), (3, 0), (3, 1), (3, 2)],
            state,
            True,
        )
    with jax.named_scope("hidden"):
        early = (0, 1, 2, 6, 7)
        places = [(0, b) for b in range(NZ)] + [(a, b) for b in early for a in (1, 2, 3)]
        refs_of = [(b, None, XROWS if b != 4 else 0) for b in range(NZ)]
        refs_of += [(NZ + i, at, 0) for i in range(len(early)) for at in range(3)]
        n = len(places) * LANES
        [act] = call(
            hidden_kernel(places, refs_of, NZ + len(early), True, False),
            [((ROWS, hidden), F32)],
            (2 * ROWS * n * hidden, 2 * ROWS * n + 2_000_000),
            [pltpu.VMEM((ROWS, n), BF16), pltpu.VMEM((hidden, n), BF16)],
        )(*[z_got[b] if b != 4 else grad_far for b in range(NZ)], *[g_got[b] for b in early], wd)
        places = [(a, b) for b in (3, 5, 4) for a in (1, 2, 3)]
        refs_of = [(i, at, 0) for i in range(2) for at in range(3)] + [(2, 0, 0), (2, 1, 0), (3, 0, 0)]
        n = len(places) * LANES
        gg, ug, p = call(
            hidden_kernel(places, refs_of, 4, False, True),
            [((ROWS, hidden), BF16), ((ROWS, hidden), BF16), ((1, ROWS), F32)],
            (2 * ROWS * n * hidden, 2 * ROWS * n + 4_000_000),
            [pltpu.VMEM((ROWS, n), BF16), pltpu.VMEM((hidden, n), BF16), pltpu.VMEM((ROWS, hidden), F32)],
        )(g_got[3], g_got[5], *g_far, wd, act, gate, up)

    flops = 4 * ROWS * D * hidden
    line_z, line_y = ((NY, HALF, LANES), BF16), ((NZ, HALF, LANES), BF16)
    half_z, half_y = ((NY // 2, HALF, LANES), BF16), ((NZ // 2, HALF, LANES), BF16)
    with jax.named_scope("back"):
        a4lo, a4hi, b2lo, b2hi = call(back_far_kernel, [half_z] * 2 + [half_y] * 2, (flops // 6, 4_000_000))(
            gg, ug, wg, wu
        )
        a3, a5, b1, b3, a2, a6, a1, a7, a0, b0 = call(
            back_near_kernel, [line_z] * 2 + [line_y] * 2 + [line_z] * 5 + [line_y], (flops, 8_000_000)
        )(gg, ug, wg, wu)

    steps = [
        lambda v, axis=axis, bit=bit: butterfly(v, axis, bit)
        for axis, bit in (
            ("tensor_1", 1),
            ("tensor_1", 2),
            ("tensor_1", 4),
            ("tensor_0", 1),
            ("tensor_0", 2),
            ("kv", 1),
        )
    ]
    with jax.named_scope("scatter_bottom"):
        low, _ = scatter_ring({0: b0, 1: b1, 3: b3}, (b2lo, b2hi), "tensor_0")
        low = exchange_sum(low, "tensor_1")
    with jax.named_scope("scatter_top"):
        top, p = scatter_ring(
            {0: a0, 1: a1, 2: a2, 3: a3, 5: a5, 6: a6, 7: a7}, (a4lo, a4hi), "tensor_1", p, steps[:4]
        )
        top = exchange_sum(top, "tensor_0")
    with jax.named_scope("projection_sum"):
        for step in steps[4:]:
            p = step(p)
        scalars = jnp.concatenate([inv * inv * p / D, inv], axis=0)
        scalars = jnp.stack([scalars[:, b * CAP : (b + 1) * CAP] for b in range(GROUPS)])
        scalars = lax.all_to_all(scalars, "expert", 0, 0, tiled=True)
        scalars = jnp.concatenate([scalars[e] for e in range(GROUPS)], axis=1)
        scalars = jnp.concatenate([scalars, jnp.zeros((6, ROWS), F32)], axis=0)

    with jax.named_scope("combine"):
        pieces = jnp.stack([top[:CAP], top[CAP:], low[:CAP], low[CAP:]])
        pieces = jnp.broadcast_to(pieces[:, None], (GROUPS, 2, CAP, LANES)).reshape(2 * GROUPS, CAP, LANES)
        got = lax.all_to_all(pieces, LINE, 0, 0, tiled=True).reshape(GROUPS, 2, CAP, LANES)
        gain_square = jnp.broadcast_to(norm_gain[None], (LANES, norm_gain.shape[0]))
        [out] = call(combine_kernel, [(x_t.shape, BF16)], (2 * 640 * 256 * 128, 800000))(
            got, ids, scalars, x_t, gain_square
        )
    return out.T


def solution(mesh):
    torus = Mesh(
        mesh.devices.reshape(mesh.shape["expert"], NY, NZ, mesh.shape["kv"]),
        ("expert", "tensor_0", "tensor_1", "kv"),
    )
    return jax.shard_map(
        shards,
        mesh=torus,
        in_specs=(
            P("expert", TENSOR_KV),
            P("expert", TENSOR_KV),
            P(TENSOR_KV),
            P("expert", None),
            P("expert", None),
            P("expert", TENSOR_KV, None),
            P("expert", TENSOR_KV, None),
            P("expert", TENSOR_KV, None),
        ),
        out_specs=P("expert", TENSOR_KV),
        check_vma=False,
    )
```

```python
import jax
import jax.numpy as jnp
from jax import lax
from jax.experimental import pallas as pl
from jax.experimental.pallas import tpu as pltpu
from jax.sharding import Mesh
from jax.sharding import PartitionSpec as P

D = 4096
CAP = 160
EPS = 1e-05
GROUPS = 4
NY = 4
NZ = 8
LANES = 128
ROWS = GROUPS * CAP
HALF = ROWS // 2
GAIN_ROWS = 16
MINE = CAP // 2
XROWS = HALF + GAIN_ROWS
SPLIT = 144
PADDED = 384
PART = HALF // 2
EXTRA = 16
TENSOR_KV = ("tensor_0", "tensor_1", "kv")
LINE = ("expert", "kv")
F32 = jnp.float32
BF16 = jnp.bfloat16
NT = (((1,), (1,)), ((), ()))
TN = (((0,), (0,)), ((), ()))
VMEM_LIMIT = 60 * 1024 * 1024


def call(kernel, outs, us, scratch=()):
    return pl.pallas_call(
        kernel,
        out_shape=[jax.ShapeDtypeStruct(s, t) for s, t in outs],
        scratch_shapes=list(scratch),
        compiler_params=pltpu.CompilerParams(vmem_limit_bytes=VMEM_LIMIT),
        cost_estimate=pl.CostEstimate(flops=us * 1_000_000_000, bytes_accessed=0, transcendentals=0),
    )


def slots_of(ids):
    tokens = ids.shape[1]
    first, second = ids[0:1], ids[1:2]
    groups = lax.broadcasted_iota(jnp.int32, (8, tokens), 0)
    named = jnp.where(first == groups, 1.0, 0.0) + jnp.where(second == groups, 1.0, 0.0)
    earlier = jnp.where(
        lax.broadcasted_iota(jnp.int32, (tokens, tokens), 0)
        < lax.broadcasted_iota(jnp.int32, (tokens, tokens), 1),
        1.0,
        0.0,
    ).astype(BF16)
    before = jnp.dot(named.astype(BF16), earlier, preferred_element_type=F32).astype(jnp.int32)
    at_first = jnp.sum(jnp.where(first == groups, before, 0), axis=0, keepdims=True)
    at_second = jnp.sum(jnp.where(second == groups, before, 0), axis=0, keepdims=True)
    return first * CAP + at_first, second * CAP + at_second


def dispatch_kernel(ids_ref, probs_ref, x_ref, grad_ref, gain_ref, out_ref):
    one, two = slots_of(ids_ref[...])
    tokens = ids_ref.shape[1]
    rows = lax.broadcasted_iota(jnp.int32, (ROWS, tokens), 0)
    x = x_ref[...]
    grad = grad_ref[...].astype(F32)
    probs = probs_ref[...]
    terms = []
    for slot, k in ((one, 0), (two, 1)):
        table = jnp.where(rows == slot, 1.0, 0.0).astype(BF16)
        values = jnp.concatenate([(grad * probs[k : k + 1]).astype(BF16), x], axis=0)
        terms.append(lax.dot_general(table, values, NT, preferred_element_type=F32))
    routed = terms[0] + terms[1]
    low = lax.broadcasted_iota(jnp.int32, (MINE, LANES), 1) < LANES // 2
    gain = jnp.broadcast_to(gain_ref[0:1, :].astype(F32), (MINE, LANES))
    for e in range(GROUPS):
        first = routed[e * CAP : e * CAP + MINE]
        second = routed[e * CAP + MINE : (e + 1) * CAP]
        for k in range(2):
            top = first if k == 0 else jnp.where(low, first, second)
            out_ref[e, k, pl.ds(0, MINE), :] = top.astype(BF16)
            out_ref[e, k, pl.ds(MINE, MINE), :] = jnp.where(low, second, gain).astype(BF16)


def assemble_kernel(got_ref, a_ref, b_ref):
    grads = []
    for g in range(GROUPS):
        low, high = got_ref[g, 0].astype(F32), got_ref[g, 1].astype(F32)
        x = jnp.concatenate([low[:, 64:], high[:, 64:]], axis=1).astype(BF16)
        grads.append(jnp.concatenate([low[:, :64], high[:, :64]], axis=1).astype(BF16))
        a_ref[pl.ds(g * MINE, MINE), :] = x[:MINE]
        if g == 0:
            a_ref[pl.ds(HALF, GAIN_ROWS), :] = x[MINE : MINE + GAIN_ROWS]
    a_ref[pl.ds(XROWS, SPLIT), :] = grads[0][:SPLIT]
    b_ref[pl.ds(0, CAP - SPLIT), :] = grads[0][SPLIT:]
    for g in range(1, GROUPS):
        b_ref[pl.ds(g * CAP - SPLIT, CAP), :] = grads[g]


def block(y, z):
    return pl.ds(pl.multiple_of((y * NZ + z) * LANES, LANES), LANES)


def column(a, b):
    y = lax.rem(lax.axis_index("tensor_0") + a, NY)
    z = lax.rem(lax.axis_index("tensor_1") + b, NZ)
    return block(y, z)


def a_piece(refs, a, b):
    x0, x1, x3, lo, hi = refs
    if a == 2:
        return (lo, b) if b < NZ // 2 else (hi, b - NZ // 2)
    return (x0, x1, None, x3)[a], b


def b_piece(refs, a, b):
    if b == NZ // 2:
        return refs[NZ - 1 + a // 2], a % 2
    return refs[b if b < NZ // 2 else b - 1], a


PLACES = [(a, b) for a in range(NY) for b in range(NZ)]


def act_kernel(*refs):
    a_refs, b_refs = refs[:5], refs[5:14]
    wd_ref, mine_ref, theirs_ref, grad_ref, act_ref = refs[14:]
    for a, b in PLACES:
        ref, at = a_piece(a_refs, a, b)
        grad_ref[pl.ds(0, SPLIT), column(a, b)] = ref[at, pl.ds(XROWS, SPLIT), :]
        ref, at = b_piece(b_refs, a, b)
        grad_ref[pl.ds(SPLIT, ROWS - SPLIT), column(a, b)] = ref[at]

    @pl.loop(0, 2)
    def _(r):
        rows = pl.ds(pl.multiple_of(r * HALF, HALF), HALF)
        act_ref[rows, :] = lax.dot_general(grad_ref[rows, :], wd_ref[...], NT, preferred_element_type=F32)

    kv = lax.axis_index("kv")
    for g in range(GROUPS):
        here = pl.ds(g * MINE, MINE)
        mine_ref[here, :] = act_ref[pl.ds(pl.multiple_of(g * CAP + kv * MINE, 16), MINE), :]
        theirs_ref[here, :] = act_ref[pl.ds(pl.multiple_of(g * CAP + (1 - kv) * MINE, 16), MINE), :].astype(BF16)


def to_row(column_ref, row_ref):
    for r in range(PADDED // LANES):
        rows = pl.ds(r * LANES, LANES)
        row_ref[:, rows] = jnp.transpose(column_ref[rows, :])[0:1]


def forward_kernel(*refs):
    a_refs = refs[:5]
    wg_ref, wu_ref, wgp_ref, wup_ref, gate_ref, up_ref, gatep_ref, upp_ref, inv_ref, xn_ref, column_ref = refs[5:]

    @pl.loop(0, HALF // 64)
    def _(r):
        rows = pl.ds(pl.multiple_of(r * 64, 64), 64)
        total = jnp.zeros((64, LANES), F32)
        for a, b in PLACES:
            ref, at = a_piece(a_refs, a, b)
            v = ref[at, rows, :].astype(F32)
            total = total + v * v
        inv = lax.rsqrt(jnp.sum(total, axis=1, keepdims=True) / D + EPS)
        column_ref[rows, :] = jnp.broadcast_to(inv, (64, LANES))
        for a, b in PLACES:
            ref, at = a_piece(a_refs, a, b)
            gain = ref[at, pl.ds(HALF, GAIN_ROWS), :].astype(F32)[0:1]
            xn_ref[rows, column(a, b)] = (ref[at, rows, :].astype(F32) * inv * gain).astype(BF16)

    column_ref[pl.ds(HALF, PADDED - HALF), :] = jnp.zeros((PADDED - HALF, LANES), F32)
    to_row(column_ref, inv_ref)
    x = xn_ref[...]
    for w_ref, out_ref in ((wg_ref, gate_ref), (wu_ref, up_ref), (wgp_ref, gatep_ref), (wup_ref, upp_ref)):
        out_ref[...] = lax.dot_general(x, w_ref[...], NT, preferred_element_type=F32)


def split3(value):
    terms = []
    for _ in range(3):
        terms.append(value.astype(BF16))
        value = value - terms[-1].astype(F32)
    return terms


def back_products(gs, ws, rows, a, outs):
    y = lax.rem(lax.axis_index("tensor_0") + a, NY)
    for z in range(0, NZ, 2):
        at = pl.ds(pl.multiple_of((y * NZ + z) * LANES, 2 * LANES), 2 * LANES)
        total = 0.0
        for g_ref, w_ref in zip(gs, ws):
            total = total + jnp.dot(g_ref[rows, :], w_ref[:, at], preferred_element_type=F32)
        total = total.astype(BF16)
        outs[a][z, pl.ds(0, PART), :] = total[:, :LANES]
        outs[a][z + 1, pl.ds(0, PART), :] = total[:, LANES:]


def carried(rows):
    terms = [t.astype(F32) for t in split3(rows)]
    return jnp.concatenate(terms + [jnp.zeros((7, LANES), F32)], axis=0).astype(BF16)


def gathered_up(carried_sum):
    return carried_sum[0:3] + carried_sum[3:6] + carried_sum[6:9]


def first_kernel(*refs):
    gate_ref, up_ref, gatep_ref, upp_ref, act_ref, actp_ref, *ws = refs[:10]
    gg_ref, ug_ref, ggp_ref, ugp_ref, *outs, column_ref = refs[10:]
    sums = 0.0
    for gate_in, up_in, act_in, gg_out, ug_out in (
        (gate_ref, up_ref, act_ref, gg_ref, ug_ref),
        (gatep_ref, upp_ref, actp_ref, ggp_ref, ugp_ref),
    ):
        gate, up, act = gate_in[...], up_in[...], act_in[...].astype(F32)
        sigma = jax.nn.sigmoid(gate)
        gg = (act * up * sigma * (1.0 + gate * (1.0 - sigma))).astype(BF16)
        ug = (act * (gate * sigma)).astype(BF16)
        gg_out[...] = gg
        ug_out[...] = ug
        sums = sums + jnp.sum(gg.astype(F32) * gate + ug.astype(F32) * up, axis=1, keepdims=True)
    column_ref[pl.ds(0, HALF), :] = jnp.broadcast_to(sums, (HALF, LANES))
    column_ref[pl.ds(HALF, PADDED - HALF), :] = jnp.zeros((PADDED - HALF, LANES), F32)
    rows = [jnp.transpose(column_ref[pl.ds(r * LANES, LANES), :])[0:1] for r in range(PADDED // LANES)]
    projection = carried(jnp.concatenate(rows, axis=0))
    for a in (2, 1, 3, 0):
        back_products((gg_ref, ug_ref, ggp_ref, ugp_ref), ws, pl.ds(0, PART), a, outs)
        for z in range(NZ):
            outs[a][z, pl.ds(PART, EXTRA), :] = projection


def second_kernel(gg_ref, ug_ref, ggp_ref, ugp_ref, wg_ref, wu_ref, wgp_ref, wup_ref, *outs):
    for a in (2, 1, 3, 0):
        back_products(
            (gg_ref, ug_ref, ggp_ref, ugp_ref), (wg_ref, wu_ref, wgp_ref, wup_ref), pl.ds(PART, PART), a, outs
        )


def sum_first_kernel(*refs):
    *shares, out_ref = refs
    for z in range(NZ):
        total = 0.0
        for ref in shares:
            total = total + ref[z].astype(F32)
        out_ref[z, pl.ds(0, PART), :] = total[:PART].astype(BF16)
        out_ref[z, pl.ds(PART, EXTRA), :] = carried(gathered_up(total[PART:]))


def sum_second_kernel(*refs):
    *shares, out_ref = refs
    for z in range(NZ):
        total = 0.0
        for ref in shares:
            total = total + ref[z].astype(F32)
        out_ref[z] = total.astype(BF16)


def finish_kernel(first_ref, second_ref, inv_ref, out_ref):
    first, second = first_ref[0].astype(F32), second_ref[0].astype(F32)
    for z in range(1, NZ):
        first = first + first_ref[z].astype(F32)
        second = second + second_ref[z].astype(F32)
    rows = gathered_up(first[PART:])
    projection = jnp.concatenate([rows[r : r + 1] for r in range(PADDED // LANES)], axis=1)
    inv = inv_ref[...]
    terms = split3(inv * inv * projection / D) + split3(inv)
    terms = jnp.concatenate([t.astype(F32) for t in terms] + [jnp.zeros((10, PADDED), F32)], axis=0)
    for b in range(GROUPS):
        here = (first, second)[b // 2][(b % 2) * MINE : (b % 2 + 1) * MINE].astype(BF16)
        scalars = terms[:, b * MINE : b * MINE + LANES]
        for k in range(2):
            out_ref[2 * b + k, pl.ds(0, MINE), :] = here
            out_ref[2 * b + k, pl.ds(MINE, EXTRA), :] = scalars.astype(BF16)


def combine_kernel(got_ref, ids_ref, x_ref, gain_ref, out_ref):
    one, two = slots_of(ids_ref[...])
    tokens = ids_ref.shape[1]
    rows = lax.broadcasted_iota(jnp.int32, (ROWS, tokens), 0)
    table = jnp.where((rows == one) | (rows == two), 1.0, 0.0).astype(BF16)
    slot_grad = jnp.concatenate([got_ref[i, pl.ds(0, MINE), :] for i in range(2 * GROUPS)], axis=0)
    both = lax.dot_general(slot_grad, table, TN, preferred_element_type=F32)
    token_grad = jnp.where(lax.axis_index("kv") == 0, both[:64], both[64:])
    scalars = jnp.concatenate(
        [got_ref[i, pl.ds(MINE, EXTRA), :].astype(F32)[:, :MINE] for i in range(2 * GROUPS)], axis=1
    )
    found = jnp.dot(scalars.astype(BF16), table, preferred_element_type=F32)
    coefficient = found[0:1] + found[1:2] + found[2:3]
    inverse_rms = 0.5 * (found[3:4] + found[4:5] + found[5:6])
    gain = jnp.transpose(gain_ref[...].astype(F32))[:, 0:1]
    x = x_ref[...].astype(F32)
    out_ref[...] = (inverse_rms * (token_grad * gain) - x * coefficient).astype(BF16)


def shift(value, axis, by):
    n = lax.axis_size(axis)
    return lax.ppermute(value, axis, [(i, (i + by) % n) for i in range(n)])


def gather_ring(value, axis, cut, meet=None):
    n = lax.axis_size(axis)
    got = {0: value}
    right = left = value
    for step in range(1, n // 2):
        right, left = shift(right, axis, 1), shift(left, axis, -1)
        got[n - step], got[step] = right, left
    if meet is not None:
        right, left, meet = lax.optimization_barrier((right, left, meet))
    far = (shift(right[:cut], axis, 1), shift(left[cut:], axis, -1))
    return got, far, meet


def shards(residual_stream, grad_output, norm_gain, expert_ids, gate_probs, w_gate, w_up, w_down):
    wg, wu, wd = w_gate[0], w_up[0], w_down[0]
    ids, probs = expert_ids.T, gate_probs.T
    x_t, grad_t = residual_stream.T, grad_output.T
    gain_rows = jnp.broadcast_to(jnp.concatenate([norm_gain, norm_gain])[None], (GAIN_ROWS, LANES))
    hidden = wg.shape[0]

    with jax.named_scope("weights"):
        wgp = shift(wg, "kv", 1)

    with jax.named_scope("dispatch"):
        [routed] = call(dispatch_kernel, [((GROUPS, 2, CAP, LANES), BF16)], 2)(
            ids, probs, x_t, grad_t, gain_rows
        )
        got = lax.all_to_all(routed.reshape(2 * GROUPS, CAP, LANES), LINE, 0, 0, tiled=True)
        piece_a, piece_b = call(
            assemble_kernel, [((XROWS + SPLIT, LANES), BF16), ((ROWS - SPLIT, LANES), BF16)], 2
        )(got.reshape(GROUPS, 2, CAP, LANES))

    with jax.named_scope("gather_a"):
        z_got, z_far, wgp = gather_ring(piece_a, "tensor_1", (XROWS + SPLIT) // 2, wgp)
        later, wgp = lax.optimization_barrier((wu, wgp))
        wup = shift(later, "kv", 1)
        z_got[4] = jnp.concatenate(z_far, axis=0)
        line = jnp.stack([z_got[b] for b in range(NZ)])
        a_got, a_far, wup = gather_ring(line, "tensor_0", NZ // 2, wup)
        a_refs = (a_got[0], a_got[1], a_got[3], *a_far)
    with jax.named_scope("gather_b"):
        line = jnp.stack([piece_b] + [shift(piece_b, "tensor_0", -a) for a in (1, 2, 3)])
        line, _ = lax.optimization_barrier((line, z_got[2]))
        b_got, b_far, _ = gather_ring(line, "tensor_1", NY // 2)
        b_refs = (*[b_got[b] for b in range(NZ) if b != 4], *b_far)

    with jax.named_scope("act"):
        act, theirs = call(
            act_kernel,
            [((HALF, hidden), F32), ((HALF, hidden), BF16)],
            7,
            [pltpu.VMEM((ROWS, D), BF16), pltpu.VMEM((ROWS, hidden), F32)],
        )(*a_refs, *b_refs, wd)
        actp = shift(theirs, "kv", 1)
    with jax.named_scope("forward"):
        gate, up, gatep, upp, inv = call(
            forward_kernel,
            [((HALF, hidden), F32)] * 4 + [((1, PADDED), F32)],
            8,
            [pltpu.VMEM((HALF, D), BF16), pltpu.VMEM((PADDED, LANES), F32)],
        )(*a_refs, wg, wu, wgp, wup)
    with jax.named_scope("back"):
        gg, ug, ggp, ugp, *first = call(
            first_kernel,
            [((HALF, hidden), BF16)] * 4 + [((NZ, PART + EXTRA, LANES), BF16)] * NY,
            5,
            [pltpu.VMEM((PADDED, LANES), F32)],
        )(gate, up, gatep, upp, act, actp, wg, wu, wgp, wup)
        second = call(second_kernel, [((NZ, PART, LANES), BF16)] * NY, 4)(
            gg, ug, ggp, ugp, wg, wu, wgp, wup
        )
    with jax.named_scope("scatter"):
        own_first, own_second = lax.optimization_barrier((first[0], second[0]))
        first = [own_first] + [shift(first[a], "tensor_0", a) for a in (2, 1, 3)]
        second = [own_second] + [shift(second[a], "tensor_0", a) for a in (2, 1, 3)]
        [first] = call(sum_first_kernel, [((NZ, PART + EXTRA, LANES), BF16)], 3)(*first)
        first = lax.all_to_all(first, "tensor_1", 0, 0, tiled=True)
        [second] = call(sum_second_kernel, [((NZ, PART, LANES), BF16)], 3)(*second)
        first, second = lax.optimization_barrier((first, second))
        second = lax.all_to_all(second, "tensor_1", 0, 0, tiled=True)

    with jax.named_scope("combine"):
        [pieces] = call(finish_kernel, [((2 * GROUPS, MINE + EXTRA, LANES), BF16)], 2)(first, second, inv)
        got = lax.all_to_all(pieces, LINE, 0, 0, tiled=True)
        gain_square = jnp.broadcast_to(norm_gain[None], (LANES, norm_gain.shape[0]))
        [out] = call(combine_kernel, [(x_t.shape, BF16)], 2)(
            got, ids, x_t, gain_square
        )
    return out.T


def solution(mesh):
    torus = Mesh(
        mesh.devices.reshape(mesh.shape["expert"], NY, NZ, mesh.shape["kv"]),
        ("expert", "tensor_0", "tensor_1", "kv"),
    )
    return jax.shard_map(
        shards,
        mesh=torus,
        in_specs=(
            P("expert", TENSOR_KV),
            P("expert", TENSOR_KV),
            P(TENSOR_KV),
            P("expert", None),
            P("expert", None),
            P("expert", TENSOR_KV, None),
            P("expert", TENSOR_KV, None),
            P("expert", TENSOR_KV, None),
        ),
        out_specs=P("expert", TENSOR_KV),
        check_vma=False,
    )
```

```python
import jax
import jax.numpy as jnp
from jax import lax
from jax.experimental import pallas as pl
from jax.experimental.pallas import tpu as pltpu
from jax.sharding import Mesh
from jax.sharding import PartitionSpec as P

D = 4096
CAP = 160
EPS = 1e-05
GROUPS = 4
NY = 4
NZ = 8
LANES = 128
ROWS = GROUPS * CAP
HALF = ROWS // 2
GAIN_ROWS = 16
MINE = CAP // 2
XROWS = HALF + GAIN_ROWS
SPLIT = 144
PADDED = 384
ZFIRST = 128
YFIRST = HALF - ZFIRST
EXTRA = 16
TENSOR_KV = ("tensor_0", "tensor_1", "kv")
LINE = ("expert", "kv")
F32 = jnp.float32
BF16 = jnp.bfloat16
NT = (((1,), (1,)), ((), ()))
TN = (((0,), (0,)), ((), ()))
VMEM_LIMIT = 60 * 1024 * 1024


def call(kernel, outs, us, scratch=()):
    return pl.pallas_call(
        kernel,
        out_shape=[jax.ShapeDtypeStruct(s, t) for s, t in outs],
        scratch_shapes=list(scratch),
        compiler_params=pltpu.CompilerParams(vmem_limit_bytes=VMEM_LIMIT),
        cost_estimate=pl.CostEstimate(flops=us * 1_000_000_000, bytes_accessed=0, transcendentals=0),
    )


def slots_of(ids):
    tokens = ids.shape[1]
    first, second = ids[0:1], ids[1:2]
    groups = lax.broadcasted_iota(jnp.int32, (8, tokens), 0)
    named = jnp.where(first == groups, 1.0, 0.0) + jnp.where(second == groups, 1.0, 0.0)
    earlier = jnp.where(
        lax.broadcasted_iota(jnp.int32, (tokens, tokens), 0)
        < lax.broadcasted_iota(jnp.int32, (tokens, tokens), 1),
        1.0,
        0.0,
    ).astype(BF16)
    before = jnp.dot(named.astype(BF16), earlier, preferred_element_type=F32).astype(jnp.int32)
    at_first = jnp.sum(jnp.where(first == groups, before, 0), axis=0, keepdims=True)
    at_second = jnp.sum(jnp.where(second == groups, before, 0), axis=0, keepdims=True)
    return first * CAP + at_first, second * CAP + at_second


def dispatch_kernel(ids_ref, probs_ref, x_ref, grad_ref, gain_ref, out_ref):
    one, two = slots_of(ids_ref[...])
    tokens = ids_ref.shape[1]
    rows = lax.broadcasted_iota(jnp.int32, (ROWS, tokens), 0)
    x = x_ref[...]
    grad = grad_ref[...].astype(F32)
    probs = probs_ref[...]
    terms = []
    for slot, k in ((one, 0), (two, 1)):
        table = jnp.where(rows == slot, 1.0, 0.0).astype(BF16)
        values = jnp.concatenate([(grad * probs[k : k + 1]).astype(BF16), x], axis=0)
        terms.append(lax.dot_general(table, values, NT, preferred_element_type=F32))
    routed = terms[0] + terms[1]
    low = lax.broadcasted_iota(jnp.int32, (MINE, LANES), 1) < LANES // 2
    gain = jnp.broadcast_to(gain_ref[0:1, :].astype(F32), (MINE, LANES))
    for e in range(GROUPS):
        first = routed[e * CAP : e * CAP + MINE]
        second = routed[e * CAP + MINE : (e + 1) * CAP]
        for k in range(2):
            top = first if k == 0 else jnp.where(low, first, second)
            out_ref[e, k, pl.ds(0, MINE), :] = top.astype(BF16)
            out_ref[e, k, pl.ds(MINE, MINE), :] = jnp.where(low, second, gain).astype(BF16)


def assemble_kernel(got_ref, a_ref, b_ref):
    grads = []
    for g in range(GROUPS):
        low, high = got_ref[g, 0].astype(F32), got_ref[g, 1].astype(F32)
        x = jnp.concatenate([low[:, 64:], high[:, 64:]], axis=1).astype(BF16)
        grads.append(jnp.concatenate([low[:, :64], high[:, :64]], axis=1).astype(BF16))
        a_ref[pl.ds(g * MINE, MINE), :] = x[:MINE]
        if g == 0:
            a_ref[pl.ds(HALF, GAIN_ROWS), :] = x[MINE : MINE + GAIN_ROWS]
    a_ref[pl.ds(XROWS, SPLIT), :] = grads[0][:SPLIT]
    b_ref[pl.ds(0, CAP - SPLIT), :] = grads[0][SPLIT:]
    for g in range(1, GROUPS):
        b_ref[pl.ds(g * CAP - SPLIT, CAP), :] = grads[g]


def block(y, z):
    return pl.ds(pl.multiple_of((y * NZ + z) * LANES, LANES), LANES)


def column(a, b):
    y = lax.rem(lax.axis_index("tensor_0") + a, NY)
    z = lax.rem(lax.axis_index("tensor_1") + b, NZ)
    return block(y, z)


def row_of(a, z):
    return block(lax.rem(lax.axis_index("tensor_0") + a, NY), z)


def a_piece(refs, a, b):
    if a == 0:
        return refs[0], b
    return refs[(None, 1, 5, 3)[a] + b // 4], b % 4


def b_piece(refs, a, b):
    if b == NZ // 2:
        return refs[NZ - 1 + a // 2], a % 2
    return refs[b if b < NZ // 2 else b - 1], a


PLACES = [(a, b) for a in range(NY) for b in range(NZ)]


def act_kernel(*refs):
    a_refs, b_refs = refs[:7], refs[7:16]
    wd_ref, mine_ref, theirs_ref, grad_ref, act_ref = refs[16:]
    for a, b in PLACES:
        ref, at = a_piece(a_refs, a, b)
        grad_ref[pl.ds(0, SPLIT), row_of(a, b)] = ref[at, pl.ds(XROWS, SPLIT), :]
        ref, at = b_piece(b_refs, a, b)
        grad_ref[pl.ds(SPLIT, ROWS - SPLIT), column(a, b)] = ref[at]

    @pl.loop(0, 2)
    def _(r):
        rows = pl.ds(pl.multiple_of(r * HALF, HALF), HALF)
        act_ref[rows, :] = lax.dot_general(grad_ref[rows, :], wd_ref[...], NT, preferred_element_type=F32)

    kv = lax.axis_index("kv")
    for g in range(GROUPS):
        here = pl.ds(g * MINE, MINE)
        mine_ref[here, :] = act_ref[pl.ds(pl.multiple_of(g * CAP + kv * MINE, 16), MINE), :]
        theirs_ref[here, :] = act_ref[pl.ds(pl.multiple_of(g * CAP + (1 - kv) * MINE, 16), MINE), :].astype(BF16)


def to_row(column_ref, row_ref):
    for r in range(PADDED // LANES):
        rows = pl.ds(r * LANES, LANES)
        row_ref[:, rows] = jnp.transpose(column_ref[rows, :])[0:1]


def forward_kernel(*refs):
    a_refs = refs[:7]
    wg_ref, wu_ref, wgp_ref, wup_ref, gate_ref, up_ref, gatep_ref, upp_ref, inv_ref, xn_ref, column_ref = refs[7:]

    @pl.loop(0, HALF // 64)
    def _(r):
        rows = pl.ds(pl.multiple_of(r * 64, 64), 64)
        total = jnp.zeros((64, LANES), F32)
        for a, b in PLACES:
            ref, at = a_piece(a_refs, a, b)
            v = ref[at, rows, :].astype(F32)
            total = total + v * v
        inv = lax.rsqrt(jnp.sum(total, axis=1, keepdims=True) / D + EPS)
        column_ref[rows, :] = jnp.broadcast_to(inv, (64, LANES))
        for a, b in PLACES:
            ref, at = a_piece(a_refs, a, b)
            gain = ref[at, pl.ds(HALF, GAIN_ROWS), :].astype(F32)[0:1]
            xn_ref[rows, row_of(a, b)] = (ref[at, rows, :].astype(F32) * inv * gain).astype(BF16)

    column_ref[pl.ds(HALF, PADDED - HALF), :] = jnp.zeros((PADDED - HALF, LANES), F32)
    to_row(column_ref, inv_ref)
    x = xn_ref[...]
    for w_ref, out_ref in ((wg_ref, gate_ref), (wu_ref, up_ref), (wgp_ref, gatep_ref), (wup_ref, upp_ref)):
        out_ref[...] = lax.dot_general(x, w_ref[...], NT, preferred_element_type=F32)


def split3(value):
    terms = []
    for _ in range(3):
        terms.append(value.astype(BF16))
        value = value - terms[-1].astype(F32)
    return terms


def carried(rows):
    terms = [t.astype(F32) for t in split3(rows)]
    return jnp.concatenate(terms + [jnp.zeros((7, LANES), F32)], axis=0).astype(BF16)


def gathered_up(carried_sum):
    return carried_sum[0:3] + carried_sum[3:6] + carried_sum[6:9]


def back_kernel(*refs):
    gate_ref, up_ref, gatep_ref, upp_ref, act_ref, actp_ref, *ws = refs[:10]
    top_ref, *outs, gg_ref, ug_ref, ggp_ref, ugp_ref, column_ref = refs[10:]
    sums = 0.0
    for gate_in, up_in, act_in, gg_out, ug_out in (
        (gate_ref, up_ref, act_ref, gg_ref, ug_ref),
        (gatep_ref, upp_ref, actp_ref, ggp_ref, ugp_ref),
    ):
        gate, up, act = gate_in[...], up_in[...], act_in[...].astype(F32)
        sigma = jax.nn.sigmoid(gate)
        gg = (act * up * sigma * (1.0 + gate * (1.0 - sigma))).astype(BF16)
        ug = (act * (gate * sigma)).astype(BF16)
        gg_out[...] = gg
        ug_out[...] = ug
        sums = sums + jnp.sum(gg.astype(F32) * gate + ug.astype(F32) * up, axis=1, keepdims=True)
    column_ref[pl.ds(0, HALF), :] = jnp.broadcast_to(sums, (HALF, LANES))
    column_ref[pl.ds(HALF, PADDED - HALF), :] = jnp.zeros((PADDED - HALF, LANES), F32)
    rows = [jnp.transpose(column_ref[pl.ds(r * LANES, LANES), :])[0:1] for r in range(PADDED // LANES)]
    projection = carried(jnp.concatenate(rows, axis=0))
    gs = (gg_ref, ug_ref, ggp_ref, ugp_ref)
    for a in range(NY):
        y = lax.rem(lax.axis_index("tensor_0") + a, NY)
        for z in range(0, NZ, 2):
            at = pl.ds(pl.multiple_of((y * NZ + z) * LANES, 2 * LANES), 2 * LANES)
            total = 0.0
            for g_ref, w_ref in zip(gs, ws):
                total = total + jnp.dot(g_ref[...], w_ref[:, at], preferred_element_type=F32)
            total = total.astype(BF16)
            for k in range(2):
                part = total[:, k * LANES : (k + 1) * LANES]
                top_ref[z + k, a] = part[:ZFIRST]
                outs[a][z + k, pl.ds(0, YFIRST), :] = part[ZFIRST:]
                outs[a][z + k, pl.ds(YFIRST, EXTRA), :] = projection


def sum_top_kernel(got_ref, *outs):
    for a in range(NY):
        total = got_ref[0, a].astype(F32)
        for z in range(1, NZ):
            total = total + got_ref[z, a].astype(F32)
        outs[a][...] = total.astype(BF16)


def sum_low_kernel(*refs):
    *shares, out_ref = refs
    for z in range(NZ):
        total = 0.0
        for ref in shares:
            total = total + ref[z].astype(F32)
        out_ref[z, pl.ds(0, YFIRST), :] = total[:YFIRST].astype(BF16)
        out_ref[z, pl.ds(YFIRST, EXTRA), :] = carried(gathered_up(total[YFIRST:]))


def finish_kernel(*refs):
    *tops, low_ref, inv_ref, out_ref = refs
    top, low = 0.0, low_ref[0].astype(F32)
    for ref in tops:
        top = top + ref[...].astype(F32)
    for z in range(1, NZ):
        low = low + low_ref[z].astype(F32)
    slot_grad = jnp.concatenate([top, low[:YFIRST]], axis=0).astype(BF16)
    rows = gathered_up(low[YFIRST:])
    projection = jnp.concatenate([rows[r : r + 1] for r in range(PADDED // LANES)], axis=1)
    inv = inv_ref[...]
    terms = split3(inv * inv * projection / D) + split3(inv)
    terms = jnp.concatenate([t.astype(F32) for t in terms] + [jnp.zeros((10, PADDED), F32)], axis=0)
    for b in range(GROUPS):
        here = slot_grad[b * MINE : (b + 1) * MINE]
        scalars = terms[:, b * MINE : b * MINE + LANES].astype(BF16)
        for k in range(2):
            out_ref[2 * b + k, pl.ds(0, MINE), :] = here
            out_ref[2 * b + k, pl.ds(MINE, EXTRA), :] = scalars


def combine_kernel(got_ref, ids_ref, x_ref, gain_ref, out_ref):
    one, two = slots_of(ids_ref[...])
    tokens = ids_ref.shape[1]
    rows = lax.broadcasted_iota(jnp.int32, (ROWS, tokens), 0)
    table = jnp.where((rows == one) | (rows == two), 1.0, 0.0).astype(BF16)
    slot_grad = jnp.concatenate([got_ref[i, pl.ds(0, MINE), :] for i in range(2 * GROUPS)], axis=0)
    both = lax.dot_general(slot_grad, table, TN, preferred_element_type=F32)
    token_grad = jnp.where(lax.axis_index("kv") == 0, both[:64], both[64:])
    scalars = jnp.concatenate(
        [got_ref[i, pl.ds(MINE, EXTRA), :].astype(F32)[:, :MINE] for i in range(2 * GROUPS)], axis=1
    )
    found = jnp.dot(scalars.astype(BF16), table, preferred_element_type=F32)
    coefficient = found[0:1] + found[1:2] + found[2:3]
    inverse_rms = 0.5 * (found[3:4] + found[4:5] + found[5:6])
    gain = jnp.transpose(gain_ref[...].astype(F32))[:, 0:1]
    x = x_ref[...].astype(F32)
    out_ref[...] = (inverse_rms * (token_grad * gain) - x * coefficient).astype(BF16)


def shift(value, axis, by):
    n = lax.axis_size(axis)
    return lax.ppermute(value, axis, [(i, (i + by) % n) for i in range(n)])


def gather_ring(value, axis, cut, meet=lambda step, right, left: (right, left)):
    n = lax.axis_size(axis)
    got = {0: value}
    right = left = value
    for step in range(1, n // 2):
        right, left = meet(step, right, left)
        right, left = shift(right, axis, 1), shift(left, axis, -1)
        got[n - step], got[step] = right, left
    right, left = meet(n // 2, right, left)
    return got, (shift(right[:cut], axis, 1), shift(left[cut:], axis, -1))


def shards(residual_stream, grad_output, norm_gain, expert_ids, gate_probs, w_gate, w_up, w_down):
    wg, wu, wd = w_gate[0], w_up[0], w_down[0]
    ids, probs = expert_ids.T, gate_probs.T
    x_t, grad_t = residual_stream.T, grad_output.T
    gain_rows = jnp.broadcast_to(jnp.concatenate([norm_gain, norm_gain])[None], (GAIN_ROWS, LANES))
    hidden = wg.shape[0]

    with jax.named_scope("dispatch"):
        [routed] = call(dispatch_kernel, [((GROUPS, 2, CAP, LANES), BF16)], 2)(
            ids, probs, x_t, grad_t, gain_rows
        )
        got = lax.all_to_all(routed.reshape(2 * GROUPS, CAP, LANES), LINE, 0, 0, tiled=True)
        got, own_wg = lax.optimization_barrier((got, wg))
        piece_a, piece_b = call(
            assemble_kernel, [((XROWS + SPLIT, LANES), BF16), ((ROWS - SPLIT, LANES), BF16)], 2
        )(got.reshape(GROUPS, 2, CAP, LANES))

    with jax.named_scope("weights"):
        wgp = shift(own_wg, "kv", 1)
    with jax.named_scope("gather"):
        copies = jnp.broadcast_to(piece_a[None], (NZ, *piece_a.shape))
        line_a = lax.all_to_all(copies, "tensor_1", 0, 0, tiled=True)
        line_b = jnp.stack([piece_b] + [shift(piece_b, "tensor_0", -a) for a in (1, 2, 3)])

        near, far = [], []

        def meet(step, right, left):
            nonlocal line_a, wgp
            if step == 2:
                right, left, line_a = lax.optimization_barrier((right, left, line_a))
                near[:] = [shift(line_a[: NZ // 2], "tensor_0", by) for by in (1, -1)]
                far[:] = [shift(line_a[NZ // 2 :], "tensor_0", by) for by in (1, -1)]
            if step == 3:
                right, left, wgp, *near[:] = lax.optimization_barrier((right, left, wgp, *near))
            if step == 4:
                right, left, *far[:] = lax.optimization_barrier((right, left, *far))
            return right, left

        b_got, b_far = gather_ring(line_b, "tensor_1", NY // 2, meet)
        b_refs = (*[b_got[b] for b in range(NZ) if b != 4], *b_far)
        a_far = (shift(near[0], "tensor_0", 1), shift(far[1], "tensor_0", -1))
        a_refs = (line_a, near[1], far[1], near[0], far[0], *a_far)
    with jax.named_scope("weights"):
        wgp, own_wu = lax.optimization_barrier((wgp, wu))
        wup = shift(own_wu, "kv", 1)

    with jax.named_scope("act"):
        wd, wgp, wup = lax.optimization_barrier((wd, wgp, wup))
        act, theirs = call(
            act_kernel,
            [((HALF, hidden), F32), ((HALF, hidden), BF16)],
            7,
            [pltpu.VMEM((ROWS, D), BF16), pltpu.VMEM((ROWS, hidden), F32)],
        )(*a_refs, *b_refs, wd)
        actp = shift(theirs, "kv", 1)
    with jax.named_scope("forward"):
        gate, up, gatep, upp, inv = call(
            forward_kernel,
            [((HALF, hidden), F32)] * 4 + [((1, PADDED), F32)],
            8,
            [pltpu.VMEM((HALF, D), BF16), pltpu.VMEM((PADDED, LANES), F32)],
        )(*a_refs, wg, wu, wgp, wup)
    with jax.named_scope("back"):
        top, *low = call(
            back_kernel,
            [((NZ, NY, ZFIRST, LANES), BF16)] + [((NZ, YFIRST + EXTRA, LANES), BF16)] * NY,
            8,
            [pltpu.VMEM((HALF, hidden), BF16)] * 4 + [pltpu.VMEM((PADDED, LANES), F32)],
        )(gate, up, gatep, upp, act, actp, wg, wu, wgp, wup)
    with jax.named_scope("scatter"):
        top = lax.all_to_all(top, "tensor_1", 0, 0, tiled=True)
        low = [low[0]] + [shift(low[a], "tensor_0", a) for a in (2, 1, 3)]
        [low] = call(sum_low_kernel, [((NZ, YFIRST + EXTRA, LANES), BF16)], 3)(*low)
        top, low = lax.optimization_barrier((top, low))
        top = call(sum_top_kernel, [((ZFIRST, LANES), BF16)] * NY, 3)(top)
        low = lax.all_to_all(low, "tensor_1", 0, 0, tiled=True)
        top = [top[0]] + [shift(top[a], "tensor_0", a) for a in (2, 1, 3)]

    with jax.named_scope("combine"):
        [pieces] = call(finish_kernel, [((2 * GROUPS, MINE + EXTRA, LANES), BF16)], 2)(*top, low, inv)
        got = lax.all_to_all(pieces, LINE, 0, 0, tiled=True)
        gain_square = jnp.broadcast_to(norm_gain[None], (LANES, norm_gain.shape[0]))
        [out] = call(combine_kernel, [(x_t.shape, BF16)], 2)(
            got, ids, x_t, gain_square
        )
    return out.T


def solution(mesh):
    torus = Mesh(
        mesh.devices.reshape(mesh.shape["expert"], NY, NZ, mesh.shape["kv"]),
        ("expert", "tensor_0", "tensor_1", "kv"),
    )
    return jax.shard_map(
        shards,
        mesh=torus,
        in_specs=(
            P("expert", TENSOR_KV),
            P("expert", TENSOR_KV),
            P(TENSOR_KV),
            P("expert", None),
            P("expert", None),
            P("expert", TENSOR_KV, None),
            P("expert", TENSOR_KV, None),
            P("expert", TENSOR_KV, None),
        ),
        out_specs=P("expert", TENSOR_KV),
        check_vma=False,
    )
```

```python
import jax
import jax.numpy as jnp
from jax import lax
from jax.experimental import pallas as pl
from jax.experimental.pallas import tpu as pltpu
from jax.sharding import Mesh
from jax.sharding import PartitionSpec as P

D = 4096
CAP = 160
EPS = 1e-05
GROUPS = 4
NY = 4
NZ = 8
LANES = 128
ROWS = GROUPS * CAP
HALF = ROWS // 2
GAIN_ROWS = 16
MINE = CAP // 2
XROWS = HALF + GAIN_ROWS
SPLIT = 144
PADDED = 384
ZFIRST = 128
YFIRST = HALF - ZFIRST
EXTRA = 16
TENSOR_KV = ("tensor_0", "tensor_1", "kv")
LINE = ("expert", "kv")
F32 = jnp.float32
BF16 = jnp.bfloat16
NT = (((1,), (1,)), ((), ()))
TN = (((0,), (0,)), ((), ()))


def call(kernel, outs, us, scratch=(), limit=16):
    here = pl.BlockSpec(memory_space=pltpu.VMEM)

    def called(*arrays):
        return run(arrays)(*arrays)

    run = lambda arrays: pl.pallas_call(
        kernel,
        in_specs=[here] * len(arrays),
        out_specs=[here] * len(outs),
        out_shape=[jax.ShapeDtypeStruct(s, t) for s, t in outs],
        scratch_shapes=list(scratch),
        compiler_params=pltpu.CompilerParams(vmem_limit_bytes=limit * 1024 * 1024),
        cost_estimate=pl.CostEstimate(flops=us * 1_000_000_000, bytes_accessed=0, transcendentals=0),
    )
    return called


def slots_of(ids):
    tokens = ids.shape[1]
    first, second = ids[0:1], ids[1:2]
    groups = lax.broadcasted_iota(jnp.int32, (8, tokens), 0)
    named = jnp.where(first == groups, 1.0, 0.0) + jnp.where(second == groups, 1.0, 0.0)
    earlier = jnp.where(
        lax.broadcasted_iota(jnp.int32, (tokens, tokens), 0)
        < lax.broadcasted_iota(jnp.int32, (tokens, tokens), 1),
        1.0,
        0.0,
    ).astype(BF16)
    before = jnp.dot(named.astype(BF16), earlier, preferred_element_type=F32).astype(jnp.int32)
    at_first = jnp.sum(jnp.where(first == groups, before, 0), axis=0, keepdims=True)
    at_second = jnp.sum(jnp.where(second == groups, before, 0), axis=0, keepdims=True)
    return first * CAP + at_first, second * CAP + at_second


def dispatch_kernel(ids_ref, probs_ref, x_ref, grad_ref, gain_ref, out_ref):
    one, two = slots_of(ids_ref[...])
    tokens = ids_ref.shape[1]
    rows = lax.broadcasted_iota(jnp.int32, (ROWS, tokens), 0)
    x = x_ref[...]
    grad = grad_ref[...].astype(F32)
    probs = probs_ref[...]
    terms = []
    for slot, k in ((one, 0), (two, 1)):
        table = jnp.where(rows == slot, 1.0, 0.0).astype(BF16)
        values = jnp.concatenate([(grad * probs[k : k + 1]).astype(BF16), x], axis=0)
        terms.append(lax.dot_general(table, values, NT, preferred_element_type=F32))
    routed = terms[0] + terms[1]
    low = lax.broadcasted_iota(jnp.int32, (MINE, LANES), 1) < LANES // 2
    gain = gain_ref[...].astype(F32)
    gain = jnp.broadcast_to(jnp.concatenate([gain, gain], axis=1), (MINE, LANES))
    for e in range(GROUPS):
        first = routed[e * CAP : e * CAP + MINE]
        second = routed[e * CAP + MINE : (e + 1) * CAP]
        for k in range(2):
            top = first if k == 0 else jnp.where(low, first, second)
            out_ref[e, k, pl.ds(0, MINE), :] = top.astype(BF16)
            out_ref[e, k, pl.ds(MINE, MINE), :] = jnp.where(low, second, gain).astype(BF16)


def assemble_kernel(got_ref, copies_ref, b_ref):
    a_ref = copies_ref.at[0]
    grads = []
    for g in range(GROUPS):
        low, high = got_ref[g, 0].astype(F32), got_ref[g, 1].astype(F32)
        x = jnp.concatenate([low[:, 64:], high[:, 64:]], axis=1).astype(BF16)
        grads.append(jnp.concatenate([low[:, :64], high[:, :64]], axis=1).astype(BF16))
        a_ref[pl.ds(g * MINE, MINE), :] = x[:MINE]
        if g == 0:
            a_ref[pl.ds(HALF, GAIN_ROWS), :] = x[MINE : MINE + GAIN_ROWS]
    a_ref[pl.ds(XROWS, SPLIT), :] = grads[0][:SPLIT]
    b_ref[pl.ds(0, CAP - SPLIT), :] = grads[0][SPLIT:]
    for g in range(1, GROUPS):
        b_ref[pl.ds(g * CAP - SPLIT, CAP), :] = grads[g]
    for z in range(1, NZ):
        copies_ref[z] = copies_ref[0]


def block(y, z):
    return pl.ds(pl.multiple_of((y * NZ + z) * LANES, LANES), LANES)


def column(a, b):
    y = lax.rem(lax.axis_index("tensor_0") + a, NY)
    z = lax.rem(lax.axis_index("tensor_1") + b, NZ)
    return block(y, z)


def row_of(a, z):
    return block(lax.rem(lax.axis_index("tensor_0") + a, NY), z)


def a_piece(refs, a, b):
    if a == 0:
        return refs[0], b
    return refs[(None, 1, 5, 3)[a] + b // 4], b % 4


def b_piece(refs, a, b):
    if b == NZ // 2:
        return refs[NZ - 1 + a // 2], a % 2
    return refs[b if b < NZ // 2 else b - 1], a


PLACES = [(a, b) for a in range(NY) for b in range(NZ)]


def act_kernel(*refs):
    a_refs, b_refs = refs[:7], refs[7:16]
    wd_ref, mine_ref, theirs_ref, grad_ref, act_ref = refs[16:]
    for a, b in PLACES:
        ref, at = a_piece(a_refs, a, b)
        grad_ref[pl.ds(0, SPLIT), row_of(a, b)] = ref[at, pl.ds(XROWS, SPLIT), :]
        ref, at = b_piece(b_refs, a, b)
        grad_ref[pl.ds(SPLIT, ROWS - SPLIT), column(a, b)] = ref[at]

    @pl.loop(0, 2)
    def _(r):
        rows = pl.ds(pl.multiple_of(r * HALF, HALF), HALF)
        act_ref[rows, :] = lax.dot_general(grad_ref[rows, :], wd_ref[...], NT, preferred_element_type=F32)

    kv = lax.axis_index("kv")
    for g in range(GROUPS):
        here = pl.ds(g * MINE, MINE)
        mine_ref[here, :] = act_ref[pl.ds(pl.multiple_of(g * CAP + kv * MINE, 16), MINE), :]
        theirs_ref[here, :] = act_ref[pl.ds(pl.multiple_of(g * CAP + (1 - kv) * MINE, 16), MINE), :].astype(BF16)


def to_row(column_ref, row_ref):
    for r in range(PADDED // LANES):
        rows = pl.ds(r * LANES, LANES)
        row_ref[:, rows] = jnp.transpose(column_ref[rows, :])[0:1]


def forward_kernel(*refs):
    a_refs = refs[:7]
    wg_ref, wu_ref, wgp_ref, wup_ref, gate_ref, up_ref, gatep_ref, upp_ref, inv_ref, xn_ref, column_ref = refs[7:]

    @pl.loop(0, HALF // 64)
    def _(r):
        rows = pl.ds(pl.multiple_of(r * 64, 64), 64)
        total = jnp.zeros((64, LANES), F32)
        for a, b in PLACES:
            ref, at = a_piece(a_refs, a, b)
            v = ref[at, rows, :].astype(F32)
            total = total + v * v
        inv = lax.rsqrt(jnp.sum(total, axis=1, keepdims=True) / D + EPS)
        column_ref[rows, :] = jnp.broadcast_to(inv, (64, LANES))
        for a, b in PLACES:
            ref, at = a_piece(a_refs, a, b)
            gain = ref[at, pl.ds(HALF, GAIN_ROWS), :].astype(F32)[0:1]
            xn_ref[rows, row_of(a, b)] = (ref[at, rows, :].astype(F32) * inv * gain).astype(BF16)

    column_ref[pl.ds(HALF, PADDED - HALF), :] = jnp.zeros((PADDED - HALF, LANES), F32)
    to_row(column_ref, inv_ref)
    x = xn_ref[...]
    for w_ref, out_ref in ((wg_ref, gate_ref), (wu_ref, up_ref), (wgp_ref, gatep_ref), (wup_ref, upp_ref)):
        out_ref[...] = lax.dot_general(x, w_ref[...], NT, preferred_element_type=F32)


def split3(value):
    terms = []
    for _ in range(3):
        terms.append(value.astype(BF16))
        value = value - terms[-1].astype(F32)
    return terms


def carried(rows):
    terms = [t.astype(F32) for t in split3(rows)]
    return jnp.concatenate(terms + [jnp.zeros((7, LANES), F32)], axis=0).astype(BF16)


def gathered_up(carried_sum):
    return carried_sum[0:3] + carried_sum[3:6] + carried_sum[6:9]


def back_kernel(*refs):
    gate_ref, up_ref, gatep_ref, upp_ref, act_ref, actp_ref, *ws = refs[:10]
    top_ref, *outs, gg_ref, ug_ref, ggp_ref, ugp_ref, column_ref = refs[10:]
    sums = 0.0
    for gate_in, up_in, act_in, gg_out, ug_out in (
        (gate_ref, up_ref, act_ref, gg_ref, ug_ref),
        (gatep_ref, upp_ref, actp_ref, ggp_ref, ugp_ref),
    ):
        gate, up, act = gate_in[...], up_in[...], act_in[...].astype(F32)
        sigma = jax.nn.sigmoid(gate)
        gg = (act * up * sigma * (1.0 + gate * (1.0 - sigma))).astype(BF16)
        ug = (act * (gate * sigma)).astype(BF16)
        gg_out[...] = gg
        ug_out[...] = ug
        sums = sums + jnp.sum(gg.astype(F32) * gate + ug.astype(F32) * up, axis=1, keepdims=True)
    column_ref[pl.ds(0, HALF), :] = jnp.broadcast_to(sums, (HALF, LANES))
    column_ref[pl.ds(HALF, PADDED - HALF), :] = jnp.zeros((PADDED - HALF, LANES), F32)
    rows = [jnp.transpose(column_ref[pl.ds(r * LANES, LANES), :])[0:1] for r in range(PADDED // LANES)]
    projection = carried(jnp.concatenate(rows, axis=0))
    gs = (gg_ref, ug_ref, ggp_ref, ugp_ref)
    for a in range(NY):
        y = lax.rem(lax.axis_index("tensor_0") + a, NY)
        for z in range(0, NZ, 2):
            at = pl.ds(pl.multiple_of((y * NZ + z) * LANES, 2 * LANES), 2 * LANES)
            total = 0.0
            for g_ref, w_ref in zip(gs, ws):
                total = total + jnp.dot(g_ref[...], w_ref[:, at], preferred_element_type=F32)
            total = total.astype(BF16)
            for k in range(2):
                part = total[:, k * LANES : (k + 1) * LANES]
                top_ref[z + k, a] = part[:ZFIRST]
                outs[a][z + k, pl.ds(0, YFIRST), :] = part[ZFIRST:]
                outs[a][z + k, pl.ds(YFIRST, EXTRA), :] = projection


def sum_top_kernel(got_ref, *outs):
    for a in range(NY):
        total = got_ref[0, a].astype(F32)
        for z in range(1, NZ):
            total = total + got_ref[z, a].astype(F32)
        outs[a][...] = total.astype(BF16)


def sum_low_kernel(*refs):
    *shares, out_ref = refs
    for z in range(NZ):
        total = 0.0
        for ref in shares:
            total = total + ref[z].astype(F32)
        out_ref[z, pl.ds(0, YFIRST), :] = total[:YFIRST].astype(BF16)
        out_ref[z, pl.ds(YFIRST, EXTRA), :] = carried(gathered_up(total[YFIRST:]))


def finish_kernel(*refs):
    *tops, low_ref, inv_ref, out_ref = refs
    top, low = 0.0, low_ref[0].astype(F32)
    for ref in tops:
        top = top + ref[...].astype(F32)
    for z in range(1, NZ):
        low = low + low_ref[z].astype(F32)
    slot_grad = jnp.concatenate([top, low[:YFIRST]], axis=0).astype(BF16)
    rows = gathered_up(low[YFIRST:])
    projection = jnp.concatenate([rows[r : r + 1] for r in range(PADDED // LANES)], axis=1)
    inv = inv_ref[...]
    terms = split3(inv * inv * projection / D) + split3(inv)
    terms = jnp.concatenate([t.astype(F32) for t in terms] + [jnp.zeros((10, PADDED), F32)], axis=0)
    for b in range(GROUPS):
        here = slot_grad[b * MINE : (b + 1) * MINE]
        scalars = terms[:, b * MINE : b * MINE + LANES].astype(BF16)
        for k in range(2):
            out_ref[2 * b + k, pl.ds(0, MINE), :] = here
            out_ref[2 * b + k, pl.ds(MINE, EXTRA), :] = scalars


def combine_kernel(got_ref, ids_ref, x_ref, gain_ref, out_ref):
    one, two = slots_of(ids_ref[...])
    tokens = ids_ref.shape[1]
    rows = lax.broadcasted_iota(jnp.int32, (ROWS, tokens), 0)
    table = jnp.where((rows == one) | (rows == two), 1.0, 0.0).astype(BF16)
    slot_grad = jnp.concatenate([got_ref[i, pl.ds(0, MINE), :] for i in range(2 * GROUPS)], axis=0)
    both = lax.dot_general(slot_grad, table, TN, preferred_element_type=F32)
    token_grad = jnp.where(lax.axis_index("kv") == 0, both[:64], both[64:])
    scalars = jnp.concatenate(
        [got_ref[i, pl.ds(MINE, EXTRA), :].astype(F32)[:, :MINE] for i in range(2 * GROUPS)], axis=1
    )
    found = jnp.dot(scalars.astype(BF16), table, preferred_element_type=F32)
    coefficient = found[0:1] + found[1:2] + found[2:3]
    inverse_rms = 0.5 * (found[3:4] + found[4:5] + found[5:6])
    gain = jnp.broadcast_to(gain_ref[...].astype(F32), (LANES, gain_ref.shape[1]))
    gain = jnp.transpose(gain)[:, 0:1]
    x = x_ref[...].astype(F32)
    out_ref[...] = (inverse_rms * (token_grad * gain) - x * coefficient).astype(BF16)


def shift(value, axis, by):
    n = lax.axis_size(axis)
    return lax.ppermute(value, axis, [(i, (i + by) % n) for i in range(n)])


def gather_ring(value, axis, cut, meet=lambda step, right, left: (right, left)):
    n = lax.axis_size(axis)
    got = {0: value}
    right = left = value
    for step in range(1, n // 2):
        right, left = meet(step, right, left)
        right, left = shift(right, axis, 1), shift(left, axis, -1)
        got[n - step], got[step] = right, left
    right, left = meet(n // 2, right, left)
    return got, (shift(right[:cut], axis, 1), shift(left[cut:], axis, -1))


def shards(residual_stream, grad_output, norm_gain, expert_ids, gate_probs, w_gate, w_up, w_down):
    wg, wu, wd = w_gate[0], w_up[0], w_down[0]
    ids, probs = expert_ids.T, gate_probs.T
    x_t, grad_t = residual_stream.T, grad_output.T
    gain_row = norm_gain[None]
    hidden = wg.shape[0]

    with jax.named_scope("dispatch"):
        [routed] = call(dispatch_kernel, [((GROUPS, 2, CAP, LANES), BF16)], 2)(
            ids, probs, x_t, grad_t, gain_row
        )
        got = lax.all_to_all(routed.reshape(2 * GROUPS, CAP, LANES), LINE, 0, 0, tiled=True)
        got, own_wg = lax.optimization_barrier((got, wg))
        copies, piece_b = call(
            assemble_kernel, [((NZ, XROWS + SPLIT, LANES), BF16), ((ROWS - SPLIT, LANES), BF16)], 2
        )(got.reshape(GROUPS, 2, CAP, LANES))

    with jax.named_scope("weights"):
        wgp = shift(own_wg, "kv", 1)
    with jax.named_scope("gather"):
        line_a = lax.all_to_all(copies, "tensor_1", 0, 0, tiled=True)
        line_b = jnp.stack([piece_b] + [shift(piece_b, "tensor_0", -a) for a in (1, 2, 3)])

        near, far = [], []

        def meet(step, right, left):
            nonlocal line_a, wgp
            if step == 2:
                right, left, line_a, wgp = lax.optimization_barrier((right, left, line_a, wgp))
                near[:] = [shift(line_a[: NZ // 2], "tensor_0", by) for by in (1, -1)]
                far[:] = [shift(line_a[NZ // 2 :], "tensor_0", by) for by in (1, -1)]
            if step == 3:
                right, left, *near[:] = lax.optimization_barrier((right, left, *near))
            if step == 4:
                right, left, *far[:] = lax.optimization_barrier((right, left, *far))
            return right, left

        b_got, b_far = gather_ring(line_b, "tensor_1", NY // 2, meet)
        b_refs = (*[b_got[b] for b in range(NZ) if b != 4], *b_far)
        a_far = (shift(near[0], "tensor_0", 1), shift(far[1], "tensor_0", -1))
        a_refs = (line_a, near[1], far[1], near[0], far[0], *a_far)
    with jax.named_scope("weights"):
        wgp, own_wu = lax.optimization_barrier((wgp, wu))
        wup = shift(own_wu, "kv", 1)

    with jax.named_scope("act"):
        act, theirs = call(
            act_kernel,
            [((HALF, hidden), F32), ((HALF, hidden), BF16)],
            7,
            [pltpu.VMEM((ROWS, D), BF16), pltpu.VMEM((ROWS, hidden), F32)],
        )(*a_refs, *b_refs, wd)
        actp = shift(theirs, "kv", 1)
    with jax.named_scope("forward"):
        gate, up, gatep, upp, inv = call(
            forward_kernel,
            [((HALF, hidden), F32)] * 4 + [((1, PADDED), F32)],
            8,
            [pltpu.VMEM((HALF, D), BF16), pltpu.VMEM((PADDED, LANES), F32)],
        )(*a_refs, wg, wu, wgp, wup)
    with jax.named_scope("back"):
        top, *low = call(
            back_kernel,
            [((NZ, NY, ZFIRST, LANES), BF16)] + [((NZ, YFIRST + EXTRA, LANES), BF16)] * NY,
            8,
            [pltpu.VMEM((HALF, hidden), BF16)] * 4 + [pltpu.VMEM((PADDED, LANES), F32)],
        )(gate, up, gatep, upp, act, actp, wg, wu, wgp, wup)
    with jax.named_scope("scatter"):
        top = lax.all_to_all(top, "tensor_1", 0, 0, tiled=True)
        low = [low[0]] + [shift(low[a], "tensor_0", a) for a in (2, 1, 3)]
        [low] = call(sum_low_kernel, [((NZ, YFIRST + EXTRA, LANES), BF16)], 3)(*low)
        top, low = lax.optimization_barrier((top, low))
        top = call(sum_top_kernel, [((ZFIRST, LANES), BF16)] * NY, 3)(top)
        low = lax.all_to_all(low, "tensor_1", 0, 0, tiled=True)
        top = [top[0]] + [shift(top[a], "tensor_0", a) for a in (2, 1, 3)]

    with jax.named_scope("combine"):
        [pieces] = call(finish_kernel, [((2 * GROUPS, MINE + EXTRA, LANES), BF16)], 2)(*top, low, inv)
        got = lax.all_to_all(pieces, LINE, 0, 0, tiled=True)
        [out] = call(combine_kernel, [(x_t.shape, BF16)], 2)(
            got, ids, x_t, gain_row
        )
    return out.T


def solution(mesh):
    torus = Mesh(
        mesh.devices.reshape(mesh.shape["expert"], NY, NZ, mesh.shape["kv"]),
        ("expert", "tensor_0", "tensor_1", "kv"),
    )
    return jax.shard_map(
        shards,
        mesh=torus,
        in_specs=(
            P("expert", TENSOR_KV),
            P("expert", TENSOR_KV),
            P(TENSOR_KV),
            P("expert", None),
            P("expert", None),
            P("expert", TENSOR_KV, None),
            P("expert", TENSOR_KV, None),
            P("expert", TENSOR_KV, None),
        ),
        out_specs=P("expert", TENSOR_KV),
        check_vma=False,
    )
```

```python
import jax
import jax.numpy as jnp
from jax import lax
from jax.experimental import pallas as pl
from jax.experimental.pallas import tpu as pltpu
from jax.sharding import Mesh
from jax.sharding import PartitionSpec as P

D = 4096
CAP = 160
EPS = 1e-05
GROUPS = 4
NY = 4
NZ = 8
LANES = 128
ROWS = GROUPS * CAP
HALF = ROWS // 2
GAIN_ROWS = 16
MINE = CAP // 2
XROWS = HALF + GAIN_ROWS
SPLIT = 144
PADDED = 384
ZFIRST = 112
YFIRST = HALF - ZFIRST
EXTRA = 16
TENSOR_KV = ("tensor_0", "tensor_1", "kv")
LINE = ("expert", "kv")
F32 = jnp.float32
BF16 = jnp.bfloat16
NT = (((1,), (1,)), ((), ()))
TN = (((0,), (0,)), ((), ()))


def call(kernel, outs, us, scratch=(), limit=6, aliases=None):
    here = pl.BlockSpec(memory_space=pltpu.VMEM) if limit < 32 else pl.BlockSpec()

    def run(*arrays):
        return pl.pallas_call(
            kernel,
            in_specs=[here] * len(arrays),
            out_specs=[here] * len(outs),
            out_shape=[jax.ShapeDtypeStruct(s, t) for s, t in outs],
            scratch_shapes=list(scratch),
            input_output_aliases=aliases or {},
            compiler_params=pltpu.CompilerParams(vmem_limit_bytes=limit * 1024 * 1024),
            cost_estimate=pl.CostEstimate(flops=us * 1_000_000_000, bytes_accessed=0, transcendentals=0),
        )(*arrays)

    return run


def slots_of(ids):
    tokens = ids.shape[1]
    first, second = ids[0:1], ids[1:2]
    groups = lax.broadcasted_iota(jnp.int32, (8, tokens), 0)
    named = jnp.where(first == groups, 1.0, 0.0) + jnp.where(second == groups, 1.0, 0.0)
    earlier = jnp.where(
        lax.broadcasted_iota(jnp.int32, (tokens, tokens), 0)
        < lax.broadcasted_iota(jnp.int32, (tokens, tokens), 1),
        1.0,
        0.0,
    ).astype(BF16)
    before = jnp.dot(named.astype(BF16), earlier, preferred_element_type=F32).astype(jnp.int32)
    at_first = jnp.sum(jnp.where(first == groups, before, 0), axis=0, keepdims=True)
    at_second = jnp.sum(jnp.where(second == groups, before, 0), axis=0, keepdims=True)
    return first * CAP + at_first, second * CAP + at_second


def dispatch_kernel(ids_ref, probs_ref, x_ref, grad_ref, gain_ref, out_ref):
    one, two = slots_of(ids_ref[...])
    tokens = ids_ref.shape[1]
    rows = lax.broadcasted_iota(jnp.int32, (ROWS, tokens), 0)
    x = x_ref[...]
    grad = grad_ref[...].astype(F32)
    probs = probs_ref[...]
    terms = []
    for slot, k in ((one, 0), (two, 1)):
        table = jnp.where(rows == slot, 1.0, 0.0).astype(BF16)
        values = jnp.concatenate([(grad * probs[k : k + 1]).astype(BF16), x], axis=0)
        terms.append(lax.dot_general(table, values, NT, preferred_element_type=F32))
    routed = terms[0] + terms[1]
    low = lax.broadcasted_iota(jnp.int32, (MINE, LANES), 1) < LANES // 2
    gain = gain_ref[...].astype(F32)
    gain = jnp.broadcast_to(jnp.concatenate([gain, gain], axis=1), (MINE, LANES))
    for e in range(GROUPS):
        first = routed[e * CAP : e * CAP + MINE]
        second = routed[e * CAP + MINE : (e + 1) * CAP]
        for k in range(2):
            top = first if k == 0 else jnp.where(low, first, second)
            out_ref[e, k, pl.ds(0, MINE), :] = top.astype(BF16)
            out_ref[e, k, pl.ds(MINE, MINE), :] = jnp.where(low, second, gain).astype(BF16)


def assemble_kernel(got_ref, copies_ref, b_ref):
    a_ref = copies_ref.at[0]
    grads = []
    for g in range(GROUPS):
        low, high = got_ref[g, 0].astype(F32), got_ref[g, 1].astype(F32)
        x = jnp.concatenate([low[:, 64:], high[:, 64:]], axis=1).astype(BF16)
        grads.append(jnp.concatenate([low[:, :64], high[:, :64]], axis=1).astype(BF16))
        a_ref[pl.ds(g * MINE, MINE), :] = x[:MINE]
        if g == 0:
            a_ref[pl.ds(HALF, GAIN_ROWS), :] = x[MINE : MINE + GAIN_ROWS]
    a_ref[pl.ds(XROWS, SPLIT), :] = grads[0][:SPLIT]
    b_ref[pl.ds(0, CAP - SPLIT), :] = grads[0][SPLIT:]
    for g in range(1, GROUPS):
        b_ref[pl.ds(g * CAP - SPLIT, CAP), :] = grads[g]
    for z in range(1, NZ):
        copies_ref[z] = copies_ref[0]


def block(y, z):
    return pl.ds(pl.multiple_of((y * NZ + z) * LANES, LANES), LANES)


def column(a, b):
    y = lax.rem(lax.axis_index("tensor_0") + a, NY)
    z = lax.rem(lax.axis_index("tensor_1") + b, NZ)
    return block(y, z)


def row_of(a, z):
    return block(lax.rem(lax.axis_index("tensor_0") + a, NY), z)


def place_x(pieces, xs_ref, sq_ref, begins):
    @pl.loop(0, HALF // 64)
    def _(r):
        rows = pl.ds(pl.multiple_of(r * 64, 64), 64)
        total = jnp.zeros((64, LANES), F32) if begins else sq_ref[rows, :]
        for ref, at, a, z in pieces:
            v = ref[at, rows, :].astype(F32)
            total = total + v * v
            gain = ref[at, pl.ds(HALF, GAIN_ROWS), :].astype(F32)[0:1]
            xs_ref[rows, row_of(a, z)] = (v * gain).astype(BF16)
        sq_ref[rows, :] = total


def place_grad(a_pieces, b_pieces, ds_ref):
    for ref, at, a, z in a_pieces:
        ds_ref[pl.ds(0, SPLIT), row_of(a, z)] = ref[at, pl.ds(XROWS, SPLIT), :]
    for ref, at, a, b in b_pieces:
        ds_ref[pl.ds(SPLIT, ROWS - SPLIT), column(a, b)] = ref[at]


def place_first_kernel(line_ref, near1_ref, near3_ref, b0, b1, b2, b6, b7, xs_ref, ds_ref, sq_ref):
    a_pieces = [(line_ref, z, 0, z) for z in range(NZ)]
    a_pieces += [(ref, z, a, z) for a, ref in ((1, near1_ref), (3, near3_ref)) for z in range(NZ // 2)]
    b_pieces = [(ref, a, a, b) for b, ref in ((0, b0), (1, b1), (2, b2), (6, b6), (7, b7)) for a in range(NY)]
    place_grad(a_pieces, b_pieces, ds_ref)
    place_x(a_pieces, xs_ref, sq_ref, True)


def place_second_kernel(_xs, _ds, _sq, far1_ref, far3_ref, b3, b5, xs_ref, ds_ref, sq_ref):
    a_pieces = [(ref, z, a, NZ // 2 + z) for a, ref in ((1, far1_ref), (3, far3_ref)) for z in range(NZ // 2)]
    b_pieces = [(ref, a, a, b) for b, ref in ((3, b3), (5, b5)) for a in range(NY)]
    place_grad(a_pieces, b_pieces, ds_ref)
    place_x(a_pieces, xs_ref, sq_ref, False)


def act_kernel(_ds, lo_ref, hi_ref, b4lo_ref, b4hi_ref, wd_ref, ds_ref, mine_ref, theirs_ref, act_ref):
    a_pieces = [((lo_ref, hi_ref)[z // 4], z % 4, 2, z) for z in range(NZ)]
    b_pieces = [((b4lo_ref, b4hi_ref)[a // 2], a % 2, a, NZ // 2) for a in range(NY)]
    place_grad(a_pieces, b_pieces, ds_ref)

    @pl.loop(0, 2)
    def _(r):
        rows = pl.ds(pl.multiple_of(r * HALF, HALF), HALF)
        act_ref[rows, :] = lax.dot_general(ds_ref[rows, :], wd_ref[...], NT, preferred_element_type=F32)

    kv = lax.axis_index("kv")
    for g in range(GROUPS):
        here = pl.ds(g * MINE, MINE)
        mine_ref[here, :] = act_ref[pl.ds(pl.multiple_of(g * CAP + kv * MINE, 16), MINE), :]
        theirs_ref[here, :] = act_ref[pl.ds(pl.multiple_of(g * CAP + (1 - kv) * MINE, 16), MINE), :].astype(BF16)


def to_row(column_ref, row_ref):
    for r in range(PADDED // LANES):
        rows = pl.ds(r * LANES, LANES)
        row_ref[:, rows] = jnp.transpose(column_ref[rows, :])[0:1]


def forward_kernel(*refs):
    _xs, _sq, lo_ref, hi_ref, wg_ref, wu_ref, wgp_ref, wup_ref = refs[:8]
    xs_ref, sq_ref, gate_ref, up_ref, gatep_ref, upp_ref, inv_ref, column_ref = refs[8:]
    place_x([((lo_ref, hi_ref)[z // 4], z % 4, 2, z) for z in range(NZ)], xs_ref, sq_ref, False)
    inv = lax.rsqrt(jnp.sum(sq_ref[...], axis=1, keepdims=True) / D + EPS)
    column_ref[pl.ds(0, HALF), :] = jnp.broadcast_to(inv, (HALF, LANES))
    column_ref[pl.ds(HALF, PADDED - HALF), :] = jnp.zeros((PADDED - HALF, LANES), F32)
    to_row(column_ref, inv_ref)
    x = xs_ref[...]
    for w_ref, out_ref in ((wg_ref, gate_ref), (wu_ref, up_ref), (wgp_ref, gatep_ref), (wup_ref, upp_ref)):
        out_ref[...] = inv * lax.dot_general(x, w_ref[...], NT, preferred_element_type=F32)


def split3(value):
    terms = []
    for _ in range(3):
        terms.append(value.astype(BF16))
        value = value - terms[-1].astype(F32)
    return terms


def carried(rows):
    terms = [t.astype(F32) for t in split3(rows)]
    return jnp.concatenate(terms + [jnp.zeros((7, LANES), F32)], axis=0).astype(BF16)


def gathered_up(carried_sum):
    return carried_sum[0:3] + carried_sum[3:6] + carried_sum[6:9]


def back_kernel(*refs):
    gate_ref, up_ref, gatep_ref, upp_ref, act_ref, actp_ref, *ws = refs[:10]
    top_ref, *outs, gg_ref, ug_ref, ggp_ref, ugp_ref, column_ref = refs[10:]
    sums = 0.0
    for gate_in, up_in, act_in, gg_out, ug_out in (
        (gate_ref, up_ref, act_ref, gg_ref, ug_ref),
        (gatep_ref, upp_ref, actp_ref, ggp_ref, ugp_ref),
    ):
        gate, up, act = gate_in[...], up_in[...], act_in[...].astype(F32)
        sigma = jax.nn.sigmoid(gate)
        gg = (act * up * sigma * (1.0 + gate * (1.0 - sigma))).astype(BF16)
        ug = (act * (gate * sigma)).astype(BF16)
        gg_out[...] = gg
        ug_out[...] = ug
        sums = sums + jnp.sum(gg.astype(F32) * gate + ug.astype(F32) * up, axis=1, keepdims=True)
    column_ref[pl.ds(0, HALF), :] = jnp.broadcast_to(sums, (HALF, LANES))
    column_ref[pl.ds(HALF, PADDED - HALF), :] = jnp.zeros((PADDED - HALF, LANES), F32)
    rows = [jnp.transpose(column_ref[pl.ds(r * LANES, LANES), :])[0:1] for r in range(PADDED // LANES)]
    projection = carried(jnp.concatenate(rows, axis=0))
    gs = (gg_ref, ug_ref, ggp_ref, ugp_ref)
    for a in range(NY):
        y = lax.rem(lax.axis_index("tensor_0") + a, NY)
        for z in range(0, NZ, 2):
            at = pl.ds(pl.multiple_of((y * NZ + z) * LANES, 2 * LANES), 2 * LANES)
            total = 0.0
            for g_ref, w_ref in zip(gs, ws):
                total = total + jnp.dot(g_ref[...], w_ref[:, at], preferred_element_type=F32)
            total = total.astype(BF16)
            for k in range(2):
                part = total[:, k * LANES : (k + 1) * LANES]
                top_ref[z + k, a] = part[:ZFIRST]
                outs[a][z + k, pl.ds(0, YFIRST), :] = part[ZFIRST:]
                outs[a][z + k, pl.ds(YFIRST, EXTRA), :] = projection


def sum_top_kernel(got_ref, *outs):
    for a in range(NY):
        total = got_ref[0, a].astype(F32)
        for z in range(1, NZ):
            total = total + got_ref[z, a].astype(F32)
        outs[a][...] = total.astype(BF16)


def sum_low_kernel(*refs):
    *shares, out_ref = refs
    for z in range(NZ):
        total = 0.0
        for ref in shares:
            total = total + ref[z].astype(F32)
        out_ref[z, pl.ds(0, YFIRST), :] = total[:YFIRST].astype(BF16)
        out_ref[z, pl.ds(YFIRST, EXTRA), :] = carried(gathered_up(total[YFIRST:]))


def finish_kernel(*refs):
    *tops, low_ref, inv_ref, out_ref = refs
    top, low = 0.0, low_ref[0].astype(F32)
    for ref in tops:
        top = top + ref[...].astype(F32)
    for z in range(1, NZ):
        low = low + low_ref[z].astype(F32)
    slot_grad = jnp.concatenate([top, low[:YFIRST]], axis=0).astype(BF16)
    rows = gathered_up(low[YFIRST:])
    projection = jnp.concatenate([rows[r : r + 1] for r in range(PADDED // LANES)], axis=1)
    inv = inv_ref[...]
    terms = split3(inv * inv * projection / D) + split3(inv)
    terms = jnp.concatenate([t.astype(F32) for t in terms] + [jnp.zeros((10, PADDED), F32)], axis=0)
    for b in range(GROUPS):
        here = slot_grad[b * MINE : (b + 1) * MINE]
        scalars = terms[:, b * MINE : b * MINE + LANES].astype(BF16)
        for k in range(2):
            out_ref[2 * b + k, pl.ds(0, MINE), :] = here
            out_ref[2 * b + k, pl.ds(MINE, EXTRA), :] = scalars


def combine_kernel(got_ref, ids_ref, x_ref, gain_ref, out_ref):
    one, two = slots_of(ids_ref[...])
    tokens = ids_ref.shape[1]
    rows = lax.broadcasted_iota(jnp.int32, (ROWS, tokens), 0)
    table = jnp.where((rows == one) | (rows == two), 1.0, 0.0).astype(BF16)
    slot_grad = jnp.concatenate([got_ref[i, pl.ds(0, MINE), :] for i in range(2 * GROUPS)], axis=0)
    both = lax.dot_general(slot_grad, table, TN, preferred_element_type=F32)
    token_grad = jnp.where(lax.axis_index("kv") == 0, both[:64], both[64:])
    scalars = jnp.concatenate(
        [got_ref[i, pl.ds(MINE, EXTRA), :].astype(F32)[:, :MINE] for i in range(2 * GROUPS)], axis=1
    )
    found = jnp.dot(scalars.astype(BF16), table, preferred_element_type=F32)
    coefficient = found[0:1] + found[1:2] + found[2:3]
    inverse_rms = 0.5 * (found[3:4] + found[4:5] + found[5:6])
    gain = jnp.broadcast_to(gain_ref[...].astype(F32), (LANES, gain_ref.shape[1]))
    gain = jnp.transpose(gain)[:, 0:1]
    x = x_ref[...].astype(F32)
    out_ref[...] = (inverse_rms * (token_grad * gain) - x * coefficient).astype(BF16)


def shift(value, axis, by):
    n = lax.axis_size(axis)
    return lax.ppermute(value, axis, [(i, (i + by) % n) for i in range(n)])


def gather_ring(value, axis, cut, meet=lambda step, right, left, got: (right, left)):
    n = lax.axis_size(axis)
    got = {0: value}
    right = left = value
    for step in range(1, n // 2):
        right, left = meet(step, right, left, got)
        right, left = shift(right, axis, 1), shift(left, axis, -1)
        got[n - step], got[step] = right, left
    right, left = meet(n // 2, right, left, got)
    return got, (shift(right[:cut], axis, 1), shift(left[cut:], axis, -1))


def shards(residual_stream, grad_output, norm_gain, expert_ids, gate_probs, w_gate, w_up, w_down):
    wg, wu, wd = w_gate[0], w_up[0], w_down[0]
    ids, probs = expert_ids.T, gate_probs.T
    x_t, grad_t = residual_stream.T, grad_output.T
    gain_row = norm_gain[None]
    hidden = wg.shape[0]

    with jax.named_scope("dispatch"):
        [routed] = call(dispatch_kernel, [((GROUPS, 2, CAP, LANES), BF16)], 2, limit=60)(
            ids, probs, x_t, grad_t, gain_row
        )
        got = lax.all_to_all(routed.reshape(2 * GROUPS, CAP, LANES), LINE, 0, 0, tiled=True)
        got, own_wg = lax.optimization_barrier((got, wg))
        copies, piece_b = call(
            assemble_kernel, [((NZ, XROWS + SPLIT, LANES), BF16), ((ROWS - SPLIT, LANES), BF16)], 2
        )(got.reshape(GROUPS, 2, CAP, LANES))

    with jax.named_scope("weights"):
        wgp = shift(own_wg, "kv", 1)
    with jax.named_scope("gather"):
        line_a = lax.all_to_all(copies, "tensor_1", 0, 0, tiled=True)
        line_b = jnp.stack([piece_b] + [shift(piece_b, "tensor_0", -a) for a in (1, 2, 3)])

        near, far, state = [], [], None
        placed = [((HALF, D), BF16), ((ROWS, D), BF16), ((HALF, LANES), F32)]

        def meet(step, right, left, got):
            nonlocal line_a, wgp, state
            if step == 2:
                right, left, line_a, wgp = lax.optimization_barrier((right, left, line_a, wgp))
                near[:] = [shift(line_a[: NZ // 2], "tensor_0", by) for by in (1, -1)]
                far[:] = [shift(line_a[NZ // 2 :], "tensor_0", by) for by in (1, -1)]
            if step == 3:
                right, left, *near[:] = lax.optimization_barrier((right, left, *near))
                early = [got[b] for b in (0, 1, 2, 6, 7)]
                state = [*call(place_first_kernel, placed, 5)(line_a, near[1], near[0], *early)]
            if step == 4:
                right, left, state[2], *far[:] = lax.optimization_barrier((right, left, state[2], *far))
            return right, left

        b_got, b_far = gather_ring(line_b, "tensor_1", NY // 2, meet)
        lo, hi = shift(near[0], "tensor_0", 1), shift(far[1], "tensor_0", -1)
    with jax.named_scope("place"):
        xs, ds, sq = call(place_second_kernel, placed, 3, aliases={0: 0, 1: 1, 2: 2})(
            *state, far[1], far[0], b_got[3], b_got[5]
        )
    with jax.named_scope("weights"):
        wgp, own_wu = lax.optimization_barrier((wgp, wu))
        wup = shift(own_wu, "kv", 1)

    with jax.named_scope("act"):
        _, act, theirs = call(
            act_kernel,
            [placed[1], ((HALF, hidden), F32), ((HALF, hidden), BF16)],
            3,
            [pltpu.VMEM((ROWS, hidden), F32)],
            aliases={0: 0},
        )(ds, lo, hi, *b_far, wd)
        actp = shift(theirs, "kv", 1)
    with jax.named_scope("forward"):
        _, _, gate, up, gatep, upp, inv = call(
            forward_kernel,
            [placed[0], placed[2]] + [((HALF, hidden), F32)] * 4 + [((1, PADDED), F32)],
            5,
            [pltpu.VMEM((PADDED, LANES), F32)],
            aliases={0: 0, 1: 1},
        )(xs, sq, lo, hi, wg, wu, wgp, wup)
    with jax.named_scope("back"):
        top, *low = call(
            back_kernel,
            [((NZ, NY, ZFIRST, LANES), BF16)] + [((NZ, YFIRST + EXTRA, LANES), BF16)] * NY,
            8,
            [pltpu.VMEM((HALF, hidden), BF16)] * 4 + [pltpu.VMEM((PADDED, LANES), F32)],
        )(gate, up, gatep, upp, act, actp, wg, wu, wgp, wup)
    with jax.named_scope("scatter"):
        top = lax.all_to_all(top, "tensor_1", 0, 0, tiled=True)
        low = [low[0]] + [shift(low[a], "tensor_0", a) for a in (2, 1, 3)]
        [low] = call(sum_low_kernel, [((NZ, YFIRST + EXTRA, LANES), BF16)], 3)(*low)
        top, low = lax.optimization_barrier((top, low))
        top = call(sum_top_kernel, [((ZFIRST, LANES), BF16)] * NY, 3)(top)
        low = lax.all_to_all(low, "tensor_1", 0, 0, tiled=True)
        top = [top[0]] + [shift(top[a], "tensor_0", a) for a in (2, 1, 3)]

    with jax.named_scope("combine"):
        [pieces] = call(finish_kernel, [((2 * GROUPS, MINE + EXTRA, LANES), BF16)], 2)(*top, low, inv)
        got = lax.all_to_all(pieces, LINE, 0, 0, tiled=True)
        [out] = call(combine_kernel, [(x_t.shape, BF16)], 2)(
            got, ids, x_t, gain_row
        )
    return out.T


def solution(mesh):
    torus = Mesh(
        mesh.devices.reshape(mesh.shape["expert"], NY, NZ, mesh.shape["kv"]),
        ("expert", "tensor_0", "tensor_1", "kv"),
    )
    return jax.shard_map(
        shards,
        mesh=torus,
        in_specs=(
            P("expert", TENSOR_KV),
            P("expert", TENSOR_KV),
            P(TENSOR_KV),
            P("expert", None),
            P("expert", None),
            P("expert", TENSOR_KV, None),
            P("expert", TENSOR_KV, None),
            P("expert", TENSOR_KV, None),
        ),
        out_specs=P("expert", TENSOR_KV),
        check_vma=False,
    )
```

```python
import jax
import jax.numpy as jnp
from jax import lax
from jax.experimental import pallas as pl
from jax.experimental.pallas import tpu as pltpu
from jax.sharding import Mesh
from jax.sharding import PartitionSpec as P

D = 4096
CAP = 160
EPS = 1e-05
GROUPS = 4
NY = 4
NZ = 8
LANES = 128
ROWS = GROUPS * CAP
HALF = ROWS // 2
GAIN_ROWS = 16
MINE = CAP // 2
XROWS = HALF + GAIN_ROWS
SPLIT = 192
PADDED = 384
ZFIRST = 112
YFIRST = HALF - ZFIRST
EXTRA = 16
TENSOR_KV = ("tensor_0", "tensor_1", "kv")
LINE = ("expert", "kv")
F32 = jnp.float32
BF16 = jnp.bfloat16
NT = (((1,), (1,)), ((), ()))
TN = (((0,), (0,)), ((), ()))


def call(kernel, outs, us, scratch=(), limit=6, aliases=None):
    here = pl.BlockSpec(memory_space=pltpu.VMEM) if limit < 32 else pl.BlockSpec()

    def run(*arrays):
        return pl.pallas_call(
            kernel,
            in_specs=[here] * len(arrays),
            out_specs=[here] * len(outs),
            out_shape=[jax.ShapeDtypeStruct(s, t) for s, t in outs],
            scratch_shapes=list(scratch),
            input_output_aliases=aliases or {},
            compiler_params=pltpu.CompilerParams(vmem_limit_bytes=limit * 1024 * 1024),
            cost_estimate=pl.CostEstimate(flops=us * 1_000_000_000, bytes_accessed=0, transcendentals=0),
        )(*arrays)

    return run


def slots_of(ids):
    tokens = ids.shape[1]
    first, second = ids[0:1], ids[1:2]
    groups = lax.broadcasted_iota(jnp.int32, (8, tokens), 0)
    named = jnp.where(first == groups, 1.0, 0.0) + jnp.where(second == groups, 1.0, 0.0)
    earlier = jnp.where(
        lax.broadcasted_iota(jnp.int32, (tokens, tokens), 0)
        < lax.broadcasted_iota(jnp.int32, (tokens, tokens), 1),
        1.0,
        0.0,
    ).astype(BF16)
    before = jnp.dot(named.astype(BF16), earlier, preferred_element_type=F32).astype(jnp.int32)
    at_first = jnp.sum(jnp.where(first == groups, before, 0), axis=0, keepdims=True)
    at_second = jnp.sum(jnp.where(second == groups, before, 0), axis=0, keepdims=True)
    return first * CAP + at_first, second * CAP + at_second


def dispatch_kernel(ids_ref, probs_ref, x_ref, grad_ref, gain_ref, out_ref):
    one, two = slots_of(ids_ref[...])
    tokens = ids_ref.shape[1]
    rows = lax.broadcasted_iota(jnp.int32, (ROWS, tokens), 0)
    x = x_ref[...]
    grad = grad_ref[...].astype(F32)
    probs = probs_ref[...]
    terms = []
    for slot, k in ((one, 0), (two, 1)):
        table = jnp.where(rows == slot, 1.0, 0.0).astype(BF16)
        values = jnp.concatenate([(grad * probs[k : k + 1]).astype(BF16), x], axis=0)
        terms.append(lax.dot_general(table, values, NT, preferred_element_type=F32))
    routed = terms[0] + terms[1]
    low = lax.broadcasted_iota(jnp.int32, (MINE, LANES), 1) < LANES // 2
    gain = gain_ref[...].astype(F32)
    gain = jnp.broadcast_to(jnp.concatenate([gain, gain], axis=1), (MINE, LANES))
    for e in range(GROUPS):
        first = routed[e * CAP : e * CAP + MINE]
        second = routed[e * CAP + MINE : (e + 1) * CAP]
        for k in range(2):
            top = first if k == 0 else jnp.where(low, first, second)
            out_ref[e, k, pl.ds(0, MINE), :] = top.astype(BF16)
            out_ref[e, k, pl.ds(MINE, MINE), :] = jnp.where(low, second, gain).astype(BF16)


def assemble_kernel(got_ref, a_ref, b_ref):
    grads = []
    for g in range(GROUPS):
        low, high = got_ref[g, 0].astype(F32), got_ref[g, 1].astype(F32)
        x = jnp.concatenate([low[:, 64:], high[:, 64:]], axis=1).astype(BF16)
        grads.append(jnp.concatenate([low[:, :64], high[:, :64]], axis=1).astype(BF16))
        a_ref[pl.ds(g * MINE, MINE), :] = x[:MINE]
        if g == 0:
            a_ref[pl.ds(HALF, GAIN_ROWS), :] = x[MINE : MINE + GAIN_ROWS]
    grads = jnp.concatenate(grads, axis=0)
    a_ref[pl.ds(XROWS, SPLIT), :] = grads[:SPLIT]
    b_ref[...] = grads[SPLIT:]


def block(y, z):
    return pl.ds(pl.multiple_of((y * NZ + z) * LANES, LANES), LANES)


def column(a, b):
    y = lax.rem(lax.axis_index("tensor_0") + a, NY)
    z = lax.rem(lax.axis_index("tensor_1") + b, NZ)
    return block(y, z)


def row_of(a, z):
    return block(lax.rem(lax.axis_index("tensor_0") + a, NY), z)


def place_x(pieces, xs_ref, sq_ref, begins):
    @pl.loop(0, HALF // 64)
    def _(r):
        rows = pl.ds(pl.multiple_of(r * 64, 64), 64)
        total = jnp.zeros((64, LANES), F32) if begins else sq_ref[rows, :]
        for ref, at, a, z in pieces:
            v = ref[at, rows, :].astype(F32)
            total = total + v * v
            gain = ref[at, pl.ds(HALF, GAIN_ROWS), :].astype(F32)[0:1]
            xs_ref[rows, row_of(a, z)] = (v * gain).astype(BF16)
        sq_ref[rows, :] = total


def place_grad(a_pieces, b_pieces, ds_ref):
    for ref, at, a, z in a_pieces:
        ds_ref[pl.ds(0, SPLIT), row_of(a, z)] = ref[at, pl.ds(XROWS, SPLIT), :]
    for ref, at, a, b in b_pieces:
        ds_ref[pl.ds(SPLIT, ROWS - SPLIT), column(a, b)] = ref[at]


def place_first_kernel(line_ref, near1_ref, near3_ref, b0, b1, b2, b6, b7, xs_ref, ds_ref, sq_ref):
    a_pieces = [(line_ref, z, 0, z) for z in range(NZ)]
    a_pieces += [(ref, z, a, z) for a, ref in ((1, near1_ref), (3, near3_ref)) for z in range(NZ // 2)]
    b_pieces = [(ref, a, a, b) for b, ref in ((0, b0), (1, b1), (2, b2), (6, b6), (7, b7)) for a in range(NY)]
    place_grad(a_pieces, b_pieces, ds_ref)
    place_x(a_pieces, xs_ref, sq_ref, True)


def place_second_kernel(_xs, _ds, _sq, far1_ref, far3_ref, b3, b5, xs_ref, ds_ref, sq_ref):
    a_pieces = [(ref, z, a, NZ // 2 + z) for a, ref in ((1, far1_ref), (3, far3_ref)) for z in range(NZ // 2)]
    b_pieces = [(ref, a, a, b) for b, ref in ((3, b3), (5, b5)) for a in range(NY)]
    place_grad(a_pieces, b_pieces, ds_ref)
    place_x(a_pieces, xs_ref, sq_ref, False)


def act_kernel(_ds, lo_ref, hi_ref, b4lo_ref, b4hi_ref, wd_ref, ds_ref, mine_ref, theirs_ref, act_ref):
    a_pieces = [((lo_ref, hi_ref)[z // 4], z % 4, 2, z) for z in range(NZ)]
    b_pieces = [((b4lo_ref, b4hi_ref)[a // 2], a % 2, a, NZ // 2) for a in range(NY)]
    place_grad(a_pieces, b_pieces, ds_ref)

    @pl.loop(0, 2)
    def _(r):
        rows = pl.ds(pl.multiple_of(r * HALF, HALF), HALF)
        act_ref[rows, :] = lax.dot_general(ds_ref[rows, :], wd_ref[...], NT, preferred_element_type=F32)

    kv = lax.axis_index("kv")
    for g in range(GROUPS):
        here = pl.ds(g * MINE, MINE)
        mine_ref[here, :] = act_ref[pl.ds(pl.multiple_of(g * CAP + kv * MINE, 16), MINE), :]
        theirs_ref[here, :] = act_ref[pl.ds(pl.multiple_of(g * CAP + (1 - kv) * MINE, 16), MINE), :].astype(BF16)


def to_row(column_ref, row_ref):
    for r in range(PADDED // LANES):
        rows = pl.ds(r * LANES, LANES)
        row_ref[:, rows] = jnp.transpose(column_ref[rows, :])[0:1]


def forward_kernel(*refs):
    _xs, _sq, lo_ref, hi_ref, wg_ref, wu_ref, wgp_ref, wup_ref = refs[:8]
    xs_ref, sq_ref, gate_ref, up_ref, gatep_ref, upp_ref, inv_ref, column_ref = refs[8:]
    place_x([((lo_ref, hi_ref)[z // 4], z % 4, 2, z) for z in range(NZ)], xs_ref, sq_ref, False)
    inv = lax.rsqrt(jnp.sum(sq_ref[...], axis=1, keepdims=True) / D + EPS)
    column_ref[pl.ds(0, HALF), :] = jnp.broadcast_to(inv, (HALF, LANES))
    column_ref[pl.ds(HALF, PADDED - HALF), :] = jnp.zeros((PADDED - HALF, LANES), F32)
    to_row(column_ref, inv_ref)
    x = xs_ref[...]
    for w_ref, out_ref in ((wg_ref, gate_ref), (wu_ref, up_ref), (wgp_ref, gatep_ref), (wup_ref, upp_ref)):
        out_ref[...] = inv * lax.dot_general(x, w_ref[...], NT, preferred_element_type=F32)


def split3(value):
    terms = []
    for _ in range(3):
        terms.append(value.astype(BF16))
        value = value - terms[-1].astype(F32)
    return terms


def carried(rows):
    terms = [t.astype(F32) for t in split3(rows)]
    return jnp.concatenate(terms + [jnp.zeros((7, LANES), F32)], axis=0).astype(BF16)


def gathered_up(carried_sum):
    return carried_sum[0:3] + carried_sum[3:6] + carried_sum[6:9]


def back_kernel(*refs):
    gate_ref, up_ref, gatep_ref, upp_ref, act_ref, actp_ref, *ws = refs[:10]
    top_ref, *outs, gg_ref, ug_ref, ggp_ref, ugp_ref, column_ref = refs[10:]
    sums = 0.0
    for gate_in, up_in, act_in, gg_out, ug_out in (
        (gate_ref, up_ref, act_ref, gg_ref, ug_ref),
        (gatep_ref, upp_ref, actp_ref, ggp_ref, ugp_ref),
    ):
        gate, up, act = gate_in[...], up_in[...], act_in[...].astype(F32)
        sigma = jax.nn.sigmoid(gate)
        gg = (act * up * sigma * (1.0 + gate * (1.0 - sigma))).astype(BF16)
        ug = (act * (gate * sigma)).astype(BF16)
        gg_out[...] = gg
        ug_out[...] = ug
        sums = sums + jnp.sum(gg.astype(F32) * gate + ug.astype(F32) * up, axis=1, keepdims=True)
    column_ref[pl.ds(0, HALF), :] = jnp.broadcast_to(sums, (HALF, LANES))
    column_ref[pl.ds(HALF, PADDED - HALF), :] = jnp.zeros((PADDED - HALF, LANES), F32)
    rows = [jnp.transpose(column_ref[pl.ds(r * LANES, LANES), :])[0:1] for r in range(PADDED // LANES)]
    projection = carried(jnp.concatenate(rows, axis=0))
    gs = (gg_ref, ug_ref, ggp_ref, ugp_ref)
    for a in range(NY):
        y = lax.rem(lax.axis_index("tensor_0") + a, NY)
        for z in range(0, NZ, 2):
            at = pl.ds(pl.multiple_of((y * NZ + z) * LANES, 2 * LANES), 2 * LANES)
            total = 0.0
            for g_ref, w_ref in zip(gs, ws):
                total = total + jnp.dot(g_ref[...], w_ref[:, at], preferred_element_type=F32)
            total = total.astype(BF16)
            for k in range(2):
                part = total[:, k * LANES : (k + 1) * LANES]
                top_ref[z + k, a] = part[:ZFIRST]
                outs[a][z + k, pl.ds(0, YFIRST), :] = part[ZFIRST:]
                outs[a][z + k, pl.ds(YFIRST, EXTRA), :] = projection


def sum_top_kernel(got_ref, *outs):
    for a in range(NY):
        total = got_ref[0, a].astype(F32)
        for z in range(1, NZ):
            total = total + got_ref[z, a].astype(F32)
        outs[a][...] = total.astype(BF16)


def sum_low_kernel(*refs):
    *shares, out_ref = refs
    for z in range(NZ):
        total = 0.0
        for ref in shares:
            total = total + ref[z].astype(F32)
        out_ref[z, pl.ds(0, YFIRST), :] = total[:YFIRST].astype(BF16)
        out_ref[z, pl.ds(YFIRST, EXTRA), :] = carried(gathered_up(total[YFIRST:]))


def finish_kernel(*refs):
    *tops, low_ref, inv_ref, out_ref = refs
    top, low = 0.0, low_ref[0].astype(F32)
    for ref in tops:
        top = top + ref[...].astype(F32)
    for z in range(1, NZ):
        low = low + low_ref[z].astype(F32)
    slot_grad = jnp.concatenate([top, low[:YFIRST]], axis=0).astype(BF16)
    rows = gathered_up(low[YFIRST:])
    projection = jnp.concatenate([rows[r : r + 1] for r in range(PADDED // LANES)], axis=1)
    inv = inv_ref[...]
    terms = split3(inv * inv * projection / D) + split3(inv)
    terms = jnp.concatenate([t.astype(F32) for t in terms] + [jnp.zeros((10, PADDED), F32)], axis=0)
    for b in range(GROUPS):
        here = slot_grad[b * MINE : (b + 1) * MINE]
        scalars = terms[:, b * MINE : b * MINE + LANES].astype(BF16)
        for k in range(2):
            out_ref[2 * b + k, pl.ds(0, MINE), :] = here
            out_ref[2 * b + k, pl.ds(MINE, EXTRA), :] = scalars


def combine_kernel(got_ref, ids_ref, x_ref, gain_ref, out_ref):
    one, two = slots_of(ids_ref[...])
    tokens = ids_ref.shape[1]
    rows = lax.broadcasted_iota(jnp.int32, (ROWS, tokens), 0)
    table = jnp.where((rows == one) | (rows == two), 1.0, 0.0).astype(BF16)
    slot_grad = jnp.concatenate([got_ref[i, pl.ds(0, MINE), :] for i in range(2 * GROUPS)], axis=0)
    both = lax.dot_general(slot_grad, table, TN, preferred_element_type=F32)
    token_grad = jnp.where(lax.axis_index("kv") == 0, both[:64], both[64:])
    scalars = jnp.concatenate(
        [got_ref[i, pl.ds(MINE, EXTRA), :].astype(F32)[:, :MINE] for i in range(2 * GROUPS)], axis=1
    )
    found = jnp.dot(scalars.astype(BF16), table, preferred_element_type=F32)
    coefficient = found[0:1] + found[1:2] + found[2:3]
    inverse_rms = 0.5 * (found[3:4] + found[4:5] + found[5:6])
    gain = jnp.broadcast_to(gain_ref[...].astype(F32), (LANES, gain_ref.shape[1]))
    gain = jnp.transpose(gain)[:, 0:1]
    x = x_ref[...].astype(F32)
    out_ref[...] = (inverse_rms * (token_grad * gain) - x * coefficient).astype(BF16)


def shift(value, axis, by):
    n = lax.axis_size(axis)
    return lax.ppermute(value, axis, [(i, (i + by) % n) for i in range(n)])


def gather_ring(value, axis, cut, meet=lambda step, right, left, got: (right, left)):
    n = lax.axis_size(axis)
    got = {0: value}
    right = left = value
    for step in range(1, n // 2):
        right, left = meet(step, right, left, got)
        right, left = shift(right, axis, 1), shift(left, axis, -1)
        got[n - step], got[step] = right, left
    right, left = meet(n // 2, right, left, got)
    return got, (shift(right[:cut], axis, 1), shift(left[cut:], axis, -1))


def shards(residual_stream, grad_output, norm_gain, expert_ids, gate_probs, w_gate, w_up, w_down):
    wg, wu, wd = w_gate[0], w_up[0], w_down[0]
    ids, probs = expert_ids.T, gate_probs.T
    x_t, grad_t = residual_stream.T, grad_output.T
    gain_row = norm_gain[None]
    hidden = wg.shape[0]

    with jax.named_scope("dispatch"):
        [routed] = call(dispatch_kernel, [((GROUPS, 2, CAP, LANES), BF16)], 2, limit=60)(
            ids, probs, x_t, grad_t, gain_row
        )
        got = lax.all_to_all(routed.reshape(2 * GROUPS, CAP, LANES), LINE, 0, 0, tiled=True)
        piece_a, piece_b = call(
            assemble_kernel, [((XROWS + SPLIT, LANES), BF16), ((ROWS - SPLIT, LANES), BF16)], 2
        )(got.reshape(GROUPS, 2, CAP, LANES))

        piece_a, own_wg = lax.optimization_barrier((piece_a, wg))

    with jax.named_scope("weights"):
        wgp = shift(own_wg, "kv", 1)
    with jax.named_scope("gather"):
        line_a = lax.all_gather(piece_a, "tensor_1", axis=0)
        line_b = jnp.stack([piece_b] + [shift(piece_b, "tensor_0", -a) for a in (1, 2, 3)])

        near, far, state = [], [], None
        placed = [((HALF, D), BF16), ((ROWS, D), BF16), ((HALF, LANES), F32)]

        def meet(step, right, left, got):
            nonlocal line_a, wgp, state
            if step == 2:
                right, left, line_a = lax.optimization_barrier((right, left, line_a))
                near[:] = [shift(line_a[: NZ // 2], "tensor_0", by) for by in (1, -1)]
                far[:] = [shift(line_a[NZ // 2 :], "tensor_0", by) for by in (1, -1)]
            if step == 3:
                right, left, wgp, *near[:] = lax.optimization_barrier((right, left, wgp, *near))
                early = [got[b] for b in (0, 1, 2, 6, 7)]
                state = [*call(place_first_kernel, placed, 5)(line_a, near[1], near[0], *early)]
            if step == 4:
                right, left, state[2], *far[:] = lax.optimization_barrier((right, left, state[2], *far))
            return right, left

        b_got, b_far = gather_ring(line_b, "tensor_1", NY // 2, meet)
        lo, hi = shift(near[0], "tensor_0", 1), shift(far[1], "tensor_0", -1)
    with jax.named_scope("place"):
        xs, ds, sq = call(place_second_kernel, placed, 3, aliases={0: 0, 1: 1, 2: 2})(
            *state, far[1], far[0], b_got[3], b_got[5]
        )
    with jax.named_scope("weights"):
        wgp, own_wu = lax.optimization_barrier((wgp, wu))
        wup = shift(own_wu, "kv", 1)

    with jax.named_scope("act"):
        _, act, theirs = call(
            act_kernel,
            [placed[1], ((HALF, hidden), F32), ((HALF, hidden), BF16)],
            3,
            [pltpu.VMEM((ROWS, hidden), F32)],
            aliases={0: 0},
        )(ds, lo, hi, *b_far, wd)
        actp = shift(theirs, "kv", 1)
    with jax.named_scope("forward"):
        _, _, gate, up, gatep, upp, inv = call(
            forward_kernel,
            [placed[0], placed[2]] + [((HALF, hidden), F32)] * 4 + [((1, PADDED), F32)],
            5,
            [pltpu.VMEM((PADDED, LANES), F32)],
            aliases={0: 0, 1: 1},
        )(xs, sq, lo, hi, wg, wu, wgp, wup)
    with jax.named_scope("back"):
        top, *low = call(
            back_kernel,
            [((NZ, NY, ZFIRST, LANES), BF16)] + [((NZ, YFIRST + EXTRA, LANES), BF16)] * NY,
            8,
            [pltpu.VMEM((HALF, hidden), BF16)] * 4 + [pltpu.VMEM((PADDED, LANES), F32)],
        )(gate, up, gatep, upp, act, actp, wg, wu, wgp, wup)
    with jax.named_scope("scatter"):
        top = lax.all_to_all(top, "tensor_1", 0, 0, tiled=True)
        low = [low[0]] + [shift(low[a], "tensor_0", a) for a in (2, 1, 3)]
        [low] = call(sum_low_kernel, [((NZ, YFIRST + EXTRA, LANES), BF16)], 3)(*low)
        top, low = lax.optimization_barrier((top, low))
        top = call(sum_top_kernel, [((ZFIRST, LANES), BF16)] * NY, 3)(top)
        low = lax.all_to_all(low, "tensor_1", 0, 0, tiled=True)
        top = [top[0]] + [shift(top[a], "tensor_0", a) for a in (2, 1, 3)]

    with jax.named_scope("combine"):
        [pieces] = call(finish_kernel, [((2 * GROUPS, MINE + EXTRA, LANES), BF16)], 2)(*top, low, inv)
        got = lax.all_to_all(pieces, LINE, 0, 0, tiled=True)
        [out] = call(combine_kernel, [(x_t.shape, BF16)], 2)(
            got, ids, x_t, gain_row
        )
    return out.T


def solution(mesh):
    torus = Mesh(
        mesh.devices.reshape(mesh.shape["expert"], NY, NZ, mesh.shape["kv"]),
        ("expert", "tensor_0", "tensor_1", "kv"),
    )
    return jax.shard_map(
        shards,
        mesh=torus,
        in_specs=(
            P("expert", TENSOR_KV),
            P("expert", TENSOR_KV),
            P(TENSOR_KV),
            P("expert", None),
            P("expert", None),
            P("expert", TENSOR_KV, None),
            P("expert", TENSOR_KV, None),
            P("expert", TENSOR_KV, None),
        ),
        out_specs=P("expert", TENSOR_KV),
        check_vma=False,
    )
```

```python
import jax
import jax.numpy as jnp
from jax import lax
from jax.experimental import pallas as pl
from jax.experimental.pallas import tpu as pltpu
from jax.sharding import Mesh
from jax.sharding import PartitionSpec as P

D = 4096
CAP = 160
EPS = 1e-05
GROUPS = 4
NY = 4
NZ = 8
LANES = 128
ROWS = GROUPS * CAP
HALF = ROWS // 2
GAIN_ROWS = 16
MINE = CAP // 2
XROWS = HALF + GAIN_ROWS
SPLIT = 144
PADDED = 384
ZFIRST = 112
YFIRST = HALF - ZFIRST
EXTRA = 16
TENSOR_KV = ("tensor_0", "tensor_1", "kv")
LINE = ("expert", "kv")
F32 = jnp.float32
BF16 = jnp.bfloat16
NT = (((1,), (1,)), ((), ()))
TN = (((0,), (0,)), ((), ()))


def call(kernel, outs, us, scratch=(), limit=10, aliases=None):
    here = pl.BlockSpec(memory_space=pltpu.VMEM) if limit < 32 else pl.BlockSpec()

    def run(*arrays):
        return pl.pallas_call(
            kernel,
            in_specs=[here] * len(arrays),
            out_specs=[here] * len(outs),
            out_shape=[jax.ShapeDtypeStruct(s, t) for s, t in outs],
            scratch_shapes=list(scratch),
            input_output_aliases=aliases or {},
            compiler_params=pltpu.CompilerParams(vmem_limit_bytes=limit * 1024 * 1024),
            cost_estimate=pl.CostEstimate(flops=us * 1_000_000_000, bytes_accessed=0, transcendentals=0),
        )(*arrays)

    return run


def slots_of(ids):
    tokens = ids.shape[1]
    first, second = ids[0:1], ids[1:2]
    groups = lax.broadcasted_iota(jnp.int32, (8, tokens), 0)
    named = jnp.where(first == groups, 1.0, 0.0) + jnp.where(second == groups, 1.0, 0.0)
    earlier = jnp.where(
        lax.broadcasted_iota(jnp.int32, (tokens, tokens), 0)
        < lax.broadcasted_iota(jnp.int32, (tokens, tokens), 1),
        1.0,
        0.0,
    ).astype(BF16)
    before = jnp.dot(named.astype(BF16), earlier, preferred_element_type=F32).astype(jnp.int32)
    at_first = jnp.sum(jnp.where(first == groups, before, 0), axis=0, keepdims=True)
    at_second = jnp.sum(jnp.where(second == groups, before, 0), axis=0, keepdims=True)
    return first * CAP + at_first, second * CAP + at_second


def dispatch_kernel(ids_ref, probs_ref, x_ref, grad_ref, gain_ref, out_ref):
    one, two = slots_of(ids_ref[...])
    tokens = ids_ref.shape[1]
    rows = lax.broadcasted_iota(jnp.int32, (ROWS, tokens), 0)
    x = x_ref[...]
    grad = grad_ref[...].astype(F32)
    probs = probs_ref[...]
    terms = []
    for slot, k in ((one, 0), (two, 1)):
        table = jnp.where(rows == slot, 1.0, 0.0).astype(BF16)
        values = jnp.concatenate([(grad * probs[k : k + 1]).astype(BF16), x], axis=0)
        terms.append(lax.dot_general(table, values, NT, preferred_element_type=F32))
    routed = terms[0] + terms[1]
    low = lax.broadcasted_iota(jnp.int32, (MINE, LANES), 1) < LANES // 2
    gain = gain_ref[...].astype(F32)
    gain = jnp.broadcast_to(jnp.concatenate([gain, gain], axis=1), (MINE, LANES))
    for e in range(GROUPS):
        first = routed[e * CAP : e * CAP + MINE]
        second = routed[e * CAP + MINE : (e + 1) * CAP]
        for k in range(2):
            top = first if k == 0 else jnp.where(low, first, second)
            out_ref[e, k, pl.ds(0, MINE), :] = top.astype(BF16)
            out_ref[e, k, pl.ds(MINE, MINE), :] = jnp.where(low, second, gain).astype(BF16)


def assemble_kernel(got_ref, copies_ref, b_ref):
    a_ref = copies_ref.at[0]
    grads = []
    for g in range(GROUPS):
        low, high = got_ref[g, 0].astype(F32), got_ref[g, 1].astype(F32)
        x = jnp.concatenate([low[:, 64:], high[:, 64:]], axis=1).astype(BF16)
        grads.append(jnp.concatenate([low[:, :64], high[:, :64]], axis=1).astype(BF16))
        a_ref[pl.ds(g * MINE, MINE), :] = x[:MINE]
        if g == 0:
            a_ref[pl.ds(HALF, GAIN_ROWS), :] = x[MINE : MINE + GAIN_ROWS]
    a_ref[pl.ds(XROWS, SPLIT), :] = grads[0][:SPLIT]
    b_ref[pl.ds(0, CAP - SPLIT), :] = grads[0][SPLIT:]
    for g in range(1, GROUPS):
        b_ref[pl.ds(g * CAP - SPLIT, CAP), :] = grads[g]
    for z in range(1, NZ):
        copies_ref[z] = copies_ref[0]


def block(y, z):
    return pl.ds(pl.multiple_of((y * NZ + z) * LANES, LANES), LANES)


def column(a, b):
    y = lax.rem(lax.axis_index("tensor_0") + a, NY)
    z = lax.rem(lax.axis_index("tensor_1") + b, NZ)
    return block(y, z)


def row_of(a, z):
    return block(lax.rem(lax.axis_index("tensor_0") + a, NY), z)


def place_x(pieces, xs_ref, sq_ref, begins):
    @pl.loop(0, HALF // 64)
    def _(r):
        rows = pl.ds(pl.multiple_of(r * 64, 64), 64)
        total = jnp.zeros((64, LANES), F32) if begins else sq_ref[rows, :]
        for ref, at, a, z in pieces:
            v = ref[at, rows, :].astype(F32)
            total = total + v * v
            gain = ref[at, pl.ds(HALF, GAIN_ROWS), :].astype(F32)[0:1]
            xs_ref[rows, row_of(a, z)] = (v * gain).astype(BF16)
        sq_ref[rows, :] = total


def place_grad(a_pieces, b_pieces, ds_ref):
    for ref, at, a, z in a_pieces:
        ds_ref[pl.ds(0, SPLIT), row_of(a, z)] = ref[at, pl.ds(XROWS, SPLIT), :]
    for ref, at, a, b in b_pieces:
        ds_ref[pl.ds(SPLIT, ROWS - SPLIT), column(a, b)] = ref[at]


def place_first_kernel(line_ref, near1_ref, near3_ref, b0, b1, b2, b6, b7, xs_ref, ds_ref, sq_ref):
    a_pieces = [(line_ref, z, 0, z) for z in range(NZ)]
    a_pieces += [(ref, z, a, z) for a, ref in ((1, near1_ref), (3, near3_ref)) for z in range(NZ // 2)]
    b_pieces = [(ref, a, a, b) for b, ref in ((0, b0), (1, b1), (2, b2), (6, b6), (7, b7)) for a in range(NY)]
    place_grad(a_pieces, b_pieces, ds_ref)
    place_x(a_pieces, xs_ref, sq_ref, True)


def place_second_kernel(_xs, _ds, _sq, far1_ref, far3_ref, b3, b5, xs_ref, ds_ref, sq_ref):
    a_pieces = [(ref, z, a, NZ // 2 + z) for a, ref in ((1, far1_ref), (3, far3_ref)) for z in range(NZ // 2)]
    b_pieces = [(ref, a, a, b) for b, ref in ((3, b3), (5, b5)) for a in range(NY)]
    place_grad(a_pieces, b_pieces, ds_ref)
    place_x(a_pieces, xs_ref, sq_ref, False)


def act_kernel(_ds, lo_ref, hi_ref, b4lo_ref, b4hi_ref, wd_ref, ds_ref, mine_ref, theirs_ref, act_ref):
    a_pieces = [((lo_ref, hi_ref)[z // 4], z % 4, 2, z) for z in range(NZ)]
    b_pieces = [((b4lo_ref, b4hi_ref)[a // 2], a % 2, a, NZ // 2) for a in range(NY)]
    place_grad(a_pieces, b_pieces, ds_ref)

    @pl.loop(0, 2)
    def _(r):
        rows = pl.ds(pl.multiple_of(r * HALF, HALF), HALF)
        act_ref[rows, :] = lax.dot_general(ds_ref[rows, :], wd_ref[...], NT, preferred_element_type=F32)

    kv = lax.axis_index("kv")
    for g in range(GROUPS):
        here = pl.ds(g * MINE, MINE)
        mine_ref[here, :] = act_ref[pl.ds(pl.multiple_of(g * CAP + kv * MINE, 16), MINE), :]
        theirs_ref[here, :] = act_ref[pl.ds(pl.multiple_of(g * CAP + (1 - kv) * MINE, 16), MINE), :].astype(BF16)


def to_row(column_ref, row_ref):
    for r in range(PADDED // LANES):
        rows = pl.ds(r * LANES, LANES)
        row_ref[:, rows] = jnp.transpose(column_ref[rows, :])[0:1]


def forward_kernel(*refs):
    _xs, _sq, lo_ref, hi_ref, wg_ref, wu_ref, wgp_ref, wup_ref = refs[:8]
    xs_ref, sq_ref, gate_ref, up_ref, gatep_ref, upp_ref, inv_ref, column_ref = refs[8:]
    place_x([((lo_ref, hi_ref)[z // 4], z % 4, 2, z) for z in range(NZ)], xs_ref, sq_ref, False)
    inv = lax.rsqrt(jnp.sum(sq_ref[...], axis=1, keepdims=True) / D + EPS)
    column_ref[pl.ds(0, HALF), :] = jnp.broadcast_to(inv, (HALF, LANES))
    column_ref[pl.ds(HALF, PADDED - HALF), :] = jnp.zeros((PADDED - HALF, LANES), F32)
    to_row(column_ref, inv_ref)
    x = xs_ref[...]
    for w_ref, out_ref in ((wg_ref, gate_ref), (wu_ref, up_ref), (wgp_ref, gatep_ref), (wup_ref, upp_ref)):
        out_ref[...] = inv * lax.dot_general(x, w_ref[...], NT, preferred_element_type=F32)


def split3(value):
    terms = []
    for _ in range(3):
        terms.append(value.astype(BF16))
        value = value - terms[-1].astype(F32)
    return terms


def carried(rows):
    terms = [t.astype(F32) for t in split3(rows)]
    return jnp.concatenate(terms + [jnp.zeros((7, LANES), F32)], axis=0).astype(BF16)


def gathered_up(carried_sum):
    return carried_sum[0:3] + carried_sum[3:6] + carried_sum[6:9]


def back_kernel(*refs):
    gate_ref, up_ref, gatep_ref, upp_ref, act_ref, actp_ref, *ws = refs[:10]
    top_ref, *outs, gg_ref, ug_ref, ggp_ref, ugp_ref, column_ref = refs[10:]
    sums = 0.0
    for gate_in, up_in, act_in, gg_out, ug_out in (
        (gate_ref, up_ref, act_ref, gg_ref, ug_ref),
        (gatep_ref, upp_ref, actp_ref, ggp_ref, ugp_ref),
    ):
        gate, up, act = gate_in[...], up_in[...], act_in[...].astype(F32)
        sigma = jax.nn.sigmoid(gate)
        gg = (act * up * sigma * (1.0 + gate * (1.0 - sigma))).astype(BF16)
        ug = (act * (gate * sigma)).astype(BF16)
        gg_out[...] = gg
        ug_out[...] = ug
        sums = sums + jnp.sum(gg.astype(F32) * gate + ug.astype(F32) * up, axis=1, keepdims=True)
    column_ref[pl.ds(0, HALF), :] = jnp.broadcast_to(sums, (HALF, LANES))
    column_ref[pl.ds(HALF, PADDED - HALF), :] = jnp.zeros((PADDED - HALF, LANES), F32)
    rows = [jnp.transpose(column_ref[pl.ds(r * LANES, LANES), :])[0:1] for r in range(PADDED // LANES)]
    projection = carried(jnp.concatenate(rows, axis=0))
    gs = (gg_ref, ug_ref, ggp_ref, ugp_ref)
    for a in range(NY):
        y = lax.rem(lax.axis_index("tensor_0") + a, NY)
        for z in range(0, NZ, 2):
            at = pl.ds(pl.multiple_of((y * NZ + z) * LANES, 2 * LANES), 2 * LANES)
            total = 0.0
            for g_ref, w_ref in zip(gs, ws):
                total = total + jnp.dot(g_ref[...], w_ref[:, at], preferred_element_type=F32)
            total = total.astype(BF16)
            for k in range(2):
                part = total[:, k * LANES : (k + 1) * LANES]
                top_ref[z + k, a] = part[:ZFIRST]
                outs[a][z + k, pl.ds(0, YFIRST), :] = part[ZFIRST:]
                outs[a][z + k, pl.ds(YFIRST, EXTRA), :] = projection


def sum_top_kernel(got_ref, *outs):
    for a in range(NY):
        total = got_ref[0, a].astype(F32)
        for z in range(1, NZ):
            total = total + got_ref[z, a].astype(F32)
        outs[a][...] = total.astype(BF16)


def sum_low_kernel(*refs):
    *shares, out_ref = refs
    for z in range(NZ):
        total = 0.0
        for ref in shares:
            total = total + ref[z].astype(F32)
        out_ref[z, pl.ds(0, YFIRST), :] = total[:YFIRST].astype(BF16)
        out_ref[z, pl.ds(YFIRST, EXTRA), :] = carried(gathered_up(total[YFIRST:]))


def finish_kernel(*refs):
    *tops, low_ref, inv_ref, out_ref = refs
    top, low = 0.0, low_ref[0].astype(F32)
    for ref in tops:
        top = top + ref[...].astype(F32)
    for z in range(1, NZ):
        low = low + low_ref[z].astype(F32)
    slot_grad = jnp.concatenate([top, low[:YFIRST]], axis=0).astype(BF16)
    rows = gathered_up(low[YFIRST:])
    projection = jnp.concatenate([rows[r : r + 1] for r in range(PADDED // LANES)], axis=1)
    inv = inv_ref[...]
    terms = split3(inv * inv * projection / D) + split3(inv)
    terms = jnp.concatenate([t.astype(F32) for t in terms] + [jnp.zeros((10, PADDED), F32)], axis=0)
    for b in range(GROUPS):
        here = slot_grad[b * MINE : (b + 1) * MINE]
        scalars = terms[:, b * MINE : b * MINE + LANES].astype(BF16)
        for k in range(2):
            out_ref[2 * b + k, pl.ds(0, MINE), :] = here
            out_ref[2 * b + k, pl.ds(MINE, EXTRA), :] = scalars


def combine_kernel(got_ref, ids_ref, x_ref, gain_ref, out_ref):
    one, two = slots_of(ids_ref[...])
    tokens = ids_ref.shape[1]
    rows = lax.broadcasted_iota(jnp.int32, (ROWS, tokens), 0)
    table = jnp.where((rows == one) | (rows == two), 1.0, 0.0).astype(BF16)
    slot_grad = jnp.concatenate([got_ref[i, pl.ds(0, MINE), :] for i in range(2 * GROUPS)], axis=0)
    both = lax.dot_general(slot_grad, table, TN, preferred_element_type=F32)
    token_grad = jnp.where(lax.axis_index("kv") == 0, both[:64], both[64:])
    scalars = jnp.concatenate(
        [got_ref[i, pl.ds(MINE, EXTRA), :].astype(F32)[:, :MINE] for i in range(2 * GROUPS)], axis=1
    )
    found = jnp.dot(scalars.astype(BF16), table, preferred_element_type=F32)
    coefficient = found[0:1] + found[1:2] + found[2:3]
    inverse_rms = 0.5 * (found[3:4] + found[4:5] + found[5:6])
    gain = jnp.broadcast_to(gain_ref[...].astype(F32), (LANES, gain_ref.shape[1]))
    gain = jnp.transpose(gain)[:, 0:1]
    x = x_ref[...].astype(F32)
    out_ref[...] = (inverse_rms * (token_grad * gain) - x * coefficient).astype(BF16)


def shift(value, axis, by):
    n = lax.axis_size(axis)
    return lax.ppermute(value, axis, [(i, (i + by) % n) for i in range(n)])


def gather_ring(value, axis, cut, meet=lambda step, right, left, got: (right, left)):
    n = lax.axis_size(axis)
    got = {0: value}
    right = left = value
    for step in range(1, n // 2):
        right, left = meet(step, right, left, got)
        right, left = shift(right, axis, 1), shift(left, axis, -1)
        got[n - step], got[step] = right, left
    right, left = meet(n // 2, right, left, got)
    return got, (shift(right[:cut], axis, 1), shift(left[cut:], axis, -1))


def shards(residual_stream, grad_output, norm_gain, expert_ids, gate_probs, w_gate, w_up, w_down):
    wg, wu, wd = w_gate[0], w_up[0], w_down[0]
    ids, probs = expert_ids.T, gate_probs.T
    x_t, grad_t = residual_stream.T, grad_output.T
    gain_row = norm_gain[None]
    hidden = wg.shape[0]

    with jax.named_scope("dispatch"):
        [routed] = call(dispatch_kernel, [((GROUPS, 2, CAP, LANES), BF16)], 2, limit=60)(
            ids, probs, x_t, grad_t, gain_row
        )
        got = lax.all_to_all(routed.reshape(2 * GROUPS, CAP, LANES), LINE, 0, 0, tiled=True)
        copies, piece_b = call(
            assemble_kernel, [((NZ, XROWS + SPLIT, LANES), BF16), ((ROWS - SPLIT, LANES), BF16)], 2
        )(got.reshape(GROUPS, 2, CAP, LANES))

        piece_b, own_wg = lax.optimization_barrier((piece_b, wg))

    with jax.named_scope("weights"):
        wgp = shift(own_wg, "kv", 1)
    with jax.named_scope("gather"):
        line_a = lax.all_to_all(copies, "tensor_1", 0, 0, tiled=True)
        line_b = jnp.stack([piece_b] + [shift(piece_b, "tensor_0", -a) for a in (1, 2, 3)])

        line_b, own_wu = lax.optimization_barrier((line_b, wu))
        wup = shift(own_wu, "kv", 1)
        near, far, state = [], [], None
        placed = [((HALF, D), BF16), ((ROWS, D), BF16), ((HALF, LANES), F32)]

        def meet(step, right, left, got):
            nonlocal line_a, wgp, state
            if step == 2:
                right, left, line_a = lax.optimization_barrier((right, left, line_a))
                near[:] = [shift(line_a[: NZ // 2], "tensor_0", by) for by in (1, -1)]
                far[:] = [shift(line_a[NZ // 2 :], "tensor_0", by) for by in (1, -1)]
            if step == 3:
                right, left, wgp, *near[:] = lax.optimization_barrier((right, left, wgp, *near))
                early = [got[b] for b in (0, 1, 2, 6, 7)]
                state = [*call(place_first_kernel, placed, 5)(line_a, near[1], near[0], *early)]
            if step == 4:
                right, left, state[2], *far[:] = lax.optimization_barrier((right, left, state[2], *far))
            return right, left

        b_got, b_far = gather_ring(line_b, "tensor_1", NY // 2, meet)
        lo, hi = shift(near[0], "tensor_0", 1), shift(far[1], "tensor_0", -1)
    with jax.named_scope("place"):
        xs, ds, sq = call(place_second_kernel, placed, 3, aliases={0: 0, 1: 1, 2: 2})(
            *state, far[1], far[0], b_got[3], b_got[5]
        )
    with jax.named_scope("act"):
        _, act, theirs = call(
            act_kernel,
            [placed[1], ((HALF, hidden), F32), ((HALF, hidden), BF16)],
            3,
            [pltpu.VMEM((ROWS, hidden), F32)],
            aliases={0: 0},
        )(ds, lo, hi, *b_far, wd)
        actp = shift(theirs, "kv", 1)
    with jax.named_scope("forward"):
        _, _, gate, up, gatep, upp, inv = call(
            forward_kernel,
            [placed[0], placed[2]] + [((HALF, hidden), F32)] * 4 + [((1, PADDED), F32)],
            5,
            [pltpu.VMEM((PADDED, LANES), F32)],
            aliases={0: 0, 1: 1},
        )(xs, sq, lo, hi, wg, wu, wgp, wup)
    with jax.named_scope("back"):
        top, *low = call(
            back_kernel,
            [((NZ, NY, ZFIRST, LANES), BF16)] + [((NZ, YFIRST + EXTRA, LANES), BF16)] * NY,
            8,
            [pltpu.VMEM((HALF, hidden), BF16)] * 4 + [pltpu.VMEM((PADDED, LANES), F32)],
        )(gate, up, gatep, upp, act, actp, wg, wu, wgp, wup)
    with jax.named_scope("scatter"):
        top = lax.all_to_all(top, "tensor_1", 0, 0, tiled=True)
        low = [low[0]] + [shift(low[a], "tensor_0", a) for a in (2, 1, 3)]
        [low] = call(sum_low_kernel, [((NZ, YFIRST + EXTRA, LANES), BF16)], 3)(*low)
        top, low = lax.optimization_barrier((top, low))
        top = call(sum_top_kernel, [((ZFIRST, LANES), BF16)] * NY, 3)(top)
        low = lax.all_to_all(low, "tensor_1", 0, 0, tiled=True)
        top = [top[0]] + [shift(top[a], "tensor_0", a) for a in (2, 1, 3)]

    with jax.named_scope("combine"):
        [pieces] = call(finish_kernel, [((2 * GROUPS, MINE + EXTRA, LANES), BF16)], 2)(*top, low, inv)
        got = lax.all_to_all(pieces, LINE, 0, 0, tiled=True)
        [out] = call(combine_kernel, [(x_t.shape, BF16)], 2)(
            got, ids, x_t, gain_row
        )
    return out.T


def solution(mesh):
    torus = Mesh(
        mesh.devices.reshape(mesh.shape["expert"], NY, NZ, mesh.shape["kv"]),
        ("expert", "tensor_0", "tensor_1", "kv"),
    )
    return jax.shard_map(
        shards,
        mesh=torus,
        in_specs=(
            P("expert", TENSOR_KV),
            P("expert", TENSOR_KV),
            P(TENSOR_KV),
            P("expert", None),
            P("expert", None),
            P("expert", TENSOR_KV, None),
            P("expert", TENSOR_KV, None),
            P("expert", TENSOR_KV, None),
        ),
        out_specs=P("expert", TENSOR_KV),
        check_vma=False,
    )
```

```python
import jax
import jax.numpy as jnp
from jax import lax
from jax.experimental import pallas as pl
from jax.experimental.pallas import tpu as pltpu
from jax.sharding import Mesh
from jax.sharding import PartitionSpec as P

D = 4096
CAP = 160
EPS = 1e-05
GROUPS = 4
NY = 4
NZ = 8
LANES = 128
ROWS = GROUPS * CAP
HALF = ROWS // 2
GAIN_ROWS = 16
MINE = CAP // 2
XROWS = HALF + GAIN_ROWS
SPLIT = 96
PADDED = 384
ZFIRST = 112
YFIRST = HALF - ZFIRST
EXTRA = 16
TENSOR_KV = ("tensor_0", "tensor_1", "kv")
LINE = ("expert", "kv")
F32 = jnp.float32
BF16 = jnp.bfloat16
NT = (((1,), (1,)), ((), ()))
TN = (((0,), (0,)), ((), ()))


def call(kernel, outs, us, scratch=(), limit=10, aliases=None):
    here = pl.BlockSpec(memory_space=pltpu.VMEM) if limit < 32 else pl.BlockSpec()

    def run(*arrays):
        return pl.pallas_call(
            kernel,
            in_specs=[here] * len(arrays),
            out_specs=[here] * len(outs),
            out_shape=[jax.ShapeDtypeStruct(s, t) for s, t in outs],
            scratch_shapes=list(scratch),
            input_output_aliases=aliases or {},
            compiler_params=pltpu.CompilerParams(vmem_limit_bytes=limit * 1024 * 1024),
            cost_estimate=pl.CostEstimate(flops=us * 1_000_000_000, bytes_accessed=0, transcendentals=0),
        )(*arrays)

    return run


def slots_of(ids):
    tokens = ids.shape[1]
    first, second = ids[0:1], ids[1:2]
    groups = lax.broadcasted_iota(jnp.int32, (8, tokens), 0)
    named = jnp.where(first == groups, 1.0, 0.0) + jnp.where(second == groups, 1.0, 0.0)
    earlier = jnp.where(
        lax.broadcasted_iota(jnp.int32, (tokens, tokens), 0)
        < lax.broadcasted_iota(jnp.int32, (tokens, tokens), 1),
        1.0,
        0.0,
    ).astype(BF16)
    before = jnp.dot(named.astype(BF16), earlier, preferred_element_type=F32).astype(jnp.int32)
    at_first = jnp.sum(jnp.where(first == groups, before, 0), axis=0, keepdims=True)
    at_second = jnp.sum(jnp.where(second == groups, before, 0), axis=0, keepdims=True)
    return first * CAP + at_first, second * CAP + at_second


def dispatch_kernel(ids_ref, probs_ref, x_ref, grad_ref, gain_ref, out_ref):
    one, two = slots_of(ids_ref[...])
    tokens = ids_ref.shape[1]
    rows = lax.broadcasted_iota(jnp.int32, (ROWS, tokens), 0)
    x = x_ref[...]
    grad = grad_ref[...].astype(F32)
    probs = probs_ref[...]
    terms = []
    for slot, k in ((one, 0), (two, 1)):
        table = jnp.where(rows == slot, 1.0, 0.0).astype(BF16)
        values = jnp.concatenate([(grad * probs[k : k + 1]).astype(BF16), x], axis=0)
        terms.append(lax.dot_general(table, values, NT, preferred_element_type=F32))
    routed = terms[0] + terms[1]
    low = lax.broadcasted_iota(jnp.int32, (MINE, LANES), 1) < LANES // 2
    gain = gain_ref[...].astype(F32)
    gain = jnp.broadcast_to(jnp.concatenate([gain, gain], axis=1), (MINE, LANES))
    for e in range(GROUPS):
        first = routed[e * CAP : e * CAP + MINE]
        second = routed[e * CAP + MINE : (e + 1) * CAP]
        for k in range(2):
            top = first if k == 0 else jnp.where(low, first, second)
            out_ref[e, k, pl.ds(0, MINE), :] = top.astype(BF16)
            out_ref[e, k, pl.ds(MINE, MINE), :] = jnp.where(low, second, gain).astype(BF16)


def assemble_kernel(got_ref, copies_ref, b_ref):
    a_ref = copies_ref.at[0]
    grads = []
    for g in range(GROUPS):
        low, high = got_ref[g, 0].astype(F32), got_ref[g, 1].astype(F32)
        x = jnp.concatenate([low[:, 64:], high[:, 64:]], axis=1).astype(BF16)
        grads.append(jnp.concatenate([low[:, :64], high[:, :64]], axis=1).astype(BF16))
        a_ref[pl.ds(g * MINE, MINE), :] = x[:MINE]
        if g == 0:
            a_ref[pl.ds(HALF, GAIN_ROWS), :] = x[MINE : MINE + GAIN_ROWS]
    a_ref[pl.ds(XROWS, SPLIT), :] = grads[0][:SPLIT]
    b_ref[pl.ds(0, CAP - SPLIT), :] = grads[0][SPLIT:]
    for g in range(1, GROUPS):
        b_ref[pl.ds(g * CAP - SPLIT, CAP), :] = grads[g]
    for z in range(1, NZ):
        copies_ref[z] = copies_ref[0]


def block(y, z):
    return pl.ds(pl.multiple_of((y * NZ + z) * LANES, LANES), LANES)


def column(a, b):
    y = lax.rem(lax.axis_index("tensor_0") + a, NY)
    z = lax.rem(lax.axis_index("tensor_1") + b, NZ)
    return block(y, z)


def row_of(a, z):
    return block(lax.rem(lax.axis_index("tensor_0") + a, NY), z)


def place_x(pieces, xs_ref, sq_ref, begins):
    @pl.loop(0, HALF // 64)
    def _(r):
        rows = pl.ds(pl.multiple_of(r * 64, 64), 64)
        total = jnp.zeros((64, LANES), F32) if begins else sq_ref[rows, :]
        for ref, at, a, z in pieces:
            v = ref[at, rows, :].astype(F32)
            total = total + v * v
            gain = ref[at, pl.ds(HALF, GAIN_ROWS), :].astype(F32)[0:1]
            xs_ref[rows, row_of(a, z)] = (v * gain).astype(BF16)
        sq_ref[rows, :] = total


def place_grad(a_pieces, b_pieces, ds_ref):
    for ref, at, a, z in a_pieces:
        ds_ref[pl.ds(0, SPLIT), row_of(a, z)] = ref[at, pl.ds(XROWS, SPLIT), :]
    for ref, at, a, b in b_pieces:
        ds_ref[pl.ds(SPLIT, ROWS - SPLIT), column(a, b)] = ref[at]


def place_first_kernel(line_ref, near1_ref, near3_ref, b0, b1, b2, b6, b7, xs_ref, ds_ref, sq_ref):
    a_pieces = [(line_ref, z, 0, z) for z in range(NZ)]
    a_pieces += [(ref, z, a, z) for a, ref in ((1, near1_ref), (3, near3_ref)) for z in range(NZ // 2)]
    b_pieces = [(ref, a, a, b) for b, ref in ((0, b0), (1, b1), (2, b2), (6, b6), (7, b7)) for a in range(NY)]
    place_grad(a_pieces, b_pieces, ds_ref)
    place_x(a_pieces, xs_ref, sq_ref, True)


def place_second_kernel(_xs, _ds, _sq, far1_ref, far3_ref, b3, b5, xs_ref, ds_ref, sq_ref):
    a_pieces = [(ref, z, a, NZ // 2 + z) for a, ref in ((1, far1_ref), (3, far3_ref)) for z in range(NZ // 2)]
    b_pieces = [(ref, a, a, b) for b, ref in ((3, b3), (5, b5)) for a in range(NY)]
    place_grad(a_pieces, b_pieces, ds_ref)
    place_x(a_pieces, xs_ref, sq_ref, False)


def act_kernel(_ds, lo_ref, hi_ref, b4lo_ref, b4hi_ref, wd_ref, ds_ref, mine_ref, theirs_ref, act_ref):
    a_pieces = [((lo_ref, hi_ref)[z // 4], z % 4, 2, z) for z in range(NZ)]
    b_pieces = [((b4lo_ref, b4hi_ref)[a // 2], a % 2, a, NZ // 2) for a in range(NY)]
    place_grad(a_pieces, b_pieces, ds_ref)

    @pl.loop(0, 2)
    def _(r):
        rows = pl.ds(pl.multiple_of(r * HALF, HALF), HALF)
        act_ref[rows, :] = lax.dot_general(ds_ref[rows, :], wd_ref[...], NT, preferred_element_type=F32)

    kv = lax.axis_index("kv")
    for g in range(GROUPS):
        here = pl.ds(g * MINE, MINE)
        mine_ref[here, :] = act_ref[pl.ds(pl.multiple_of(g * CAP + kv * MINE, 16), MINE), :]
        theirs_ref[here, :] = act_ref[pl.ds(pl.multiple_of(g * CAP + (1 - kv) * MINE, 16), MINE), :].astype(BF16)


def to_row(column_ref, row_ref):
    for r in range(PADDED // LANES):
        rows = pl.ds(r * LANES, LANES)
        row_ref[:, rows] = jnp.transpose(column_ref[rows, :])[0:1]


def forward_kernel(*refs):
    _xs, _sq, lo_ref, hi_ref, wg_ref, wu_ref, wgp_ref, wup_ref = refs[:8]
    xs_ref, sq_ref, gate_ref, up_ref, gatep_ref, upp_ref, inv_ref, column_ref = refs[8:]
    place_x([((lo_ref, hi_ref)[z // 4], z % 4, 2, z) for z in range(NZ)], xs_ref, sq_ref, False)
    inv = lax.rsqrt(jnp.sum(sq_ref[...], axis=1, keepdims=True) / D + EPS)
    column_ref[pl.ds(0, HALF), :] = jnp.broadcast_to(inv, (HALF, LANES))
    column_ref[pl.ds(HALF, PADDED - HALF), :] = jnp.zeros((PADDED - HALF, LANES), F32)
    to_row(column_ref, inv_ref)
    x = xs_ref[...]
    for w_ref, out_ref in ((wg_ref, gate_ref), (wu_ref, up_ref), (wgp_ref, gatep_ref), (wup_ref, upp_ref)):
        out_ref[...] = inv * lax.dot_general(x, w_ref[...], NT, preferred_element_type=F32)


def split3(value):
    terms = []
    for _ in range(3):
        terms.append(value.astype(BF16))
        value = value - terms[-1].astype(F32)
    return terms


def carried(rows):
    terms = [t.astype(F32) for t in split3(rows)]
    return jnp.concatenate(terms + [jnp.zeros((7, LANES), F32)], axis=0).astype(BF16)


def gathered_up(carried_sum):
    return carried_sum[0:3] + carried_sum[3:6] + carried_sum[6:9]


def back_kernel(*refs):
    gate_ref, up_ref, gatep_ref, upp_ref, act_ref, actp_ref, *ws = refs[:10]
    top_ref, *outs, gg_ref, ug_ref, ggp_ref, ugp_ref, column_ref = refs[10:]
    sums = 0.0
    for gate_in, up_in, act_in, gg_out, ug_out in (
        (gate_ref, up_ref, act_ref, gg_ref, ug_ref),
        (gatep_ref, upp_ref, actp_ref, ggp_ref, ugp_ref),
    ):
        gate, up, act = gate_in[...], up_in[...], act_in[...].astype(F32)
        sigma = jax.nn.sigmoid(gate)
        gg = (act * up * sigma * (1.0 + gate * (1.0 - sigma))).astype(BF16)
        ug = (act * (gate * sigma)).astype(BF16)
        gg_out[...] = gg
        ug_out[...] = ug
        sums = sums + jnp.sum(gg.astype(F32) * gate + ug.astype(F32) * up, axis=1, keepdims=True)
    column_ref[pl.ds(0, HALF), :] = jnp.broadcast_to(sums, (HALF, LANES))
    column_ref[pl.ds(HALF, PADDED - HALF), :] = jnp.zeros((PADDED - HALF, LANES), F32)
    rows = [jnp.transpose(column_ref[pl.ds(r * LANES, LANES), :])[0:1] for r in range(PADDED // LANES)]
    projection = carried(jnp.concatenate(rows, axis=0))
    gs = (gg_ref, ug_ref, ggp_ref, ugp_ref)
    for a in range(NY):
        y = lax.rem(lax.axis_index("tensor_0") + a, NY)
        for z in range(0, NZ, 2):
            at = pl.ds(pl.multiple_of((y * NZ + z) * LANES, 2 * LANES), 2 * LANES)
            total = 0.0
            for g_ref, w_ref in zip(gs, ws):
                total = total + jnp.dot(g_ref[...], w_ref[:, at], preferred_element_type=F32)
            total = total.astype(BF16)
            for k in range(2):
                part = total[:, k * LANES : (k + 1) * LANES]
                top_ref[z + k, a] = part[:ZFIRST]
                outs[a][z + k, pl.ds(0, YFIRST), :] = part[ZFIRST:]
                outs[a][z + k, pl.ds(YFIRST, EXTRA), :] = projection


def sum_top_kernel(got_ref, *outs):
    for a in range(NY):
        total = got_ref[0, a].astype(F32)
        for z in range(1, NZ):
            total = total + got_ref[z, a].astype(F32)
        outs[a][...] = total.astype(BF16)


def sum_low_kernel(*refs):
    *shares, out_ref = refs
    for z in range(NZ):
        total = 0.0
        for ref in shares:
            total = total + ref[z].astype(F32)
        out_ref[z, pl.ds(0, YFIRST), :] = total[:YFIRST].astype(BF16)
        out_ref[z, pl.ds(YFIRST, EXTRA), :] = carried(gathered_up(total[YFIRST:]))


def finish_kernel(*refs):
    *tops, low_ref, inv_ref, out_ref = refs
    top, low = 0.0, low_ref[0].astype(F32)
    for ref in tops:
        top = top + ref[...].astype(F32)
    for z in range(1, NZ):
        low = low + low_ref[z].astype(F32)
    slot_grad = jnp.concatenate([top, low[:YFIRST]], axis=0).astype(BF16)
    rows = gathered_up(low[YFIRST:])
    projection = jnp.concatenate([rows[r : r + 1] for r in range(PADDED // LANES)], axis=1)
    inv = inv_ref[...]
    terms = split3(inv * inv * projection / D) + split3(inv)
    terms = jnp.concatenate([t.astype(F32) for t in terms] + [jnp.zeros((10, PADDED), F32)], axis=0)
    for b in range(GROUPS):
        here = slot_grad[b * MINE : (b + 1) * MINE]
        scalars = terms[:, b * MINE : b * MINE + LANES].astype(BF16)
        for k in range(2):
            out_ref[2 * b + k, pl.ds(0, MINE), :] = here
            out_ref[2 * b + k, pl.ds(MINE, EXTRA), :] = scalars


def combine_kernel(got_ref, ids_ref, x_ref, gain_ref, out_ref):
    one, two = slots_of(ids_ref[...])
    tokens = ids_ref.shape[1]
    rows = lax.broadcasted_iota(jnp.int32, (ROWS, tokens), 0)
    table = jnp.where((rows == one) | (rows == two), 1.0, 0.0).astype(BF16)
    slot_grad = jnp.concatenate([got_ref[i, pl.ds(0, MINE), :] for i in range(2 * GROUPS)], axis=0)
    both = lax.dot_general(slot_grad, table, TN, preferred_element_type=F32)
    token_grad = jnp.where(lax.axis_index("kv") == 0, both[:64], both[64:])
    scalars = jnp.concatenate(
        [got_ref[i, pl.ds(MINE, EXTRA), :].astype(F32)[:, :MINE] for i in range(2 * GROUPS)], axis=1
    )
    found = jnp.dot(scalars.astype(BF16), table, preferred_element_type=F32)
    coefficient = found[0:1] + found[1:2] + found[2:3]
    inverse_rms = 0.5 * (found[3:4] + found[4:5] + found[5:6])
    gain = jnp.broadcast_to(gain_ref[...].astype(F32), (LANES, gain_ref.shape[1]))
    gain = jnp.transpose(gain)[:, 0:1]
    x = x_ref[...].astype(F32)
    out_ref[...] = (inverse_rms * (token_grad * gain) - x * coefficient).astype(BF16)


def shift(value, axis, by):
    n = lax.axis_size(axis)
    return lax.ppermute(value, axis, [(i, (i + by) % n) for i in range(n)])


def gather_ring(value, axis, cut, meet=lambda step, right, left, got: (right, left)):
    n = lax.axis_size(axis)
    got = {0: value}
    right = left = value
    for step in range(1, n // 2):
        right, left = meet(step, right, left, got)
        right, left = shift(right, axis, 1), shift(left, axis, -1)
        got[n - step], got[step] = right, left
    right, left = meet(n // 2, right, left, got)
    return got, (shift(right[:cut], axis, 1), shift(left[cut:], axis, -1))


def shards(residual_stream, grad_output, norm_gain, expert_ids, gate_probs, w_gate, w_up, w_down):
    wg, wu, wd = w_gate[0], w_up[0], w_down[0]
    ids, probs = expert_ids.T, gate_probs.T
    x_t, grad_t = residual_stream.T, grad_output.T
    gain_row = norm_gain[None]
    hidden = wg.shape[0]

    with jax.named_scope("dispatch"):
        [routed] = call(dispatch_kernel, [((GROUPS, 2, CAP, LANES), BF16)], 2, limit=60)(
            ids, probs, x_t, grad_t, gain_row
        )
        got = lax.all_to_all(routed.reshape(2 * GROUPS, CAP, LANES), LINE, 0, 0, tiled=True)
        got, own_wg = lax.optimization_barrier((got, wg))
        copies, piece_b = call(
            assemble_kernel, [((NZ, XROWS + SPLIT, LANES), BF16), ((ROWS - SPLIT, LANES), BF16)], 2
        )(got.reshape(GROUPS, 2, CAP, LANES))

    with jax.named_scope("weights"):
        wgp = shift(own_wg, "kv", 1)
    with jax.named_scope("gather"):
        line_a = lax.all_to_all(copies, "tensor_1", 0, 0, tiled=True)
        line_b = jnp.stack([piece_b] + [shift(piece_b, "tensor_0", -a) for a in (1, 2, 3)])

        line_b, own_wu = lax.optimization_barrier((line_b, wu))
        wup = shift(own_wu, "kv", 1)
        near, far, state = [], [], None
        placed = [((HALF, D), BF16), ((ROWS, D), BF16), ((HALF, LANES), F32)]

        def meet(step, right, left, got):
            nonlocal line_a, wgp, state
            if step == 2:
                right, left, line_a, wgp = lax.optimization_barrier((right, left, line_a, wgp))
                near[:] = [shift(line_a[: NZ // 2], "tensor_0", by) for by in (1, -1)]
                far[:] = [shift(line_a[NZ // 2 :], "tensor_0", by) for by in (1, -1)]
            if step == 3:
                right, left, *near[:] = lax.optimization_barrier((right, left, *near))
                early = [got[b] for b in (0, 1, 2, 6, 7)]
                state = [*call(place_first_kernel, placed, 5)(line_a, near[1], near[0], *early)]
            if step == 4:
                right, left, state[2], *far[:] = lax.optimization_barrier((right, left, state[2], *far))
            return right, left

        b_got, b_far = gather_ring(line_b, "tensor_1", NY // 2, meet)
        lo, hi = shift(near[0], "tensor_0", 1), shift(far[1], "tensor_0", -1)
    with jax.named_scope("place"):
        xs, ds, sq = call(place_second_kernel, placed, 3, aliases={0: 0, 1: 1, 2: 2})(
            *state, far[1], far[0], b_got[3], b_got[5]
        )
    with jax.named_scope("act"):
        wd, wup = lax.optimization_barrier((wd, wup))
        _, act, theirs = call(
            act_kernel,
            [placed[1], ((HALF, hidden), F32), ((HALF, hidden), BF16)],
            3,
            [pltpu.VMEM((ROWS, hidden), F32)],
            aliases={0: 0},
        )(ds, lo, hi, *b_far, wd)
        actp = shift(theirs, "kv", 1)
    with jax.named_scope("forward"):
        _, _, gate, up, gatep, upp, inv = call(
            forward_kernel,
            [placed[0], placed[2]] + [((HALF, hidden), F32)] * 4 + [((1, PADDED), F32)],
            5,
            [pltpu.VMEM((PADDED, LANES), F32)],
            aliases={0: 0, 1: 1},
        )(xs, sq, lo, hi, wg, wu, wgp, wup)
    with jax.named_scope("back"):
        top, *low = call(
            back_kernel,
            [((NZ, NY, ZFIRST, LANES), BF16)] + [((NZ, YFIRST + EXTRA, LANES), BF16)] * NY,
            8,
            [pltpu.VMEM((HALF, hidden), BF16)] * 4 + [pltpu.VMEM((PADDED, LANES), F32)],
        )(gate, up, gatep, upp, act, actp, wg, wu, wgp, wup)
    with jax.named_scope("scatter"):
        top = lax.all_to_all(top, "tensor_1", 0, 0, tiled=True)
        low = [low[0]] + [shift(low[a], "tensor_0", a) for a in (2, 1, 3)]
        [low] = call(sum_low_kernel, [((NZ, YFIRST + EXTRA, LANES), BF16)], 3)(*low)
        top, low = lax.optimization_barrier((top, low))
        top = call(sum_top_kernel, [((ZFIRST, LANES), BF16)] * NY, 3)(top)
        low = lax.all_to_all(low, "tensor_1", 0, 0, tiled=True)
        top = [top[0]] + [shift(top[a], "tensor_0", a) for a in (2, 1, 3)]

    with jax.named_scope("combine"):
        [pieces] = call(finish_kernel, [((2 * GROUPS, MINE + EXTRA, LANES), BF16)], 2)(*top, low, inv)
        got = lax.all_to_all(pieces, LINE, 0, 0, tiled=True)
        [out] = call(combine_kernel, [(x_t.shape, BF16)], 2)(
            got, ids, x_t, gain_row
        )
    return out.T


def solution(mesh):
    torus = Mesh(
        mesh.devices.reshape(mesh.shape["expert"], NY, NZ, mesh.shape["kv"]),
        ("expert", "tensor_0", "tensor_1", "kv"),
    )
    return jax.shard_map(
        shards,
        mesh=torus,
        in_specs=(
            P("expert", TENSOR_KV),
            P("expert", TENSOR_KV),
            P(TENSOR_KV),
            P("expert", None),
            P("expert", None),
            P("expert", TENSOR_KV, None),
            P("expert", TENSOR_KV, None),
            P("expert", TENSOR_KV, None),
        ),
        out_specs=P("expert", TENSOR_KV),
        check_vma=False,
    )
```

```python
import jax
import jax.numpy as jnp
from jax import lax
from jax.experimental import pallas as pl
from jax.experimental.pallas import tpu as pltpu
from jax.sharding import Mesh
from jax.sharding import PartitionSpec as P

D = 4096
CAP = 160
EPS = 1e-05
GROUPS = 4
NY = 4
NZ = 8
LANES = 128
ROWS = GROUPS * CAP
HALF = ROWS // 2
GAIN_ROWS = 16
MINE = CAP // 2
XROWS = HALF + GAIN_ROWS
SPLIT = 96
PADDED = 384
ZFIRST = 112
YFIRST = HALF - ZFIRST
EXTRA = 16
TENSOR_KV = ("tensor_0", "tensor_1", "kv")
LINE = ("expert", "kv")
F32 = jnp.float32
BF16 = jnp.bfloat16
NT = (((1,), (1,)), ((), ()))
TN = (((0,), (0,)), ((), ()))


def call(kernel, outs, us, scratch=(), limit=10, aliases=None):
    here = pl.BlockSpec(memory_space=pltpu.VMEM) if limit < 32 else pl.BlockSpec()

    def run(*arrays):
        return pl.pallas_call(
            kernel,
            in_specs=[here] * len(arrays),
            out_specs=[here] * len(outs),
            out_shape=[jax.ShapeDtypeStruct(s, t) for s, t in outs],
            scratch_shapes=list(scratch),
            input_output_aliases=aliases or {},
            compiler_params=pltpu.CompilerParams(vmem_limit_bytes=limit * 1024 * 1024),
            cost_estimate=pl.CostEstimate(flops=us * 1_000_000_000, bytes_accessed=0, transcendentals=0),
        )(*arrays)

    return run


def slots_of(ids):
    tokens = ids.shape[1]
    first, second = ids[0:1], ids[1:2]
    groups = lax.broadcasted_iota(jnp.int32, (8, tokens), 0)
    named = jnp.where(first == groups, 1.0, 0.0) + jnp.where(second == groups, 1.0, 0.0)
    earlier = jnp.where(
        lax.broadcasted_iota(jnp.int32, (tokens, tokens), 0)
        < lax.broadcasted_iota(jnp.int32, (tokens, tokens), 1),
        1.0,
        0.0,
    ).astype(BF16)
    before = jnp.dot(named.astype(BF16), earlier, preferred_element_type=F32).astype(jnp.int32)
    at_first = jnp.sum(jnp.where(first == groups, before, 0), axis=0, keepdims=True)
    at_second = jnp.sum(jnp.where(second == groups, before, 0), axis=0, keepdims=True)
    return first * CAP + at_first, second * CAP + at_second


def dispatch_kernel(ids_ref, probs_ref, x_ref, grad_ref, gain_ref, out_ref):
    one, two = slots_of(ids_ref[...])
    tokens = ids_ref.shape[1]
    rows = lax.broadcasted_iota(jnp.int32, (ROWS, tokens), 0)
    x = x_ref[...]
    grad = grad_ref[...].astype(F32)
    probs = probs_ref[...]
    terms = []
    for slot, k in ((one, 0), (two, 1)):
        table = jnp.where(rows == slot, 1.0, 0.0).astype(BF16)
        values = jnp.concatenate([(grad * probs[k : k + 1]).astype(BF16), x], axis=0)
        terms.append(lax.dot_general(table, values, NT, preferred_element_type=F32))
    routed = terms[0] + terms[1]
    low = lax.broadcasted_iota(jnp.int32, (MINE, LANES), 1) < LANES // 2
    gain = gain_ref[...].astype(F32)
    gain = jnp.broadcast_to(jnp.concatenate([gain, gain], axis=1), (MINE, LANES))
    for e in range(GROUPS):
        first = routed[e * CAP : e * CAP + MINE]
        second = routed[e * CAP + MINE : (e + 1) * CAP]
        for k in range(2):
            top = first if k == 0 else jnp.where(low, first, second)
            out_ref[e, k, pl.ds(0, MINE), :] = top.astype(BF16)
            out_ref[e, k, pl.ds(MINE, MINE), :] = jnp.where(low, second, gain).astype(BF16)


def assemble_kernel(got_ref, copies_ref, b_ref):
    a_ref = copies_ref.at[0]
    grads = []
    for g in range(GROUPS):
        low, high = got_ref[g, 0].astype(F32), got_ref[g, 1].astype(F32)
        x = jnp.concatenate([low[:, 64:], high[:, 64:]], axis=1).astype(BF16)
        grads.append(jnp.concatenate([low[:, :64], high[:, :64]], axis=1).astype(BF16))
        a_ref[pl.ds(g * MINE, MINE), :] = x[:MINE]
        if g == 0:
            a_ref[pl.ds(HALF, GAIN_ROWS), :] = x[MINE : MINE + GAIN_ROWS]
    a_ref[pl.ds(XROWS, SPLIT), :] = grads[0][:SPLIT]
    b_ref[pl.ds(0, CAP - SPLIT), :] = grads[0][SPLIT:]
    for g in range(1, GROUPS):
        b_ref[pl.ds(g * CAP - SPLIT, CAP), :] = grads[g]
    for z in range(1, NZ):
        copies_ref[z] = copies_ref[0]


def block(y, z):
    return pl.ds(pl.multiple_of((y * NZ + z) * LANES, LANES), LANES)


def column(a, b):
    y = lax.rem(lax.axis_index("tensor_0") + a, NY)
    z = lax.rem(lax.axis_index("tensor_1") + b, NZ)
    return block(y, z)


def row_of(a, z):
    return block(lax.rem(lax.axis_index("tensor_0") + a, NY), z)


def place_x(pieces, xs_ref, sq_ref, begins):
    @pl.loop(0, HALF // 64)
    def _(r):
        rows = pl.ds(pl.multiple_of(r * 64, 64), 64)
        total = jnp.zeros((64, LANES), F32) if begins else sq_ref[rows, :]
        for ref, at, a, z in pieces:
            v = ref[at, rows, :].astype(F32)
            total = total + v * v
            gain = ref[at, pl.ds(HALF, GAIN_ROWS), :].astype(F32)[0:1]
            xs_ref[rows, row_of(a, z)] = (v * gain).astype(BF16)
        sq_ref[rows, :] = total


def place_grad(a_pieces, b_pieces, ds_ref):
    for ref, at, a, z in a_pieces:
        ds_ref[pl.ds(0, SPLIT), row_of(a, z)] = ref[at, pl.ds(XROWS, SPLIT), :]
    for ref, at, a, b in b_pieces:
        ds_ref[pl.ds(SPLIT, ROWS - SPLIT), column(a, b)] = ref[at]


def place_first_kernel(line_ref, near1_ref, near3_ref, b0, b1, b2, b6, b7, xs_ref, ds_ref, sq_ref):
    a_pieces = [(line_ref, z, 0, z) for z in range(NZ)]
    a_pieces += [(ref, z, a, z) for a, ref in ((1, near1_ref), (3, near3_ref)) for z in range(NZ // 2)]
    b_pieces = [(ref, a, a, b) for b, ref in ((0, b0), (1, b1), (2, b2), (6, b6), (7, b7)) for a in range(NY)]
    place_grad(a_pieces, b_pieces, ds_ref)
    place_x(a_pieces, xs_ref, sq_ref, True)


def place_second_kernel(_xs, _ds, _sq, far1_ref, far3_ref, b3, b5, xs_ref, ds_ref, sq_ref):
    a_pieces = [(ref, z, a, NZ // 2 + z) for a, ref in ((1, far1_ref), (3, far3_ref)) for z in range(NZ // 2)]
    b_pieces = [(ref, a, a, b) for b, ref in ((3, b3), (5, b5)) for a in range(NY)]
    place_grad(a_pieces, b_pieces, ds_ref)
    place_x(a_pieces, xs_ref, sq_ref, False)


def act_kernel(_ds, lo_ref, hi_ref, b4lo_ref, b4hi_ref, wd_ref, ds_ref, mine_ref, theirs_ref, act_ref):
    a_pieces = [((lo_ref, hi_ref)[z // 4], z % 4, 2, z) for z in range(NZ)]
    b_pieces = [((b4lo_ref, b4hi_ref)[a // 2], a % 2, a, NZ // 2) for a in range(NY)]
    place_grad(a_pieces, b_pieces, ds_ref)

    @pl.loop(0, 2)
    def _(r):
        rows = pl.ds(pl.multiple_of(r * HALF, HALF), HALF)
        act_ref[rows, :] = lax.dot_general(ds_ref[rows, :], wd_ref[...], NT, preferred_element_type=F32)

    kv = lax.axis_index("kv")
    for g in range(GROUPS):
        here = pl.ds(g * MINE, MINE)
        mine_ref[here, :] = act_ref[pl.ds(pl.multiple_of(g * CAP + kv * MINE, 16), MINE), :]
        theirs_ref[here, :] = act_ref[pl.ds(pl.multiple_of(g * CAP + (1 - kv) * MINE, 16), MINE), :].astype(BF16)


def to_row(column_ref, row_ref):
    for r in range(PADDED // LANES):
        rows = pl.ds(r * LANES, LANES)
        row_ref[:, rows] = jnp.transpose(column_ref[rows, :])[0:1]


def forward_kernel(*refs):
    _xs, _sq, lo_ref, hi_ref, wg_ref, wu_ref, wgp_ref, wup_ref = refs[:8]
    xs_ref, sq_ref, gate_ref, up_ref, gatep_ref, upp_ref, inv_ref, column_ref = refs[8:]
    place_x([((lo_ref, hi_ref)[z // 4], z % 4, 2, z) for z in range(NZ)], xs_ref, sq_ref, False)
    inv = lax.rsqrt(jnp.sum(sq_ref[...], axis=1, keepdims=True) / D + EPS)
    column_ref[pl.ds(0, HALF), :] = jnp.broadcast_to(inv, (HALF, LANES))
    column_ref[pl.ds(HALF, PADDED - HALF), :] = jnp.zeros((PADDED - HALF, LANES), F32)
    to_row(column_ref, inv_ref)
    x = xs_ref[...]
    for w_ref, out_ref in ((wg_ref, gate_ref), (wu_ref, up_ref), (wgp_ref, gatep_ref), (wup_ref, upp_ref)):
        out_ref[...] = inv * lax.dot_general(x, w_ref[...], NT, preferred_element_type=F32)


def split3(value):
    terms = []
    for _ in range(3):
        terms.append(value.astype(BF16))
        value = value - terms[-1].astype(F32)
    return terms


def carried(rows):
    terms = [t.astype(F32) for t in split3(rows)]
    return jnp.concatenate(terms + [jnp.zeros((7, LANES), F32)], axis=0).astype(BF16)


def gathered_up(carried_sum):
    return carried_sum[0:3] + carried_sum[3:6] + carried_sum[6:9]


def back_kernel(*refs):
    gate_ref, up_ref, gatep_ref, upp_ref, act_ref, actp_ref, *ws = refs[:10]
    top_ref, *outs, gg_ref, ug_ref, ggp_ref, ugp_ref, column_ref = refs[10:]
    sums = 0.0
    for gate_in, up_in, act_in, gg_out, ug_out in (
        (gate_ref, up_ref, act_ref, gg_ref, ug_ref),
        (gatep_ref, upp_ref, actp_ref, ggp_ref, ugp_ref),
    ):
        gate, up, act = gate_in[...], up_in[...], act_in[...].astype(F32)
        sigma = jax.nn.sigmoid(gate)
        gg = (act * up * sigma * (1.0 + gate * (1.0 - sigma))).astype(BF16)
        ug = (act * (gate * sigma)).astype(BF16)
        gg_out[...] = gg
        ug_out[...] = ug
        sums = sums + jnp.sum(gg.astype(F32) * gate + ug.astype(F32) * up, axis=1, keepdims=True)
    column_ref[pl.ds(0, HALF), :] = jnp.broadcast_to(sums, (HALF, LANES))
    column_ref[pl.ds(HALF, PADDED - HALF), :] = jnp.zeros((PADDED - HALF, LANES), F32)
    rows = [jnp.transpose(column_ref[pl.ds(r * LANES, LANES), :])[0:1] for r in range(PADDED // LANES)]
    projection = carried(jnp.concatenate(rows, axis=0))
    gs = (gg_ref, ug_ref, ggp_ref, ugp_ref)
    for a in range(NY):
        y = lax.rem(lax.axis_index("tensor_0") + a, NY)
        for z in range(0, NZ, 2):
            at = pl.ds(pl.multiple_of((y * NZ + z) * LANES, 2 * LANES), 2 * LANES)
            total = 0.0
            for g_ref, w_ref in zip(gs, ws):
                total = total + jnp.dot(g_ref[...], w_ref[:, at], preferred_element_type=F32)
            total = total.astype(BF16)
            for k in range(2):
                part = total[:, k * LANES : (k + 1) * LANES]
                top_ref[z + k, a] = part[:ZFIRST]
                outs[a][z + k, pl.ds(0, YFIRST), :] = part[ZFIRST:]
                outs[a][z + k, pl.ds(YFIRST, EXTRA), :] = projection


def sum_top_kernel(got_ref, *outs):
    for a in range(NY):
        total = got_ref[0, a].astype(F32)
        for z in range(1, NZ):
            total = total + got_ref[z, a].astype(F32)
        outs[a][...] = total.astype(BF16)


def sum_low_kernel(*refs):
    *shares, out_ref = refs
    for z in range(NZ):
        total = 0.0
        for ref in shares:
            total = total + ref[z].astype(F32)
        out_ref[z, pl.ds(0, YFIRST), :] = total[:YFIRST].astype(BF16)
        out_ref[z, pl.ds(YFIRST, EXTRA), :] = carried(gathered_up(total[YFIRST:]))


def finish_kernel(*refs):
    *tops, low_ref, inv_ref, out_ref = refs
    top, low = 0.0, low_ref[0].astype(F32)
    for ref in tops:
        top = top + ref[...].astype(F32)
    for z in range(1, NZ):
        low = low + low_ref[z].astype(F32)
    slot_grad = jnp.concatenate([top, low[:YFIRST]], axis=0).astype(BF16)
    rows = gathered_up(low[YFIRST:])
    projection = jnp.concatenate([rows[r : r + 1] for r in range(PADDED // LANES)], axis=1)
    inv = inv_ref[...]
    terms = split3(inv * inv * projection / D) + split3(inv)
    terms = jnp.concatenate([t.astype(F32) for t in terms] + [jnp.zeros((10, PADDED), F32)], axis=0)
    for b in range(GROUPS):
        here = slot_grad[b * MINE : (b + 1) * MINE]
        scalars = terms[:, b * MINE : b * MINE + LANES].astype(BF16)
        for k in range(2):
            out_ref[2 * b + k, pl.ds(0, MINE), :] = here
            out_ref[2 * b + k, pl.ds(MINE, EXTRA), :] = scalars


def combine_kernel(got_ref, ids_ref, x_ref, gain_ref, out_ref):
    one, two = slots_of(ids_ref[...])
    tokens = ids_ref.shape[1]
    rows = lax.broadcasted_iota(jnp.int32, (ROWS, tokens), 0)
    table = jnp.where((rows == one) | (rows == two), 1.0, 0.0).astype(BF16)
    slot_grad = jnp.concatenate([got_ref[i, pl.ds(0, MINE), :] for i in range(2 * GROUPS)], axis=0)
    both = lax.dot_general(slot_grad, table, TN, preferred_element_type=F32)
    token_grad = jnp.where(lax.axis_index("kv") == 0, both[:64], both[64:])
    scalars = jnp.concatenate(
        [got_ref[i, pl.ds(MINE, EXTRA), :].astype(F32)[:, :MINE] for i in range(2 * GROUPS)], axis=1
    )
    found = jnp.dot(scalars.astype(BF16), table, preferred_element_type=F32)
    coefficient = found[0:1] + found[1:2] + found[2:3]
    inverse_rms = 0.5 * (found[3:4] + found[4:5] + found[5:6])
    gain = jnp.broadcast_to(gain_ref[...].astype(F32), (LANES, gain_ref.shape[1]))
    gain = jnp.transpose(gain)[:, 0:1]
    x = x_ref[...].astype(F32)
    out_ref[...] = (inverse_rms * (token_grad * gain) - x * coefficient).astype(BF16)


def shift(value, axis, by):
    n = lax.axis_size(axis)
    return lax.ppermute(value, axis, [(i, (i + by) % n) for i in range(n)])


def gather_ring(value, axis, cut, meet=lambda step, right, left, got: (right, left)):
    n = lax.axis_size(axis)
    got = {0: value}
    right = left = value
    for step in range(1, n // 2):
        right, left = meet(step, right, left, got)
        right, left = shift(right, axis, 1), shift(left, axis, -1)
        got[n - step], got[step] = right, left
    right, left = meet(n // 2, right, left, got)
    return got, (shift(right[:cut], axis, 1), shift(left[cut:], axis, -1))


def shards(residual_stream, grad_output, norm_gain, expert_ids, gate_probs, w_gate, w_up, w_down):
    wg, wu, wd = w_gate[0], w_up[0], w_down[0]
    ids, probs = expert_ids.T, gate_probs.T
    x_t, grad_t = residual_stream.T, grad_output.T
    gain_row = norm_gain[None]
    hidden = wg.shape[0]

    with jax.named_scope("dispatch"):
        [routed] = call(dispatch_kernel, [((GROUPS, 2, CAP, LANES), BF16)], 2, limit=60)(
            ids, probs, x_t, grad_t, gain_row
        )
        got = lax.all_to_all(routed.reshape(2 * GROUPS, CAP, LANES), LINE, 0, 0, tiled=True)
        got, own_wg = lax.optimization_barrier((got, wg))
        copies, piece_b = call(
            assemble_kernel, [((NZ, XROWS + SPLIT, LANES), BF16), ((ROWS - SPLIT, LANES), BF16)], 2
        )(got.reshape(GROUPS, 2, CAP, LANES))

    with jax.named_scope("weights"):
        wgp = shift(own_wg, "kv", 1)
    with jax.named_scope("gather"):
        line_a = lax.all_to_all(copies, "tensor_1", 0, 0, tiled=True)
        line_b = jnp.stack([piece_b] + [shift(piece_b, "tensor_0", -a) for a in (1, 2, 3)])

        line_b, own_wu = lax.optimization_barrier((line_b, wu))
        wup = shift(own_wu, "kv", 1)
        near, far, state = [], [], None
        placed = [((HALF, D), BF16), ((ROWS, D), BF16), ((HALF, LANES), F32)]

        def meet(step, right, left, got):
            nonlocal line_a, wgp, state
            if step == 2:
                right, left, line_a, wgp = lax.optimization_barrier((right, left, line_a, wgp))
                near[:] = [shift(line_a[: NZ // 2], "tensor_0", by) for by in (1, -1)]
                far[:] = [shift(line_a[NZ // 2 :], "tensor_0", by) for by in (1, -1)]
            if step == 3:
                right, left, *near[:] = lax.optimization_barrier((right, left, *near))
                early = [got[b] for b in (0, 1, 2, 6, 7)]
                state = [*call(place_first_kernel, placed, 5)(line_a, near[1], near[0], *early)]
            if step == 4:
                right, left, state[2], *far[:] = lax.optimization_barrier((right, left, state[2], *far))
            return right, left

        b_got, b_far = gather_ring(line_b, "tensor_1", NY // 2, meet)
        lo, hi = shift(near[0], "tensor_0", 1), shift(far[1], "tensor_0", -1)
    with jax.named_scope("place"):
        xs, ds, sq = call(place_second_kernel, placed, 3, aliases={0: 0, 1: 1, 2: 2})(
            *state, far[1], far[0], b_got[3], b_got[5]
        )
    with jax.named_scope("act"):
        _, act, theirs = call(
            act_kernel,
            [placed[1], ((HALF, hidden), F32), ((HALF, hidden), BF16)],
            3,
            [pltpu.VMEM((ROWS, hidden), F32)],
            aliases={0: 0},
        )(ds, lo, hi, *b_far, wd)
        actp = shift(theirs, "kv", 1)
    with jax.named_scope("forward"):
        _, _, gate, up, gatep, upp, inv = call(
            forward_kernel,
            [placed[0], placed[2]] + [((HALF, hidden), F32)] * 4 + [((1, PADDED), F32)],
            5,
            [pltpu.VMEM((PADDED, LANES), F32)],
            aliases={0: 0, 1: 1},
        )(xs, sq, lo, hi, wg, wu, wgp, wup)
    with jax.named_scope("back"):
        top, *low = call(
            back_kernel,
            [((NZ, NY, ZFIRST, LANES), BF16)] + [((NZ, YFIRST + EXTRA, LANES), BF16)] * NY,
            8,
            [pltpu.VMEM((HALF, hidden), BF16)] * 4 + [pltpu.VMEM((PADDED, LANES), F32)],
        )(gate, up, gatep, upp, act, actp, wg, wu, wgp, wup)
    with jax.named_scope("scatter"):
        top = lax.all_to_all(top, "tensor_1", 0, 0, tiled=True)
        low = [low[0]] + [shift(low[a], "tensor_0", a) for a in (2, 1, 3)]
        [low] = call(sum_low_kernel, [((NZ, YFIRST + EXTRA, LANES), BF16)], 3)(*low)
        top, low = lax.optimization_barrier((top, low))
        top = call(sum_top_kernel, [((ZFIRST, LANES), BF16)] * NY, 3)(top)
        low = lax.all_to_all(low, "tensor_1", 0, 0, tiled=True)
        top = [top[0]] + [shift(top[a], "tensor_0", a) for a in (2, 1, 3)]

    with jax.named_scope("combine"):
        [pieces] = call(finish_kernel, [((2 * GROUPS, MINE + EXTRA, LANES), BF16)], 2)(*top, low, inv)
        got = lax.all_to_all(pieces, LINE, 0, 0, tiled=True)
        [out] = call(combine_kernel, [(x_t.shape, BF16)], 2)(
            got, ids, x_t, gain_row
        )
    return out.T


def solution(mesh):
    torus = Mesh(
        mesh.devices.reshape(mesh.shape["expert"], NY, NZ, mesh.shape["kv"]),
        ("expert", "tensor_0", "tensor_1", "kv"),
    )
    return jax.shard_map(
        shards,
        mesh=torus,
        in_specs=(
            P("expert", TENSOR_KV),
            P("expert", TENSOR_KV),
            P(TENSOR_KV),
            P("expert", None),
            P("expert", None),
            P("expert", TENSOR_KV, None),
            P("expert", TENSOR_KV, None),
            P("expert", TENSOR_KV, None),
        ),
        out_specs=P("expert", TENSOR_KV),
        check_vma=False,
    )
```

```python
import jax
import jax.numpy as jnp
from jax import lax
from jax.experimental import pallas as pl
from jax.experimental.pallas import tpu as pltpu
from jax.sharding import Mesh
from jax.sharding import PartitionSpec as P

D = 4096
CAP = 160
EPS = 1e-05
GROUPS = 4
NY = 4
NZ = 8
LANES = 128
ROWS = GROUPS * CAP
HALF = ROWS // 2
GAIN_ROWS = 16
MINE = CAP // 2
XROWS = HALF + GAIN_ROWS
SPLIT = 80
PADDED = 384
ZFIRST = 112
YFIRST = HALF - ZFIRST
EXTRA = 16
TENSOR_KV = ("tensor_0", "tensor_1", "kv")
LINE = ("expert", "kv")
F32 = jnp.float32
BF16 = jnp.bfloat16
NT = (((1,), (1,)), ((), ()))
TN = (((0,), (0,)), ((), ()))


def call(kernel, outs, us, scratch=(), limit=10, aliases=None):
    here = pl.BlockSpec(memory_space=pltpu.VMEM) if limit < 32 else pl.BlockSpec()

    def run(*arrays):
        return pl.pallas_call(
            kernel,
            in_specs=[here] * len(arrays),
            out_specs=[here] * len(outs),
            out_shape=[jax.ShapeDtypeStruct(s, t) for s, t in outs],
            scratch_shapes=list(scratch),
            input_output_aliases=aliases or {},
            compiler_params=pltpu.CompilerParams(vmem_limit_bytes=limit * 1024 * 1024),
            cost_estimate=pl.CostEstimate(flops=us * 1_000_000_000, bytes_accessed=0, transcendentals=0),
        )(*arrays)

    return run


def slots_of(ids):
    tokens = ids.shape[1]
    first, second = ids[0:1], ids[1:2]
    groups = lax.broadcasted_iota(jnp.int32, (8, tokens), 0)
    named = jnp.where(first == groups, 1.0, 0.0) + jnp.where(second == groups, 1.0, 0.0)
    earlier = jnp.where(
        lax.broadcasted_iota(jnp.int32, (tokens, tokens), 0)
        < lax.broadcasted_iota(jnp.int32, (tokens, tokens), 1),
        1.0,
        0.0,
    ).astype(BF16)
    before = jnp.dot(named.astype(BF16), earlier, preferred_element_type=F32).astype(jnp.int32)
    at_first = jnp.sum(jnp.where(first == groups, before, 0), axis=0, keepdims=True)
    at_second = jnp.sum(jnp.where(second == groups, before, 0), axis=0, keepdims=True)
    return first * CAP + at_first, second * CAP + at_second


def dispatch_kernel(ids_ref, probs_ref, x_ref, grad_ref, gain_ref, out_ref):
    one, two = slots_of(ids_ref[...])
    tokens = ids_ref.shape[1]
    rows = lax.broadcasted_iota(jnp.int32, (ROWS, tokens), 0)
    x = x_ref[...]
    grad = grad_ref[...].astype(F32)
    probs = probs_ref[...]
    terms = []
    for slot, k in ((one, 0), (two, 1)):
        table = jnp.where(rows == slot, 1.0, 0.0).astype(BF16)
        values = jnp.concatenate([(grad * probs[k : k + 1]).astype(BF16), x], axis=0)
        terms.append(lax.dot_general(table, values, NT, preferred_element_type=F32))
    routed = terms[0] + terms[1]
    low = lax.broadcasted_iota(jnp.int32, (MINE, LANES), 1) < LANES // 2
    gain = gain_ref[...].astype(F32)
    gain = jnp.broadcast_to(jnp.concatenate([gain, gain], axis=1), (MINE, LANES))
    for e in range(GROUPS):
        first = routed[e * CAP : e * CAP + MINE]
        second = routed[e * CAP + MINE : (e + 1) * CAP]
        for k in range(2):
            top = first if k == 0 else jnp.where(low, first, second)
            out_ref[e, k, pl.ds(0, MINE), :] = top.astype(BF16)
            out_ref[e, k, pl.ds(MINE, MINE), :] = jnp.where(low, second, gain).astype(BF16)


def assemble_kernel(got_ref, copies_ref, b_ref):
    a_ref = copies_ref.at[0]
    grads = []
    for g in range(GROUPS):
        low, high = got_ref[g, 0].astype(F32), got_ref[g, 1].astype(F32)
        x = jnp.concatenate([low[:, 64:], high[:, 64:]], axis=1).astype(BF16)
        grads.append(jnp.concatenate([low[:, :64], high[:, :64]], axis=1).astype(BF16))
        a_ref[pl.ds(g * MINE, MINE), :] = x[:MINE]
        if g == 0:
            a_ref[pl.ds(HALF, GAIN_ROWS), :] = x[MINE : MINE + GAIN_ROWS]
    a_ref[pl.ds(XROWS, SPLIT), :] = grads[0][:SPLIT]
    b_ref[pl.ds(0, CAP - SPLIT), :] = grads[0][SPLIT:]
    for g in range(1, GROUPS):
        b_ref[pl.ds(g * CAP - SPLIT, CAP), :] = grads[g]
    for z in range(1, NZ):
        copies_ref[z] = copies_ref[0]


def block(y, z):
    return pl.ds(pl.multiple_of((y * NZ + z) * LANES, LANES), LANES)


def column(a, b):
    y = lax.rem(lax.axis_index("tensor_0") + a, NY)
    z = lax.rem(lax.axis_index("tensor_1") + b, NZ)
    return block(y, z)


def row_of(a, z):
    return block(lax.rem(lax.axis_index("tensor_0") + a, NY), z)


def place_x(pieces, xs_ref, sq_ref, begins):
    @pl.loop(0, HALF // 64)
    def _(r):
        rows = pl.ds(pl.multiple_of(r * 64, 64), 64)
        total = jnp.zeros((64, LANES), F32) if begins else sq_ref[rows, :]
        for ref, at, a, z in pieces:
            v = ref[at, rows, :].astype(F32)
            total = total + v * v
            gain = ref[at, pl.ds(HALF, GAIN_ROWS), :].astype(F32)[0:1]
            xs_ref[rows, row_of(a, z)] = (v * gain).astype(BF16)
        sq_ref[rows, :] = total


def place_grad(a_pieces, b_pieces, ds_ref):
    for ref, at, a, z in a_pieces:
        ds_ref[pl.ds(0, SPLIT), row_of(a, z)] = ref[at, pl.ds(XROWS, SPLIT), :]
    for ref, at, a, b in b_pieces:
        ds_ref[pl.ds(SPLIT, ROWS - SPLIT), column(a, b)] = ref[at]


def place_first_kernel(line_ref, near1_ref, near3_ref, b0, b1, b2, b6, b7, xs_ref, ds_ref, sq_ref):
    a_pieces = [(line_ref, z, 0, z) for z in range(NZ)]
    a_pieces += [(ref, z, a, z) for a, ref in ((1, near1_ref), (3, near3_ref)) for z in range(NZ // 2)]
    b_pieces = [(ref, a, a, b) for b, ref in ((0, b0), (1, b1), (2, b2), (6, b6), (7, b7)) for a in range(NY)]
    place_grad(a_pieces, b_pieces, ds_ref)
    place_x(a_pieces, xs_ref, sq_ref, True)


def place_second_kernel(_xs, _ds, _sq, far1_ref, far3_ref, b3, b5, xs_ref, ds_ref, sq_ref):
    a_pieces = [(ref, z, a, NZ // 2 + z) for a, ref in ((1, far1_ref), (3, far3_ref)) for z in range(NZ // 2)]
    b_pieces = [(ref, a, a, b) for b, ref in ((3, b3), (5, b5)) for a in range(NY)]
    place_grad(a_pieces, b_pieces, ds_ref)
    place_x(a_pieces, xs_ref, sq_ref, False)


def act_kernel(_ds, lo_ref, hi_ref, b4lo_ref, b4hi_ref, wd_ref, ds_ref, mine_ref, theirs_ref, act_ref):
    a_pieces = [((lo_ref, hi_ref)[z // 4], z % 4, 2, z) for z in range(NZ)]
    b_pieces = [((b4lo_ref, b4hi_ref)[a // 2], a % 2, a, NZ // 2) for a in range(NY)]
    place_grad(a_pieces, b_pieces, ds_ref)

    @pl.loop(0, 2)
    def _(r):
        rows = pl.ds(pl.multiple_of(r * HALF, HALF), HALF)
        act_ref[rows, :] = lax.dot_general(ds_ref[rows, :], wd_ref[...], NT, preferred_element_type=F32)

    kv = lax.axis_index("kv")
    for g in range(GROUPS):
        here = pl.ds(g * MINE, MINE)
        mine_ref[here, :] = act_ref[pl.ds(pl.multiple_of(g * CAP + kv * MINE, 16), MINE), :]
        theirs_ref[here, :] = act_ref[pl.ds(pl.multiple_of(g * CAP + (1 - kv) * MINE, 16), MINE), :].astype(BF16)


def to_row(column_ref, row_ref):
    for r in range(PADDED // LANES):
        rows = pl.ds(r * LANES, LANES)
        row_ref[:, rows] = jnp.transpose(column_ref[rows, :])[0:1]


def forward_kernel(*refs):
    _xs, _sq, lo_ref, hi_ref, wg_ref, wu_ref, wgp_ref, wup_ref = refs[:8]
    xs_ref, sq_ref, gate_ref, up_ref, gatep_ref, upp_ref, inv_ref, column_ref = refs[8:]
    place_x([((lo_ref, hi_ref)[z // 4], z % 4, 2, z) for z in range(NZ)], xs_ref, sq_ref, False)
    inv = lax.rsqrt(jnp.sum(sq_ref[...], axis=1, keepdims=True) / D + EPS)
    column_ref[pl.ds(0, HALF), :] = jnp.broadcast_to(inv, (HALF, LANES))
    column_ref[pl.ds(HALF, PADDED - HALF), :] = jnp.zeros((PADDED - HALF, LANES), F32)
    to_row(column_ref, inv_ref)
    x = xs_ref[...]
    for w_ref, out_ref in ((wg_ref, gate_ref), (wu_ref, up_ref), (wgp_ref, gatep_ref), (wup_ref, upp_ref)):
        out_ref[...] = inv * lax.dot_general(x, w_ref[...], NT, preferred_element_type=F32)


def split3(value):
    terms = []
    for _ in range(3):
        terms.append(value.astype(BF16))
        value = value - terms[-1].astype(F32)
    return terms


def carried(rows):
    terms = [t.astype(F32) for t in split3(rows)]
    return jnp.concatenate(terms + [jnp.zeros((7, LANES), F32)], axis=0).astype(BF16)


def gathered_up(carried_sum):
    return carried_sum[0:3] + carried_sum[3:6] + carried_sum[6:9]


def back_kernel(*refs):
    gate_ref, up_ref, gatep_ref, upp_ref, act_ref, actp_ref, *ws = refs[:10]
    top_ref, *outs, gg_ref, ug_ref, ggp_ref, ugp_ref, column_ref = refs[10:]
    sums = 0.0
    for gate_in, up_in, act_in, gg_out, ug_out in (
        (gate_ref, up_ref, act_ref, gg_ref, ug_ref),
        (gatep_ref, upp_ref, actp_ref, ggp_ref, ugp_ref),
    ):
        gate, up, act = gate_in[...], up_in[...], act_in[...].astype(F32)
        sigma = jax.nn.sigmoid(gate)
        gg = (act * up * sigma * (1.0 + gate * (1.0 - sigma))).astype(BF16)
        ug = (act * (gate * sigma)).astype(BF16)
        gg_out[...] = gg
        ug_out[...] = ug
        sums = sums + jnp.sum(gg.astype(F32) * gate + ug.astype(F32) * up, axis=1, keepdims=True)
    column_ref[pl.ds(0, HALF), :] = jnp.broadcast_to(sums, (HALF, LANES))
    column_ref[pl.ds(HALF, PADDED - HALF), :] = jnp.zeros((PADDED - HALF, LANES), F32)
    rows = [jnp.transpose(column_ref[pl.ds(r * LANES, LANES), :])[0:1] for r in range(PADDED // LANES)]
    projection = carried(jnp.concatenate(rows, axis=0))
    gs = (gg_ref, ug_ref, ggp_ref, ugp_ref)
    for a in range(NY):
        y = lax.rem(lax.axis_index("tensor_0") + a, NY)
        for z in range(0, NZ, 2):
            at = pl.ds(pl.multiple_of((y * NZ + z) * LANES, 2 * LANES), 2 * LANES)
            total = 0.0
            for g_ref, w_ref in zip(gs, ws):
                total = total + jnp.dot(g_ref[...], w_ref[:, at], preferred_element_type=F32)
            total = total.astype(BF16)
            for k in range(2):
                part = total[:, k * LANES : (k + 1) * LANES]
                top_ref[z + k, a] = part[:ZFIRST]
                outs[a][z + k, pl.ds(0, YFIRST), :] = part[ZFIRST:]
                outs[a][z + k, pl.ds(YFIRST, EXTRA), :] = projection


def sum_top_kernel(got_ref, *outs):
    for a in range(NY):
        total = got_ref[0, a].astype(F32)
        for z in range(1, NZ):
            total = total + got_ref[z, a].astype(F32)
        outs[a][...] = total.astype(BF16)


def sum_low_kernel(*refs):
    *shares, out_ref = refs
    for z in range(NZ):
        total = 0.0
        for ref in shares:
            total = total + ref[z].astype(F32)
        out_ref[z, pl.ds(0, YFIRST), :] = total[:YFIRST].astype(BF16)
        out_ref[z, pl.ds(YFIRST, EXTRA), :] = carried(gathered_up(total[YFIRST:]))


def finish_kernel(*refs):
    *tops, low_ref, inv_ref, out_ref = refs
    top, low = 0.0, low_ref[0].astype(F32)
    for ref in tops:
        top = top + ref[...].astype(F32)
    for z in range(1, NZ):
        low = low + low_ref[z].astype(F32)
    slot_grad = jnp.concatenate([top, low[:YFIRST]], axis=0).astype(BF16)
    rows = gathered_up(low[YFIRST:])
    projection = jnp.concatenate([rows[r : r + 1] for r in range(PADDED // LANES)], axis=1)
    inv = inv_ref[...]
    terms = split3(inv * inv * projection / D) + split3(inv)
    terms = jnp.concatenate([t.astype(F32) for t in terms] + [jnp.zeros((10, PADDED), F32)], axis=0)
    for b in range(GROUPS):
        here = slot_grad[b * MINE : (b + 1) * MINE]
        scalars = terms[:, b * MINE : b * MINE + LANES].astype(BF16)
        for k in range(2):
            out_ref[2 * b + k, pl.ds(0, MINE), :] = here
            out_ref[2 * b + k, pl.ds(MINE, EXTRA), :] = scalars


def combine_kernel(got_ref, ids_ref, x_ref, gain_ref, out_ref):
    one, two = slots_of(ids_ref[...])
    tokens = ids_ref.shape[1]
    rows = lax.broadcasted_iota(jnp.int32, (ROWS, tokens), 0)
    table = jnp.where((rows == one) | (rows == two), 1.0, 0.0).astype(BF16)
    slot_grad = jnp.concatenate([got_ref[i, pl.ds(0, MINE), :] for i in range(2 * GROUPS)], axis=0)
    both = lax.dot_general(slot_grad, table, TN, preferred_element_type=F32)
    token_grad = jnp.where(lax.axis_index("kv") == 0, both[:64], both[64:])
    scalars = jnp.concatenate(
        [got_ref[i, pl.ds(MINE, EXTRA), :].astype(F32)[:, :MINE] for i in range(2 * GROUPS)], axis=1
    )
    found = jnp.dot(scalars.astype(BF16), table, preferred_element_type=F32)
    coefficient = found[0:1] + found[1:2] + found[2:3]
    inverse_rms = 0.5 * (found[3:4] + found[4:5] + found[5:6])
    gain = jnp.broadcast_to(gain_ref[...].astype(F32), (LANES, gain_ref.shape[1]))
    gain = jnp.transpose(gain)[:, 0:1]
    x = x_ref[...].astype(F32)
    out_ref[...] = (inverse_rms * (token_grad * gain) - x * coefficient).astype(BF16)


def shift(value, axis, by):
    n = lax.axis_size(axis)
    return lax.ppermute(value, axis, [(i, (i + by) % n) for i in range(n)])


def gather_ring(value, axis, cut, meet=lambda step, right, left, got: (right, left)):
    n = lax.axis_size(axis)
    got = {0: value}
    right = left = value
    for step in range(1, n // 2):
        right, left = meet(step, right, left, got)
        right, left = shift(right, axis, 1), shift(left, axis, -1)
        got[n - step], got[step] = right, left
    right, left = meet(n // 2, right, left, got)
    return got, (shift(right[:cut], axis, 1), shift(left[cut:], axis, -1))


def shards(residual_stream, grad_output, norm_gain, expert_ids, gate_probs, w_gate, w_up, w_down):
    wg, wu, wd = w_gate[0], w_up[0], w_down[0]
    ids, probs = expert_ids.T, gate_probs.T
    x_t, grad_t = residual_stream.T, grad_output.T
    gain_row = norm_gain[None]
    hidden = wg.shape[0]

    with jax.named_scope("dispatch"):
        [routed] = call(dispatch_kernel, [((GROUPS, 2, CAP, LANES), BF16)], 2, limit=60)(
            ids, probs, x_t, grad_t, gain_row
        )
        got = lax.all_to_all(routed.reshape(2 * GROUPS, CAP, LANES), LINE, 0, 0, tiled=True)
        got, own_wg = lax.optimization_barrier((got, wg))
        copies, piece_b = call(
            assemble_kernel, [((NZ, XROWS + SPLIT, LANES), BF16), ((ROWS - SPLIT, LANES), BF16)], 2
        )(got.reshape(GROUPS, 2, CAP, LANES))

    with jax.named_scope("weights"):
        wgp = shift(own_wg, "kv", 1)
    with jax.named_scope("gather"):
        line_a = lax.all_to_all(copies, "tensor_1", 0, 0, tiled=True)
        line_b = jnp.stack([piece_b] + [shift(piece_b, "tensor_0", -a) for a in (1, 2, 3)])

        line_b, own_wu = lax.optimization_barrier((line_b, wu))
        wup = shift(own_wu, "kv", 1)
        near, far, state = [], [], None
        placed = [((HALF, D), BF16), ((ROWS, D), BF16), ((HALF, LANES), F32)]

        def meet(step, right, left, got):
            nonlocal line_a, wgp, state
            if step == 2:
                right, left, line_a, wgp = lax.optimization_barrier((right, left, line_a, wgp))
                near[:] = [shift(line_a[: NZ // 2], "tensor_0", by) for by in (1, -1)]
                far[:] = [shift(line_a[NZ // 2 :], "tensor_0", by) for by in (1, -1)]
            if step == 3:
                right, left, *near[:] = lax.optimization_barrier((right, left, *near))
                early = [got[b] for b in (0, 1, 2, 6, 7)]
                state = [*call(place_first_kernel, placed, 5)(line_a, near[1], near[0], *early)]
            if step == 4:
                right, left, state[2], *far[:] = lax.optimization_barrier((right, left, state[2], *far))
            return right, left

        b_got, b_far = gather_ring(line_b, "tensor_1", NY // 2, meet)
        lo, hi = shift(near[0], "tensor_0", 1), shift(far[1], "tensor_0", -1)
    with jax.named_scope("place"):
        xs, ds, sq = call(place_second_kernel, placed, 3, aliases={0: 0, 1: 1, 2: 2})(
            *state, far[1], far[0], b_got[3], b_got[5]
        )
    with jax.named_scope("act"):
        _, act, theirs = call(
            act_kernel,
            [placed[1], ((HALF, hidden), F32), ((HALF, hidden), BF16)],
            3,
            [pltpu.VMEM((ROWS, hidden), F32)],
            aliases={0: 0},
        )(ds, lo, hi, *b_far, wd)
        actp = shift(theirs, "kv", 1)
    with jax.named_scope("forward"):
        _, _, gate, up, gatep, upp, inv = call(
            forward_kernel,
            [placed[0], placed[2]] + [((HALF, hidden), F32)] * 4 + [((1, PADDED), F32)],
            5,
            [pltpu.VMEM((PADDED, LANES), F32)],
            aliases={0: 0, 1: 1},
        )(xs, sq, lo, hi, wg, wu, wgp, wup)
    with jax.named_scope("back"):
        top, *low = call(
            back_kernel,
            [((NZ, NY, ZFIRST, LANES), BF16)] + [((NZ, YFIRST + EXTRA, LANES), BF16)] * NY,
            8,
            [pltpu.VMEM((HALF, hidden), BF16)] * 4 + [pltpu.VMEM((PADDED, LANES), F32)],
        )(gate, up, gatep, upp, act, actp, wg, wu, wgp, wup)
    with jax.named_scope("scatter"):
        top = lax.all_to_all(top, "tensor_1", 0, 0, tiled=True)
        low = [low[0]] + [shift(low[a], "tensor_0", a) for a in (2, 1, 3)]
        [low] = call(sum_low_kernel, [((NZ, YFIRST + EXTRA, LANES), BF16)], 3)(*low)
        top, low = lax.optimization_barrier((top, low))
        top = call(sum_top_kernel, [((ZFIRST, LANES), BF16)] * NY, 3)(top)
        low = lax.all_to_all(low, "tensor_1", 0, 0, tiled=True)
        top = [top[0]] + [shift(top[a], "tensor_0", a) for a in (2, 1, 3)]

    with jax.named_scope("combine"):
        [pieces] = call(finish_kernel, [((2 * GROUPS, MINE + EXTRA, LANES), BF16)], 2)(*top, low, inv)
        got = lax.all_to_all(pieces, LINE, 0, 0, tiled=True)
        [out] = call(combine_kernel, [(x_t.shape, BF16)], 2)(
            got, ids, x_t, gain_row
        )
    return out.T


def solution(mesh):
    torus = Mesh(
        mesh.devices.reshape(mesh.shape["expert"], NY, NZ, mesh.shape["kv"]),
        ("expert", "tensor_0", "tensor_1", "kv"),
    )
    return jax.shard_map(
        shards,
        mesh=torus,
        in_specs=(
            P("expert", TENSOR_KV),
            P("expert", TENSOR_KV),
            P(TENSOR_KV),
            P("expert", None),
            P("expert", None),
            P("expert", TENSOR_KV, None),
            P("expert", TENSOR_KV, None),
            P("expert", TENSOR_KV, None),
        ),
        out_specs=P("expert", TENSOR_KV),
        check_vma=False,
    )
```
